32 devices in a mesh: fsdp: 8 (over z, x), dp: 4 (over y, core).
Axes of the slice: x: 2, y: 2, z: 4, core: 2. Of those that a mesh axis runs over, the one named last changes fastest.
Arguments:
- pixels: int32 [32, 3072], P(('fsdp', 'dp')), may hold values from 0 to 255
- level_table: bfloat16 [256, 512], P('fsdp'), may hold values from -6 to 6
- channel_table: bfloat16 [3, 512], P(None, 'fsdp'), may hold values from -3 to 3
- attend_in: bfloat16 [512, 1536], P('fsdp'), may hold values from -0.25 to 0.25
- attend_out: bfloat16 [512, 512], P('fsdp'), may hold values from -1 to 1
- first_gain: bfloat16 [512], P('fsdp'), may hold values from 0.25 to 1.75
- first_bias: bfloat16 [512], P('fsdp'), may hold values from -3 to 3
- expand_weight: bfloat16 [512, 2048], P('fsdp'), may hold values from -0.25 to 0.25
- expand_bias: bfloat16 [2048], P('fsdp'), may hold values from -3 to 3
- shrink_weight: bfloat16 [2048, 512], P('fsdp'), may hold values from -0.125 to 0.125
- shrink_bias: bfloat16 [512], P('fsdp'), may hold values from -3 to 3
- second_gain: bfloat16 [512], P('fsdp'), may hold values from 0.25 to 1.75
- second_bias: bfloat16 [512], P('fsdp'), may hold values from -3 to 3
- cotangent: float32 [32, 3072, 512], P(('fsdp', 'dp')), may hold values from -6 to 6
Outputs:
- layer_out: bfloat16 [32, 3072, 512], P(('fsdp', 'dp'))
- grad_level_table: float32 [256, 512], P('fsdp')
- grad_channel_table: float32 [3, 512], P(None, 'fsdp')
- grad_attend_in: float32 [512, 1536], P('fsdp')
- grad_attend_out: float32 [512, 512], P('fsdp')
- grad_first_gain: float32 [512], P('fsdp')
- grad_first_bias: float32 [512], P('fsdp')
- grad_expand_weight: float32 [512, 2048], P('fsdp')
- grad_expand_bias: float32 [2048], P('fsdp')
- grad_shrink_weight: float32 [2048, 512], P('fsdp')
- grad_shrink_bias: float32 [512], P('fsdp')
- grad_second_gain: float32 [512], P('fsdp')
- grad_second_bias: float32 [512], P('fsdp')
The draws below stay inside these ranges and needn't reach their ends.
All inputs are finite; a program needn't handle non-finite values.
Results may differ from the reference program's by a relative error of at most 0.012.
The reference program's roundings to bfloat16 on the way count: a program that leaves them out, or rounds other values in their place, can miss the bound.
Values may be sent and summed in bfloat16 or wider, within the bound.
A program may use at most 320 MiB of HBM per device.

```python
import jax
import jax.numpy as jnp
from jax import lax

D = 512
HEADS = 8
FF = 2048
LEVELS = 256
HEAD_DIM = 64
CHANNELS = 3
FLANK_ROWS = 16
LINE = 96
SEQ = 3072
BLOCKS = 4
BLOCK = 768
KEYS = 2304
IMAGES = 32


def set_ends(entries, own_key, low, high):
    longest = entries.shape.index(max(entries.shape))
    spots = []
    for shift in (0, 1):
        where = [jax.random.randint(jax.random.fold_in(own_key, axis), (), 0, length) for axis, length in enumerate(entries.shape)]
        where[longest] = (where[longest] + shift) % entries.shape[longest]
        spots.append(tuple(where))
    return entries.at[spots[0]].set(low).at[spots[1]].set(high)


def level_of(own_key, dims, pieces, smallest, largest):
    loudness, own = 1.0, jax.random.fold_in(own_key, 6)
    for dim, shards_of in pieces:
        steps = jnp.exp(jax.random.uniform(jax.random.fold_in(own, dim), (shards_of,), jnp.float32, smallest / len(pieces), largest / len(pieces)))
        loudness = loudness * jnp.repeat(steps, dims[dim] // shards_of).reshape([-1 if axis == dim else 1 for axis in range(len(dims))])
    return loudness


def centred(rng, dims, scale, bound, pieces=(), kind=jnp.bfloat16):
    level = level_of(rng, dims, pieces, -0.22, 0.18) if pieces else 1.0
    result = jax.random.normal(rng, dims, jnp.float32) * scale * level
    return jnp.minimum(jnp.maximum(result, -bound), bound).astype(kind)


def setup_inputs(seed: int = 0) -> dict:
    keys = jax.random.split(jax.random.key(seed), 15)
    return {
        "pixels": set_ends(jax.random.randint(keys[0], (IMAGES, SEQ), 0, LEVELS), jax.random.fold_in(keys[0], 1), 0, LEVELS - 1).astype(jnp.int32),
        "level_table": centred(keys[1], (LEVELS, D), 1.0, 6.0, ((0, 8),)),
        "channel_table": centred(keys[2], (CHANNELS, D), 0.5, 3.0, ((1, 8),)),
        "attend_in": centred(keys[3], (D, 3 * D), D ** -0.5, 0.25, ((0, 8),)),
        "attend_out": centred(keys[4], (D, D), (D // 16) ** -0.5, 1.0, ((0, 8),)),
        "first_gain": jnp.clip(1.0 + 0.15 * jax.random.normal(keys[5], (D,), jnp.float32), 0.25, 1.75).astype(jnp.bfloat16),
        "first_bias": centred(keys[6], (D,), 0.5, 3.0, ((0, 8),)),
        "expand_weight": centred(keys[7], (D, FF), D ** -0.5, 0.25, ((0, 8),)),
        "expand_bias": centred(keys[8], (FF,), 0.5, 3.0, ((0, 8),)),
        "shrink_weight": centred(keys[9], (FF, D), FF ** -0.5, 0.125, ((0, 8),)),
        "shrink_bias": centred(keys[10], (D,), 0.5, 3.0, ((0, 8),)),
        "second_gain": jnp.clip(1.0 + 0.15 * jax.random.normal(keys[11], (D,), jnp.float32), 0.25, 1.75).astype(jnp.bfloat16),
        "second_bias": centred(keys[12], (D,), 0.5, 3.0, ((0, 8),)),
        "cotangent": centred(keys[13], (IMAGES, SEQ, D), 1.0, 6.0, ((0, 32),), jnp.float32),
    }


@jax.custom_vjp
def low(v):
    return lax.optimization_barrier(v.astype(jnp.bfloat16)).astype(jnp.float32)

@jax.custom_vjp
def low_back(v):
    return v

def low_keep(v):
    return (low(v), None)

def low_pass(kept, grad):
    return (grad,)

def back_keep(v):
    return (v, None)

def back_low(kept, grad):
    return (low(grad),)
low.defvjp(low_keep, low_pass)
low_back.defvjp(back_keep, back_low)
norm_eps = 1e-06
hidden_fill = -1e+30
highest = lax.Precision.HIGHEST

def product(left, right):
    return jnp.dot(left, right, preferred_element_type=jnp.float32, precision=highest)

def layer_norm(summed, gain, bias):
    centered = summed - lax.optimization_barrier(jnp.mean(summed, -1, keepdims=True))
    factor = lax.rsqrt(lax.optimization_barrier(jnp.mean(centered * centered, -1, keepdims=True)) + norm_eps)
    return centered * factor * gain + bias

def attend_block(query_blk, key_win, value_win, start):
    raw = jnp.einsum('thd,khd->htk', query_blk, key_win, precision=highest) * HEAD_DIM ** (-0.5)
    scores = low_back(raw)
    query_pos = lax.broadcasted_iota(jnp.int32, (BLOCK, KEYS), 0) + FLANK_ROWS * LINE
    key_pos = lax.broadcasted_iota(jnp.int32, (BLOCK, KEYS), 1)
    visible = (key_pos <= query_pos) & (key_pos + start >= FLANK_ROWS * LINE)
    masked = jnp.where(visible[None], scores, hidden_fill)
    top = lax.optimization_barrier(jnp.max(masked, -1, keepdims=True))
    expo = jnp.exp(masked - top)
    probs = expo / lax.optimization_barrier(jnp.sum(expo, -1, keepdims=True))
    return jnp.einsum('htk,khd->thd', low(probs), value_win, precision=highest)

def image_forward(pixel_row, params):
    level_table, channel_table, attend_in, attend_out, first_gain, first_bias, expand_weight, expand_bias, shrink_weight, shrink_bias, second_gain, second_bias = params
    channel_ids = jnp.arange(SEQ, dtype=jnp.int32) % CHANNELS
    embedded = low_back(level_table[pixel_row] + channel_table[channel_ids])
    projected = low(low_back(product(low(embedded), attend_in)))
    pad_rows = FLANK_ROWS * LINE
    queries = projected[:, :D].reshape(BLOCKS, BLOCK, HEADS, HEAD_DIM)
    key_pad = jnp.pad(projected[:, D:2 * D].reshape(SEQ, HEADS, HEAD_DIM), ((pad_rows, 0), (0, 0), (0, 0)))
    value_pad = jnp.pad(projected[:, 2 * D:].reshape(SEQ, HEADS, HEAD_DIM), ((pad_rows, 0), (0, 0), (0, 0)))
    starts = jnp.arange(BLOCKS, dtype=jnp.int32) * BLOCK

    def one_block(pair):
        query_blk, start = pair
        key_win = lax.dynamic_slice_in_dim(key_pad, start, KEYS, 0)
        value_win = lax.dynamic_slice_in_dim(value_pad, start, KEYS, 0)
        return attend_block(query_blk, key_win, value_win, start)
    attended = lax.map(jax.checkpoint(one_block), (queries, starts))
    attended = low(low_back(attended.reshape(SEQ, D)))
    summed = embedded + low_back(product(attended, attend_out))
    hidden = layer_norm(summed, first_gain, first_bias)
    preact = low_back(product(low(hidden), expand_weight) + expand_bias)
    branch = low_back(product(low(jax.nn.silu(preact)), shrink_weight) + shrink_bias)
    return layer_norm(hidden + branch, second_gain, second_bias)

def reference(pixels, level_table, channel_table, attend_in, attend_out, first_gain, first_bias, expand_weight, expand_bias, shrink_weight, shrink_bias, second_gain, second_bias, cotangent):
    params = tuple((weight.astype(jnp.float32) for weight in (level_table, channel_table, attend_in, attend_out, first_gain, first_bias, expand_weight, expand_bias, shrink_weight, shrink_bias, second_gain, second_bias)))

    def forward(weights):
        return lax.map(lambda pixel_row: image_forward(pixel_row, weights), pixels)
    layer_out, pullback = jax.vjp(forward, params)
    grads = pullback(cotangent.astype(jnp.float32))[0]
    return (layer_out.astype(jnp.bfloat16), grads[0], grads[1], grads[2], grads[3], grads[4], grads[5], grads[6], grads[7], grads[8], grads[9], grads[10], grads[11])
```

```python
import functools

import jax
import jax.numpy as jnp
from jax import lax
from jax.experimental import pallas as pl
from jax.experimental.pallas import tpu as pltpu
from jax.sharding import PartitionSpec as P

D = 512
HEADS = 8
HEAD_DIM = 64
FF = 2048
LEVELS = 256
CHANNELS = 3
SEQ = 3072
BLOCK = 768
BANDS = SEQ // BLOCK
PAIRS = HEADS // 2
PAIR = 2 * HEAD_DIM
REACH = 2
SUB = 256
EXTRA = 16
EPS = 1e-6
LOG2E = 1.4426950408889634
SAFE = 60.0

f32 = jnp.float32
bf16 = jnp.bfloat16
NT = (((1,), (1,)), ((), ()))
TN = (((0,), (0,)), ((), ()))
VMEM_LIMIT = 60 * 2**20


def mm(a, b):
    return jnp.dot(a, b, preferred_element_type=f32)


def mm_nt(a, b):
    return lax.dot_general(a, b, NT, preferred_element_type=f32)


def mm_tn(a, b):
    return lax.dot_general(a, b, TN, preferred_element_type=f32)


def params(*semantics):
    return pltpu.CompilerParams(
        vmem_limit_bytes=VMEM_LIMIT, dimension_semantics=semantics or None
    )


def one_hot_rows(pix):
    width = pix.shape[1]
    return (lax.broadcasted_iota(jnp.int32, (LEVELS, width), 0) == pix).astype(bf16)


def split3(x):
    hi = x.astype(bf16).astype(f32)
    rest = x - hi
    mid = rest.astype(bf16).astype(f32)
    return hi, mid, rest - mid


class Place:
    def __init__(self, ways):
        self.n = ways // 2
        self.f = lax.axis_index("fsdp")
        self.d = lax.axis_index("dp")
        self.near = self.f % 2
        self.far = self.f // 2
        self.core = self.d % 2
        self.side = self.d // 2
        self.quarter = self.core * 2 + self.side

    def far_at(self, step):
        return (self.far + step) % self.n

    def to_core(self):
        return {"fsdp": self.f, "dp": self.d + 1 - 2 * self.core}

    def to_side(self):
        return {"fsdp": self.f, "dp": self.d + 2 - 4 * self.side}

    def to_near(self):
        return {"fsdp": self.f + 1 - 2 * self.near, "dp": self.d}

    def to_far(self, step):
        return {"fsdp": self.far_at(step) * 2 + self.near, "dp": self.d}

    def enter(self):
        barrier = pltpu.get_barrier_semaphore()
        mates = [self.to_core(), self.to_side(), self.to_near()]
        mates += [self.to_far(step) for step in range(1, self.n)]
        for mate in mates:
            pl.semaphore_signal(barrier, inc=1, device_id=mate, device_id_type=pl.DeviceIdType.MESH)
        pl.semaphore_wait(barrier, len(mates))


def send(src, dst, sems, i, device):
    return pltpu.make_async_remote_copy(
        src_ref=src,
        dst_ref=dst,
        send_sem=sems.at[0, i],
        recv_sem=sems.at[1, i],
        device_id=device,
        device_id_type=pl.DeviceIdType.MESH,
    )


def window(which, size, count=1):
    return pl.ds(pl.multiple_of(which * size, size), size * count)


class Gather:
    def __init__(self, place, src, dst, sems, across):
        self.place, self.src, self.dst, self.sems = place, src, dst, sems
        self.across, self.n = across, place.n

    @staticmethod
    def semaphores(ways):
        return pltpu.SemaphoreType.DMA((2, 3 * (ways // 2) + 2))

    def part(self, ref, lead, start, count):
        if self.across is None:
            return ref.at[lead]
        cut = window(start, self.dst.shape[2 + self.across] // 4, count)
        return ref.at[(*lead, cut) if self.across == 0 else (*lead, slice(None), cut)]

    def source(self):
        return self.part(self.src, (0,), self.place.quarter, 1)

    def mine(self):
        return self.part(self.dst, (self.place.far, self.place.near), self.place.quarter, 1)

    def pair(self, far, start, count):
        return self.part(self.dst, (far, slice(None)), start, count)

    def local(self):
        return pltpu.make_async_copy(self.source(), self.mine(), self.sems.at[0, 3 * self.n + 1])

    def near_copy(self):
        return send(self.source(), self.mine(), self.sems, 0, self.place.to_near())

    def far_copy(self, step):
        got = self.pair(self.place.far, self.place.quarter, 1)
        return send(got, got, self.sems, step, self.place.to_far(step))

    def side_copy(self, step):
        got = self.pair(self.place.far_at(self.n - step), self.place.quarter, 1)
        return send(got, got, self.sems, self.n + step, self.place.to_side())

    def core_copy(self, step):
        got = self.pair(self.place.far_at(self.n - step), self.place.core * 2, 2)
        return send(got, got, self.sems, 2 * self.n + step, self.place.to_core())

    def start(self):
        self.near_copy().start()
        self.local().start()

    def spread(self):
        self.local().wait()
        self.near_copy().wait()
        for step in range(1, self.n):
            self.far_copy(step).start()
        if self.across is not None:
            self.side_copy(0).start()

    def swap(self, step):
        if step:
            self.far_copy(step).wait()
            if self.across is not None:
                self.side_copy(step).start()

    def share(self, step):
        if self.across is not None:
            self.side_copy(step).wait()
            self.core_copy(step).start()

    def finish(self):
        if self.across is not None:
            for step in range(self.n):
                self.core_copy(step).wait()


class Reduce:
    def __init__(self, place, src, out, bufs):
        self.place, self.src, self.out, self.n = place, src, out, place.n
        self.r1, self.a1, self.r2, self.r3, self.r4, self.sems = bufs
        self.size = src.shape[2] // 4

    @staticmethod
    def scratch(ways, rows, cols):
        n = ways // 2
        return [
            pltpu.VMEM((n, 2, rows // 2, cols), bf16),
            pltpu.VMEM((n, 2, rows // 2, cols), bf16),
            pltpu.VMEM((n, 2, rows // 4, cols), bf16),
            pltpu.VMEM((n, rows // 4, cols), bf16),
            pltpu.VMEM((n - 1, rows // 4, cols), bf16),
            pltpu.SemaphoreType.DMA((2, n + 5)),
        ]

    def half(self, which):
        return self.src.at[:, :, window(which, 2 * self.size)]

    def local(self):
        return pltpu.make_async_copy(self.half(self.place.core), self.a1, self.sems.at[0, self.n + 4])

    def core_copy(self):
        return send(self.half(1 - self.place.core), self.r1, self.sems, 0, self.place.to_core())

    def side_copy(self):
        return send(
            self.a1.at[:, :, window(1 - self.place.side, self.size)], self.r2, self.sems, 1, self.place.to_side()
        )

    def near_copy(self):
        return send(self.r2.at[:, 1 - self.place.near], self.r3, self.sems, 2, self.place.to_near())

    def far_copy(self, step):
        return send(
            self.r3.at[self.place.far_at(step)], self.r4.at[step - 1], self.sems, 2 + step, self.place.to_far(step)
        )

    def side_back(self):
        got = self.out.at[window(self.place.quarter, self.size)]
        return send(got, got, self.sems, self.n + 2, self.place.to_side())

    def core_back(self):
        got = self.out.at[window(self.place.core, 2 * self.size)]
        return send(got, got, self.sems, self.n + 3, self.place.to_core())

    def start(self):
        self.core_copy().start()
        self.local().start()

    def over_sides(self):
        self.local().wait()
        self.core_copy().wait()

        @pl.loop(0, self.n)
        def _(i):
            for near in range(2):
                both = self.a1[i, near].astype(f32) + self.r1[i, near].astype(f32)
                self.a1[i, near] = both.astype(bf16)

        self.side_copy().start()

    def over_near(self):
        self.side_copy().wait()
        cut = window(self.place.side, self.size)

        @pl.loop(0, self.n)
        def _(i):
            for near in range(2):
                both = self.a1[i, near, cut].astype(f32) + self.r2[i, near].astype(f32)
                self.r2[i, near] = both.astype(bf16)

        self.near_copy().start()

    def over_far(self):
        self.near_copy().wait()
        near = self.place.near

        @pl.loop(0, self.n)
        def _(i):
            self.r3[i] = (self.r2[i, near].astype(f32) + self.r3[i].astype(f32)).astype(bf16)

        for step in range(1, self.n):
            self.far_copy(step).start()

    def settle(self):
        whole = self.r3[self.place.far].astype(f32)
        for step in range(1, self.n):
            self.far_copy(step).wait()
            whole = whole + self.r4[step - 1].astype(f32)
        self.out[window(self.place.quarter, self.size)] = whole
        self.side_back().start()

    def swap(self):
        self.side_back().wait()
        self.core_back().start()

    def finish(self):
        self.core_back().wait()

    stages = (start, over_sides, over_near, over_far, settle, swap, finish)


class ReduceSmall:
    def __init__(self, place, src, out, bufs):
        self.place, self.src, self.out, self.n = place, src, out, place.n
        self.r1, self.r2, self.r3, self.r4, self.sems = bufs

    @staticmethod
    def scratch(ways, rows, cols):
        n = ways // 2
        return [
            pltpu.VMEM((n, 2, rows, cols), f32),
            pltpu.VMEM((n, 2, rows, cols), f32),
            pltpu.VMEM((n, rows, cols), f32),
            pltpu.VMEM((n - 1, rows, cols), f32),
            pltpu.SemaphoreType.DMA((2, n + 2)),
        ]

    def core_copy(self):
        return send(self.src, self.r1, self.sems, 0, self.place.to_core())

    def side_copy(self):
        return send(self.src, self.r2, self.sems, 1, self.place.to_side())

    def near_copy(self):
        return send(self.src.at[:, 1 - self.place.near], self.r3, self.sems, 2, self.place.to_near())

    def far_copy(self, step):
        return send(
            self.r3.at[self.place.far_at(step)], self.r4.at[step - 1], self.sems, 2 + step, self.place.to_far(step)
        )

    def start(self):
        self.core_copy().start()

    def over_sides(self):
        self.core_copy().wait()
        self.src[...] += self.r1[...]
        self.side_copy().start()

    def over_near(self):
        self.side_copy().wait()
        self.src[...] += self.r2[...]
        self.near_copy().start()

    def over_far(self):
        self.near_copy().wait()
        for i in range(self.n):
            self.r3[i] += self.src[i, self.place.near]
        for step in range(1, self.n):
            self.far_copy(step).start()

    def settle(self):
        whole = self.r3[self.place.far]
        for step in range(1, self.n):
            self.far_copy(step).wait()
            whole = whole + self.r4[step - 1]
        self.out[...] = whole

    def swap(self):
        pass

    def finish(self):
        pass

    stages = (start, over_sides, over_near, over_far, settle, swap, finish)


def embed_tile(step, pix_ref, chan_ref, level, table, w, ind_ref, emb_ref, low_ref, qkv_ref, qt_ref, vt_ref, norm_ref):
    emb = mm_tn(one_hot_rows(pix_ref[...]), level) + mm_tn(chan_ref[...], table)
    emb_ref[...] = emb
    low = emb.astype(bf16)
    low_ref[...] = low
    qkv = mm(low, w)
    q = (qkv[:, :D] * HEAD_DIM**-0.5).astype(bf16)
    k = qkv[:, D : 2 * D].astype(bf16)
    v = qkv[:, 2 * D :].astype(bf16)
    qkv_ref[:, :D] = q
    qkv_ref[:, D : 2 * D] = k
    qkv_ref[:, 2 * D :] = v
    qt_ref[...] = q.T
    vt_ref[...] = v.T
    q = q.astype(f32)
    k = k.astype(f32)
    size_q = mm((q * q).astype(bf16), ind_ref[...]).max(0, keepdims=True)
    size_k = mm((k * k).astype(bf16), ind_ref[...]).max(0, keepdims=True)
    row = lax.broadcasted_iota(jnp.int32, (8, 128), 0)
    both = jnp.where(row == 0, size_q, jnp.where(row == 1, size_k, 0.0))
    norm_ref[...] = jnp.maximum(both, jnp.where(step == 0, 0.0, norm_ref[...]))


def embed_plain_kernel(pix_ref, chan_ref, level_ref, table_ref, w_ref, ind_ref, *outs):
    embed_tile(pl.program_id(0), pix_ref, chan_ref, level_ref[...], table_ref[...], w_ref[...], ind_ref, *outs)


def embed_outs():
    rows = lambda i: (i, 0)
    cols = lambda i: (0, i)
    specs = [
        pl.BlockSpec((BLOCK, D), rows),
        pl.BlockSpec((BLOCK, D), rows),
        pl.BlockSpec((BLOCK, 3 * D), rows),
        pl.BlockSpec((D, BLOCK), cols),
        pl.BlockSpec((D, BLOCK), cols),
        pl.BlockSpec((8, 128), lambda i: (0, 0)),
    ]
    shapes = [
        jax.ShapeDtypeStruct((SEQ, D), f32),
        jax.ShapeDtypeStruct((SEQ, D), bf16),
        jax.ShapeDtypeStruct((SEQ, 3 * D), bf16),
        jax.ShapeDtypeStruct((D, SEQ), bf16),
        jax.ShapeDtypeStruct((D, SEQ), bf16),
        jax.ShapeDtypeStruct((8, 128), f32),
    ]
    return specs, shapes


def head_columns():
    return (jnp.arange(D)[:, None] // HEAD_DIM == jnp.arange(128)[None, :]).astype(bf16)


def embed_plain(pix, chan, level, table, w_in):
    whole = lambda i: (0, 0)
    specs, shapes = embed_outs()
    return pl.pallas_call(
        embed_plain_kernel,
        grid=(SEQ // BLOCK,),
        in_specs=[
            pl.BlockSpec((1, BLOCK), lambda i: (0, i)),
            pl.BlockSpec((EXTRA, BLOCK), whole),
            pl.BlockSpec((LEVELS, D), whole),
            pl.BlockSpec((EXTRA, D), whole),
            pl.BlockSpec((D, 3 * D), whole),
            pl.BlockSpec((D, 128), whole),
        ],
        out_specs=specs,
        out_shape=shapes,
        compiler_params=params("arbitrary"),
    )(pix, chan, level, table, w_in, head_columns())


def half_lanes(even, odd):
    lane = lax.broadcasted_iota(jnp.int32, even.shape, 1)
    return jnp.where(lane < HEAD_DIM, even, pltpu.roll(odd, HEAD_DIM, 1))


def embed_gather_kernel(
    ways, pix_ref, chan_ref, ind_ref, level_ref, small_ref, win_ref, wo_ref, we_ref, ws_ref,
    emb_ref, low_ref, qkv_ref, qt_ref, vt_ref, norm_ref, vec_ref, be_ref, w4_ref, wo_out, we_out, ws_out,
    level_s, small_s, win_s, sem_level, sem_small, sem_in, sem_o, sem_e, sem_s, sem_w4,
):
    step = pl.program_id(0)
    place = Place(ways)
    n = place.n
    first = [
        Gather(place, level_ref, level_s, sem_level, 1),
        Gather(place, small_ref, small_s, sem_small, None),
        Gather(place, win_ref, win_s, sem_in, 0),
    ]
    later = [
        Gather(place, wo_ref, wo_out, sem_o, 0),
        Gather(place, we_ref, we_out, sem_e, 0),
        Gather(place, ws_ref, ws_out, sem_s, 0),
    ]

    def copies():
        for i in range(3 * PAIRS):
            yield pltpu.make_async_copy(win_s.at[:, :, :, i * PAIR : (i + 1) * PAIR], w4_ref.at[i], sem_w4.at[i])

    @pl.when(step == 0)
    def _():
        place.enter()
        for g in first + later:
            g.start()
        for g in first:
            g.spread()
        for i in range(n):
            for g in first:
                g.swap(i)
            if i == 0:
                for g in later:
                    g.spread()
            for g in first:
                g.share(i)
        for g in first:
            g.finish()
        for i in range(n):
            both = [small_s[i, near].astype(f32) for near in range(2)]
            vec_ref[:, i * 128 : (i + 1) * 128] = half_lanes(*both)
            for near in range(2):
                for j in range(2):
                    at = ((2 * i + near) * 2 + j) * 128
                    be_ref[0:1, at : at + 128] = both[near][8 + j : 9 + j]
        for copy in copies():
            copy.start()

    table = vec_ref[...].astype(bf16)
    level = level_s[...].reshape(LEVELS, D)
    w = win_s[...].reshape(D, 3 * D)
    embed_tile(step, pix_ref, chan_ref, level, table, w, ind_ref, emb_ref, low_ref, qkv_ref, qt_ref, vt_ref, norm_ref)

    for at in range(n):
        @pl.when(step == at * (SEQ // BLOCK - 1) // n)
        def _():
            for g in later:
                g.swap(at)

    @pl.when(step == SEQ // BLOCK - 2)
    def _():
        for i in range(n):
            for g in later:
                g.share(i)

    @pl.when(step == SEQ // BLOCK - 1)
    def _():
        for copy in copies():
            copy.wait()
        for g in later:
            g.finish()


def embed_gather(ways, pix, chan, level, small, w_in, wo, we, ws):
    n = ways // 2
    whole = lambda i: (0, 0)
    anywhere = pl.BlockSpec(memory_space=pl.ANY)
    specs, shapes = embed_outs()
    shards = [x[None] for x in (level, small, w_in, wo, we, ws)]
    wide = [jax.ShapeDtypeStruct((n, 2, *x.shape), bf16) for x in (wo, we, ws)]
    return pl.pallas_call(
        functools.partial(embed_gather_kernel, ways),
        grid=(SEQ // BLOCK,),
        in_specs=[
            pl.BlockSpec((1, BLOCK), lambda i: (0, i)),
            pl.BlockSpec((EXTRA, BLOCK), whole),
            pl.BlockSpec((D, 128), whole),
            *[anywhere] * 6,
        ],
        out_specs=[*specs, pl.BlockSpec((EXTRA, D), whole), pl.BlockSpec((8, FF), whole), *[anywhere] * 4],
        out_shape=[
            *shapes,
            jax.ShapeDtypeStruct((EXTRA, D), f32),
            jax.ShapeDtypeStruct((8, FF), f32),
            jax.ShapeDtypeStruct((3 * PAIRS, n, 2, D // ways, PAIR), bf16),
            *wide,
        ],
        scratch_shapes=[
            *[pltpu.VMEM((n, 2, *x.shape), bf16) for x in (level, small, w_in)],
            *[Gather.semaphores(ways)] * 6,
            pltpu.SemaphoreType.DMA((3 * PAIRS,)),
        ],
        compiler_params=pltpu.CompilerParams(
            vmem_limit_bytes=VMEM_LIMIT, dimension_semantics=("arbitrary",), collective_id=0, has_side_effects=True
        ),
    )(pix, chan, head_columns(), *shards)


def units():
    found = []
    for band in range(BANDS):
        found += [(band, j) for j in range(max(0, band - REACH), band + 1)]
    return found


def lower_mask(keys, queries):
    key = lax.broadcasted_iota(jnp.int32, (keys, queries), 0)
    return key <= lax.broadcasted_iota(jnp.int32, (keys, queries), 1)


def spare_rows(x):
    row = lax.broadcasted_iota(jnp.int32, (HEAD_DIM, x.shape[1]), 0)
    hi, mid, low = split3(x)
    return jnp.where(row == 0, hi, jnp.where(row == 1, mid, jnp.where(row == 2, low, 0.0)))


def attend_kernel(flag_ref, q_ref, k_ref, vt_ref, o_ref, qe_ref, acc, lsum, probs, shift, top, ke):
    lane = lax.broadcasted_iota(jnp.int32, (BLOCK, PAIR), 1)
    shift[...] = jnp.zeros_like(shift)
    top[...] = jnp.zeros_like(top)
    for band in range(BANDS):
        here = slice(band * BLOCK, (band + 1) * BLOCK)
        k = k_ref[here, :]
        one = jnp.ones_like(k)
        zero = jnp.zeros_like(k)
        ke[0, here] = jnp.where(lane < HEAD_DIM, k, jnp.where(lane < HEAD_DIM + 3, one, zero))
        ke[1, here] = jnp.where(lane < HEAD_DIM, jnp.where(lane < 3, one, zero), k)

    def head_only(q, h, other):
        mine = (lane < HEAD_DIM) if h == 0 else (lane >= HEAD_DIM)
        return jnp.where(mine, q, other)

    @pl.when(flag_ref[0] != 0)
    def _():
        for band in range(BANDS):
            here = slice(band * BLOCK, (band + 1) * BLOCK)
            ext = [None, None]
            for h in range(2):
                qm = head_only(q_ref[here, :], h, jnp.zeros((BLOCK, PAIR), bf16))
                lsum[h] = jnp.full((8, BLOCK), -1e30, f32)
                for j in range(max(0, band - REACH), band + 1):

                    @pl.loop(0, BLOCK // 128)
                    def _(i):
                        start = pl.multiple_of(j * BLOCK + i * 128, 128)
                        scores = mm_nt(k_ref[pl.ds(start, 128), :], qm)
                        if j == band:
                            key = lax.broadcasted_iota(jnp.int32, scores.shape, 0) + i * 128
                            scores = jnp.where(key <= lax.broadcasted_iota(jnp.int32, scores.shape, 1), scores, -1e30)
                        lsum[h] = jnp.maximum(lsum[h], scores.max(0, keepdims=True))

                top[h, band] = lsum[h]
                ext[1 - h] = spare_rows(-lsum[h, 0:1])
            shift[here, :] = jnp.concatenate(ext, 0).T.astype(bf16)

    for band, j in units():
        here = slice(band * BLOCK, (band + 1) * BLOCK)
        first = j == max(0, band - REACH)
        q = q_ref[here, :]
        off = shift[here, :]
        tiles = [(0, BLOCK, BLOCK)] if j < band else [(t * SUB, SUB, (t + 1) * SUB) for t in range(BLOCK // SUB)]
        for h in range(2):
            qm = head_only(q, h, off)
            for at, width, count in tiles:
                ts = slice(at, at + width)
                scores = mm_nt(ke[h, j * BLOCK : j * BLOCK + count, :], qm[ts])
                p = jnp.exp2(scores * LOG2E)
                if j == band:
                    diag = jnp.where(lower_mask(SUB, SUB), p[count - SUB :], 0.0)
                    p = diag if count == SUB else jnp.concatenate([p[: count - SUB], diag], 0)
                part = p.reshape(count // 8, 8, width).sum(0)
                if not first:
                    part += lsum[h, :, ts]
                lsum[h, :, ts] = part
                probs[h, :count, ts] = p.astype(bf16)
        ext = [None, None]
        for h in range(2):
            mine = slice(h * HEAD_DIM, (h + 1) * HEAD_DIM)
            for at, width, count in tiles:
                ts = slice(at, at + width)
                out = mm(vt_ref[mine, j * BLOCK : j * BLOCK + count], probs[h, :count, ts])
                if not first:
                    out += acc[mine, ts]
                acc[mine, ts] = out
            if j == band:
                whole = lsum[h].sum(0, keepdims=True)
                acc[mine, :] = acc[mine, :] / whole
                ext[1 - h] = spare_rows(-(top[h, band, 0:1] + jnp.log(whole)))
        if j == band:
            o_ref[here, :] = acc[...].T.astype(bf16)
            extra = jnp.concatenate(ext, 0).T.astype(bf16)
            qe_ref[here, :PAIR] = head_only(q, 0, extra)
            qe_ref[here, PAIR:] = head_only(q, 1, extra)


def attend(flag, qkv, vt):
    return pl.pallas_call(
        attend_kernel,
        grid=(PAIRS,),
        in_specs=[
            pl.BlockSpec(memory_space=pltpu.SMEM),
            pl.BlockSpec((SEQ, PAIR), lambda p: (0, p)),
            pl.BlockSpec((SEQ, PAIR), lambda p: (0, PAIRS + p)),
            pl.BlockSpec((PAIR, SEQ), lambda p: (p, 0)),
        ],
        out_specs=[
            pl.BlockSpec((SEQ, PAIR), lambda p: (0, p)),
            pl.BlockSpec((SEQ, 2 * PAIR), lambda p: (0, p)),
        ],
        out_shape=[
            jax.ShapeDtypeStruct((SEQ, D), bf16),
            jax.ShapeDtypeStruct((SEQ, 2 * D), bf16),
        ],
        scratch_shapes=[
            pltpu.VMEM((PAIR, BLOCK), f32),
            pltpu.VMEM((2, 8, BLOCK), f32),
            pltpu.VMEM((2, BLOCK, BLOCK), bf16),
            pltpu.VMEM((SEQ, PAIR), bf16),
            pltpu.VMEM((2, BANDS, 8, BLOCK), f32),
            pltpu.VMEM((2, SEQ, PAIR), bf16),
        ],
        compiler_params=params("arbitrary"),
    )(flag, qkv, qkv, vt)


def mean(x):
    return jnp.mean(x, -1, keepdims=True)


def norm(x):
    centered = x - mean(x)
    factor = lax.rsqrt(mean(centered * centered) + EPS)
    return centered * factor, factor


def norm_back(scaled, normed, factor):
    return factor * (scaled - mean(scaled) - normed * mean(scaled * normed))


def total(x):
    return x.sum(0, keepdims=True)


def middle_kernel(
    att_ref, emb_ref, cot_ref, wo_ref, we_ref, ws_ref, vec_ref, be_ref, pick_ref,
    out_ref, go_ref, de_ref, dt_ref, gwo_out, gwe_out, gws_out, gvec_ref, gbe_ref, gwo_ref, gwe_ref, gws_ref,
):
    @pl.when(pl.program_id(0) == 0)
    def _():
        for ref in (gwo_ref, gwe_ref, gws_ref, gvec_ref, gbe_ref):
            ref[...] = jnp.zeros_like(ref)

    gain1, bias1, bs, gain2, bias2 = [vec_ref[i : i + 1, :] for i in range(5)]
    att = att_ref[...]
    cot = cot_ref[...]
    normed1, factor1 = norm(emb_ref[...] + mm(att, wo_ref[...]))
    hidden = normed1 * gain1 + bias1
    low = hidden.astype(bf16)
    preact = mm(low, we_ref[...]) + be_ref[0:1, :]
    sig = jax.nn.sigmoid(preact)
    activ = (preact * sig).astype(bf16)
    slope = sig * (1.0 + preact * (1.0 - sig))
    normed2, factor2 = norm(hidden + mm(activ, ws_ref[...]) + bs)
    out_ref[...] = (normed2 * gain2 + bias2).astype(bf16)
    gtwo = norm_back(cot * gain2, normed2, factor2)
    gbranch = gtwo.astype(bf16)
    gws_ref[...] += mm_tn(activ, gbranch)
    gpre = (mm_nt(gbranch, ws_ref[...]) * slope).astype(bf16)
    gbe_ref[0:1, :] += total(gpre.astype(f32))
    gwe_ref[...] += mm_tn(low, gpre)
    ghidden = gtwo + mm_nt(gpre, we_ref[...])
    gone = norm_back(ghidden * gain1, normed1, factor1)
    go_ref[...] = gone
    gatt_branch = gone.astype(bf16)
    gwo_ref[...] += mm_tn(att, gatt_branch)
    gatt = mm_nt(gatt_branch, wo_ref[...]).astype(bf16)
    dt_ref[...] = gatt.T
    gvec_ref[0:1, :] += total(ghidden * normed1)
    gvec_ref[1:2, :] += total(ghidden)
    gvec_ref[2:3, :] += total(gbranch.astype(f32))
    gvec_ref[3:4, :] += total(cot * normed2)
    gvec_ref[4:5, :] += total(cot)

    @pl.when(pl.program_id(0) == pl.num_programs(0) - 1)
    def _():
        gwo_out[...] = gwo_ref[...].astype(bf16)
        gwe_out[...] = gwe_ref[...].astype(bf16)
        gws_out[...] = gws_ref[...].astype(bf16)

    prod = gatt.astype(f32) * att.astype(f32)
    hi, mid, _ = split3(prod)
    pick = pick_ref[...]
    half = D // 2
    place = lax.broadcasted_iota(jnp.int32, (att.shape[0], half), 1) % HEAD_DIM
    lane = lax.broadcasted_iota(jnp.int32, (att.shape[0], PAIR), 1)
    for part in range(2):
        cols = slice(part * half, (part + 1) * half)
        inner = mm(hi[:, cols].astype(bf16), pick) + mm(mid[:, cols].astype(bf16), pick)
        a, b, c = split3(inner)
        ext = jnp.where(place == 0, a, jnp.where(place == 1, b, jnp.where(place == 2, c, 0.0))).astype(bf16)
        for i in range(2):
            pair = 2 * part + i
            e = ext[:, i * PAIR : (i + 1) * PAIR]
            d = gatt[:, pair * PAIR : (pair + 1) * PAIR]
            de_ref[:, 2 * pair * PAIR : (2 * pair + 1) * PAIR] = jnp.where(lane < HEAD_DIM, d, e)
            de_ref[:, (2 * pair + 1) * PAIR : (2 * pair + 2) * PAIR] = jnp.where(lane < HEAD_DIM, e, d)


def middle(att, emb, cot, wo, we, ws, vec, be):
    tile = 512
    half = D // 2
    src = jnp.arange(half)[:, None] // HEAD_DIM
    dst = jnp.arange(half)[None, :]
    other = (dst // HEAD_DIM) ^ 1
    pick = jnp.where((src == other) & (dst % HEAD_DIM < 3), -1.0, 0.0).astype(bf16)
    whole = lambda i: (0, 0)
    rows = lambda i: (i, 0)
    cols = lambda i: (0, i)
    one = pl.Buffered(1)
    return pl.pallas_call(
        middle_kernel,
        grid=(SEQ // tile,),
        in_specs=[
            pl.BlockSpec((tile, D), rows),
            pl.BlockSpec((tile, D), rows),
            pl.BlockSpec((tile, D), rows),
            pl.BlockSpec((D, D), whole, pipeline_mode=one),
            pl.BlockSpec((D, FF), whole, pipeline_mode=one),
            pl.BlockSpec((FF, D), whole, pipeline_mode=one),
            pl.BlockSpec((EXTRA, D), whole),
            pl.BlockSpec((8, FF), whole),
            pl.BlockSpec((half, half), whole),
        ],
        out_specs=[
            pl.BlockSpec((tile, D), rows),
            pl.BlockSpec((tile, D), rows),
            pl.BlockSpec((tile, 2 * D), rows),
            pl.BlockSpec((D, tile), cols),
            pl.BlockSpec((D, D), whole, pipeline_mode=one),
            pl.BlockSpec((D, FF), whole, pipeline_mode=one),
            pl.BlockSpec((FF, D), whole, pipeline_mode=one),
            pl.BlockSpec((8, D), whole),
            pl.BlockSpec((8, FF), whole),
        ],
        out_shape=[
            jax.ShapeDtypeStruct((SEQ, D), bf16),
            jax.ShapeDtypeStruct((SEQ, D), f32),
            jax.ShapeDtypeStruct((SEQ, 2 * D), bf16),
            jax.ShapeDtypeStruct((D, SEQ), bf16),
            jax.ShapeDtypeStruct((D, D), bf16),
            jax.ShapeDtypeStruct((D, FF), bf16),
            jax.ShapeDtypeStruct((FF, D), bf16),
            jax.ShapeDtypeStruct((8, D), f32),
            jax.ShapeDtypeStruct((8, FF), f32),
        ],
        scratch_shapes=[pltpu.VMEM((D, D), f32), pltpu.VMEM((D, FF), f32), pltpu.VMEM((FF, D), f32)],
        compiler_params=params("arbitrary"),
    )(att, emb, cot, wo, we, ws, vec, be, pick)


def back_kernel(
    ways, qe_ref, k_ref, v_ref, de_ref, qt_ref, dt_ref, low_ref, w_ref, pix_ref, chan_ref, go_ref,
    gw_ref, glev_ref, gchan_ref,
    ke, ve, km, probs, slopes, dkt, dvt, dqa, grads, gemb, sem,
):
    pair = pl.program_id(0)
    copy = pltpu.make_async_copy(go_ref, gemb, sem)

    @pl.when(pair == 0)
    def _():
        copy.start()

    lane = lax.broadcasted_iota(jnp.int32, (BLOCK, PAIR), 1)
    for band in range(BANDS):
        here = slice(band * BLOCK, (band + 1) * BLOCK)
        k = k_ref[here, :]
        v = v_ref[here, :]
        one = jnp.ones_like(k)
        zero = jnp.zeros_like(k)
        right = jnp.where(lane < HEAD_DIM + 3, one, zero)
        left = jnp.where(lane < 3, one, zero)
        ke[0, here] = jnp.where(lane < HEAD_DIM, k, right)
        ke[1, here] = jnp.where(lane < HEAD_DIM, left, k)
        ve[0, here] = jnp.where(lane < HEAD_DIM, v, right)
        ve[1, here] = jnp.where(lane < HEAD_DIM, left, v)
        km[0, here] = jnp.where(lane < HEAD_DIM, k, zero)
        km[1, here] = jnp.where(lane < HEAD_DIM, zero, k)
    for band, j in units():
        t0 = band * BLOCK
        k0 = j * BLOCK
        first = j == max(0, band - REACH)
        tiles = [(0, BLOCK)] if j < band else [(i * SUB, SUB) for i in range(BLOCK // SUB)]
        for h in range(2):
            mine = slice(h * HEAD_DIM, (h + 1) * HEAD_DIM)
            lanes = slice(h * PAIR, (h + 1) * PAIR)
            for at, count in tiles:
                ts = slice(t0 + at, t0 + BLOCK)
                ks = slice(k0 + at, k0 + at + count)
                scores = mm_nt(qe_ref[ts, lanes], ke[h, ks])
                p = jnp.exp2(scores * LOG2E)
                if j == band:
                    t = lax.broadcasted_iota(jnp.int32, p.shape, 0)
                    p = jnp.where(lax.broadcasted_iota(jnp.int32, p.shape, 1) <= t, p, 0.0)
                dp = mm_nt(de_ref[ts, lanes], ve[h, ks])
                cols = slice(at, at + count)
                probs[h, at:, cols] = p.astype(bf16)
                slopes[h, at:, cols] = (p * dp).astype(bf16)
                dv = mm(dt_ref[mine, ts], probs[h, at:, cols])
                dk = mm(qt_ref[mine, ts], slopes[h, at:, cols])
                if j == band:
                    dvt[mine, ks] = dv
                    dkt[mine, ks] = dk
                else:
                    dvt[mine, ks] += dv
                    dkt[mine, ks] += dk
        if j < band:
            dq = mm(slopes[0], km[0, k0 : k0 + BLOCK]) + mm(slopes[1], km[1, k0 : k0 + BLOCK])
            if first:
                dqa[...] = dq
            else:
                dqa[...] += dq
        else:
            for i in range(BLOCK // SUB):
                count = (i + 1) * SUB
                rows = slice(i * SUB, count)
                dq = mm(slopes[0, rows, :count], km[0, k0 : k0 + count])
                dq += mm(slopes[1, rows, :count], km[1, k0 : k0 + count])
                if not first:
                    dq += dqa[rows]
                grads[t0 + i * SUB : t0 + count, :PAIR] = (dq * HEAD_DIM**-0.5).astype(bf16)
    for band in range(BANDS):
        here = slice(band * BLOCK, (band + 1) * BLOCK)
        grads[here, PAIR : 2 * PAIR] = dkt[:, here].T.astype(bf16)
        grads[here, 2 * PAIR :] = dvt[:, here].T.astype(bf16)

    gw_ref[0] = mm_tn(low_ref[...], grads[...]).astype(bf16)

    @pl.when(pair == 0)
    def _():
        copy.wait()

    w = jnp.concatenate([w_ref[0, 0], w_ref[1, 0], w_ref[2, 0]], 1)
    for band in range(BANDS):
        here = slice(band * BLOCK, (band + 1) * BLOCK)
        gemb[here] += mm_nt(grads[here, :], w)

    @pl.when(pair == PAIRS - 1)
    def _():
        table = None
        for band in range(BANDS):
            here = slice(band * BLOCK, (band + 1) * BLOCK)
            rows = jnp.concatenate([one_hot_rows(pix_ref[:, here]), chan_ref[...]], 0)
            part = mm(rows, gemb[here].astype(bf16))
            table = part if band == 0 else table + part
        gchan_ref[...] = table[LEVELS:]
        count = LEVELS // ways
        for f in range(ways):
            mine = table[f * count : (f + 1) * count].astype(bf16)
            glev_ref[f, :count] = mine[:, : D // 2]
            glev_ref[f, count:] = mine[:, D // 2 :]


def back(ways, qe, qkv, de, qt, dt, low, w4, pix, chan, gone):
    one = pl.Buffered(1)
    return pl.pallas_call(
        functools.partial(back_kernel, ways),
        grid=(PAIRS,),
        in_specs=[
            pl.BlockSpec((SEQ, 2 * PAIR), lambda p: (0, p)),
            pl.BlockSpec((SEQ, PAIR), lambda p: (0, PAIRS + p)),
            pl.BlockSpec((SEQ, PAIR), lambda p: (0, 2 * PAIRS + p)),
            pl.BlockSpec((SEQ, 2 * PAIR), lambda p: (0, p)),
            pl.BlockSpec((PAIR, SEQ), lambda p: (p, 0)),
            pl.BlockSpec((PAIR, SEQ), lambda p: (p, 0)),
            pl.BlockSpec((SEQ, D), lambda p: (0, 0), pipeline_mode=one),
            pl.BlockSpec((3, 1, D, PAIR), lambda p: (0, p, 0, 0)),
            pl.BlockSpec((1, SEQ), lambda p: (0, 0)),
            pl.BlockSpec((EXTRA, BLOCK), lambda p: (0, 0)),
            pl.BlockSpec(memory_space=pl.ANY),
        ],
        out_specs=[
            pl.BlockSpec((1, D, 3 * PAIR), lambda p: (p, 0, 0)),
            pl.BlockSpec((ways, 2 * LEVELS // ways, D // 2), lambda p: (0, 0, 0)),
            pl.BlockSpec((EXTRA, D), lambda p: (0, 0)),
        ],
        out_shape=[
            jax.ShapeDtypeStruct((PAIRS, D, 3 * PAIR), bf16),
            jax.ShapeDtypeStruct((ways, 2 * LEVELS // ways, D // 2), bf16),
            jax.ShapeDtypeStruct((EXTRA, D), f32),
        ],
        scratch_shapes=[
            pltpu.VMEM((2, SEQ, PAIR), bf16),
            pltpu.VMEM((2, SEQ, PAIR), bf16),
            pltpu.VMEM((2, SEQ, PAIR), bf16),
            pltpu.VMEM((2, BLOCK, BLOCK), bf16),
            pltpu.VMEM((2, BLOCK, BLOCK), bf16),
            pltpu.VMEM((PAIR, SEQ), f32),
            pltpu.VMEM((PAIR, SEQ), f32),
            pltpu.VMEM((BLOCK, PAIR), f32),
            pltpu.VMEM((SEQ, 3 * PAIR), bf16),
            pltpu.VMEM((SEQ, D), f32),
            pltpu.SemaphoreType.DMA,
        ],
        compiler_params=params("arbitrary"),
    )(qe, qkv, qkv, de, qt, dt, low, w4, pix, chan, gone)


def reduce_kernel(ways, *refs):
    wo, we, ws, win, lev, gvec, gbe, gchan, o_out, e_out, s_out, in_out, lev_out, small_out, *scratch = refs
    place = Place(ways)
    n = place.n
    scratch = list(scratch)
    take = lambda count: [scratch.pop(0) for _ in range(count)]
    in_sum = take(PAIRS)
    lev_sum, small_src = take(2)
    chunks = [Reduce(place, src, out, take(6)) for src, out in ((ws, s_out), (we, e_out), (wo, o_out))]
    chunks += [Reduce(place, win.at[p], in_sum[p], take(6)) for p in range(PAIRS)]
    chunks += [Reduce(place, lev, lev_sum, take(6)), ReduceSmall(place, small_src, small_out, take(5))]
    small_src[...] = jnp.zeros_like(small_src)
    comb = gvec[...] + gchan[0:8]
    for i in range(n):
        cols = comb[:, i * 128 : (i + 1) * 128]
        for near in range(2):
            small_src[i, near, 0:8] = cols if near == 0 else pltpu.roll(cols, HEAD_DIM, 1)
            for j in range(2):
                at = ((2 * i + near) * 2 + j) * 128
                small_src[i, near, 8 + j : 9 + j] = gbe[0:1, at : at + 128]
    place.enter()
    for stage in range(len(Reduce.stages)):
        for chunk in chunks:
            chunk.stages[stage](chunk)
    for p in range(PAIRS):
        for part in range(3):
            at = (part * PAIRS + p) * PAIR
            in_out[:, at : at + PAIR] = in_sum[p][:, part * PAIR : (part + 1) * PAIR]
    half = lev_out.shape[0]
    lev_out[:, : D // 2] = lev_sum[:half]
    lev_out[:, D // 2 :] = lev_sum[half:]


def reduce_all(ways, gwo, gwe, gws, gw, glev, gvec, gbe, gchan):
    n = ways // 2
    split = lambda x: x.reshape(n, 2, x.shape[0] // ways, x.shape[1])
    rows = D // ways
    vmem = pl.BlockSpec(memory_space=pltpu.VMEM)
    anywhere = pl.BlockSpec(memory_space=pl.ANY)
    sizes = [(FF // ways, D), (rows, FF), (rows, D)] + [(rows, 3 * PAIR)] * PAIRS + [(2 * LEVELS // ways, D // 2)]
    scratch = [pltpu.VMEM((rows, 3 * PAIR), f32)] * PAIRS
    scratch += [pltpu.VMEM(sizes[-1], f32), pltpu.VMEM((n, 2, EXTRA, 128), f32)]
    for size in sizes:
        scratch += Reduce.scratch(ways, *size)
    scratch += ReduceSmall.scratch(ways, EXTRA, 128)
    return pl.pallas_call(
        functools.partial(reduce_kernel, ways),
        in_specs=[*[anywhere] * 5, *[vmem] * 3],
        out_specs=[vmem] * 6,
        out_shape=[
            jax.ShapeDtypeStruct((rows, D), f32),
            jax.ShapeDtypeStruct((rows, FF), f32),
            jax.ShapeDtypeStruct((FF // ways, D), f32),
            jax.ShapeDtypeStruct((rows, 3 * D), f32),
            jax.ShapeDtypeStruct((LEVELS // ways, D), f32),
            jax.ShapeDtypeStruct((EXTRA, 128), f32),
        ],
        scratch_shapes=scratch,
        compiler_params=pltpu.CompilerParams(vmem_limit_bytes=VMEM_LIMIT, collective_id=1, has_side_effects=True),
    )(
        split(gwo), split(gwe), split(gws), gw.reshape(PAIRS, n, 2, rows, 3 * PAIR),
        glev.reshape(n, 2, *glev.shape[1:]), gvec, gbe, gchan,
    )


def channel_rows():
    pos = jnp.arange(BLOCK, dtype=jnp.int32) % CHANNELS + 5
    return (jnp.arange(EXTRA, dtype=jnp.int32)[:, None] == pos[None, :]).astype(bf16)


def image(ways, pix, cot, chan, embedded, weights):
    emb, low, qkv, qt, vt, sizes = embedded
    w4, wo, vec, we, be, ws = weights
    bound = jnp.max(jnp.sqrt(sizes[0] * sizes[1])) * 1.01
    flag = jnp.where(bound < SAFE, 0, 1).astype(jnp.int32).reshape(1)
    att, qe = attend(flag, qkv, vt)
    out, gone, de, dt, *grads = middle(att, emb, cot, wo, we, ws, vec, be)
    return out, *grads, *back(ways, qe, qkv, de, qt, dt, low, w4, pix, chan, gone)


def pack_small(vectors, channels, bias):
    size = bias.shape[0] // 128
    rows = jnp.concatenate([jnp.stack(vectors), channels])
    rows = jnp.pad(rows, ((0, 0), (0, 128 - rows.shape[1])))
    return jnp.concatenate([rows, bias.reshape(size, 128), jnp.zeros((EXTRA - 8 - size, 128), bf16)])


def body(
    ways, pixels, level_table, channel_table, attend_in, attend_out, first_gain, first_bias, expand_weight,
    expand_bias, shrink_weight, shrink_bias, second_gain, second_bias, cotangent,
):
    chan = channel_rows()
    vectors = (first_gain, first_bias, shrink_bias, second_gain, second_bias)
    small = pack_small(vectors, channel_table, expand_bias)
    *embedded, vec, be, w4, wo, we, ws = embed_gather(
        ways, pixels, chan, level_table, small, attend_in, attend_out, expand_weight, shrink_weight
    )
    w4 = w4.reshape(3, PAIRS, D, PAIR)
    weights = (w4, wo.reshape(D, D), vec, we.reshape(D, FF), be, ws.reshape(FF, D))
    out, gwo, gwe, gws, gvec, gbe, gw, glev, gchan = image(ways, pixels, cotangent[0], chan, embedded, weights)
    gwo, gwe, gws, gwin, glev, small = reduce_all(ways, gwo, gwe, gws, gw, glev, gvec, gbe, gchan)
    each = D // ways
    return (
        out[None], glev, small[5:8, :each], gwin, gwo, small[0, :each], small[1, :each], gwe,
        small[8:10].reshape(FF // ways), gws, small[2, :each], small[3, :each], small[4, :each],
    )


def plain_body(
    ways, pixels, level_table, channel_table, attend_in, attend_out, first_gain, first_bias, expand_weight,
    expand_bias, shrink_weight, shrink_bias, second_gain, second_bias, cotangent,
):
    gather = lambda x, axis=0: lax.all_gather(x, "fsdp", axis=axis, tiled=True)
    vectors = jnp.stack((first_gain, first_bias, shrink_bias, second_gain, second_bias))
    chan = channel_rows()
    small = gather(jnp.concatenate([vectors, channel_table]), 1)
    table = jnp.pad(small, ((0, EXTRA - 8), (0, 0)))
    level = gather(level_table)
    w_in = gather(attend_in)
    be = jnp.pad(gather(expand_bias).astype(f32)[None], ((0, 7), (0, 0)))
    w4 = w_in.reshape(D, 3, PAIRS, PAIR).transpose(1, 2, 0, 3)
    weights = (w4, gather(attend_out), table.astype(f32), gather(expand_weight), be, gather(shrink_weight))
    outs = []
    sums = None
    for i in range(pixels.shape[0]):
        pix = pixels[i : i + 1]
        got = image(ways, pix, cotangent[i], chan, embed_plain(pix, chan, level, table, w_in), weights)
        outs.append(got[0])
        grads = [x.astype(f32) for x in got[1:]]
        sums = grads if sums is None else [a + b for a, b in zip(sums, grads)]
    gwo, gwe, gws, gvec, gbe, gw, glev, gchan = sums
    gwin = gw.reshape(PAIRS, D, 3, PAIR).transpose(1, 2, 0, 3).reshape(D, 3 * D)
    count = LEVELS // ways
    glev = glev.reshape(ways, 2, count, D // 2).transpose(0, 2, 1, 3).reshape(LEVELS, D)

    def scatter(x, axis=0):
        return lax.psum(lax.psum_scatter(x, "fsdp", scatter_dimension=axis, tiled=True), "dp")

    small = scatter(gvec + gchan[:8], 1)
    return (
        jnp.stack(outs), scatter(glev), small[5:8], scatter(gwin), scatter(gwo), small[0], small[1], scatter(gwe),
        scatter(gbe[0]), scatter(gws), small[2], small[3], small[4],
    )


def solution(mesh):
    row = P("fsdp", None)
    vector = P("fsdp")
    shared = P(("fsdp", "dp"), None, None)
    weights = (
        row, P(None, "fsdp"), row, row, vector, vector, row, vector, row, vector, vector, vector,
    )
    ways = mesh.shape["fsdp"]
    fits = ways == 8 and mesh.shape["dp"] == 4

    def program(pixels, *rest):
        return (body if fits and pixels.shape[0] == 1 else plain_body)(ways, pixels, *rest)

    return jax.shard_map(
        program,
        mesh=mesh,
        in_specs=(P(("fsdp", "dp"), None), *weights, shared),
        out_specs=(shared, *weights),
        check_vma=False,
    )
```

```python
import functools

import jax
import jax.numpy as jnp
import numpy as np
from jax import lax
from jax.experimental import pallas as pl
from jax.experimental.pallas import tpu as pltpu
from jax.sharding import PartitionSpec as P

D = 512
HEADS = 8
HEAD_DIM = 64
FF = 2048
LEVELS = 256
CHANNELS = 3
SEQ = 3072
BLOCK = 768
BANDS = SEQ // BLOCK
PAIRS = HEADS // 2
PAIR = 2 * HEAD_DIM
REACH = 2
SUB = 256
EXTRA = 16
EPS = 1e-6
LOG2E = 1.4426950408889634
SAFE = 60.0

f32 = jnp.float32
bf16 = jnp.bfloat16
NT = (((1,), (1,)), ((), ()))
TN = (((0,), (0,)), ((), ()))
VMEM_LIMIT = 60 * 2**20


def mm(a, b):
    return jnp.dot(a, b, preferred_element_type=f32)


def mm_nt(a, b):
    return lax.dot_general(a, b, NT, preferred_element_type=f32)


def mm_tn(a, b):
    return lax.dot_general(a, b, TN, preferred_element_type=f32)


def params(*semantics):
    return pltpu.CompilerParams(
        vmem_limit_bytes=VMEM_LIMIT, dimension_semantics=semantics or None
    )


def one_hot_rows(pix):
    width = pix.shape[1]
    return (lax.broadcasted_iota(jnp.int32, (LEVELS, width), 0) == pix).astype(bf16)


def split3(x):
    hi = x.astype(bf16).astype(f32)
    rest = x - hi
    mid = rest.astype(bf16).astype(f32)
    return hi, mid, rest - mid


class Place:
    def __init__(self, ways):
        self.n = ways
        self.f = lax.axis_index("fsdp")
        self.d = lax.axis_index("dp")
        self.core = self.d % 2
        self.side = self.d // 2
        self.quarter = self.core * 2 + self.side

    def at(self, step):
        return (self.f + step) % self.n

    def to(self, step):
        return {"fsdp": self.at(step), "dp": self.d}

    def to_core(self):
        return {"fsdp": self.f, "dp": self.d + 1 - 2 * self.core}

    def to_side(self):
        return {"fsdp": self.f, "dp": self.d + 2 - 4 * self.side}

    def to_cross(self):
        return {"fsdp": self.f, "dp": 3 - self.d}

    def mates(self):
        return [self.to_core(), self.to_side(), self.to_cross()] + [self.to(step) for step in range(1, self.n)]

    def hello(self):
        barrier = pltpu.get_barrier_semaphore()
        for mate in self.mates():
            pl.semaphore_signal(barrier, inc=1, device_id=mate, device_id_type=pl.DeviceIdType.MESH)

    def greeted(self):
        pl.semaphore_wait(pltpu.get_barrier_semaphore(), self.n + 2)


def send(src, dst, sems, i, device):
    return pltpu.make_async_remote_copy(
        src_ref=src,
        dst_ref=dst,
        send_sem=sems.at[0, i],
        recv_sem=sems.at[1, i],
        device_id=device,
        device_id_type=pl.DeviceIdType.MESH,
    )


def window(which, size, count=1):
    return pl.ds(pl.multiple_of(which * size, size), size * count)


class Gather:
    def __init__(self, place, src, dst, sems, across):
        self.place, self.src, self.dst, self.sems = place, src, dst, sems
        self.across, self.n = across, place.n

    @staticmethod
    def semaphores(ways):
        return pltpu.SemaphoreType.DMA((2, 3 * ways + 1))

    def part(self, ref, f, start, count):
        if self.across is None:
            return ref.at[f]
        cut = window(start, self.dst.shape[1 + self.across] // 4, count)
        return ref.at[f, cut] if self.across == 0 else ref.at[f, :, cut]

    def mine(self):
        return self.part(self.dst, self.place.f, self.place.quarter, 1)

    def source(self):
        return self.part(self.src, 0, self.place.quarter, 1)

    def local(self):
        return pltpu.make_async_copy(self.source(), self.mine(), self.sems.at[0, 3 * self.n])

    def copy(self, step):
        return send(self.source(), self.mine(), self.sems, step, self.place.to(step))

    def side_copy(self, step):
        got = self.part(self.dst, self.place.at(self.n - step), self.place.quarter, 1)
        return send(got, got, self.sems, self.n + step, self.place.to_side())

    def core_copy(self, step):
        got = self.part(self.dst, self.place.at(self.n - step), self.place.core * 2, 2)
        return send(got, got, self.sems, 2 * self.n + step, self.place.to_core())

    def start(self):
        self.local().start()
        for step in range(1, self.n):
            self.copy(step).start()

    def swap(self, step):
        if step:
            self.copy(step).wait()
        else:
            self.local().wait()
        if self.across is not None:
            self.side_copy(step).start()

    def share(self, step):
        if self.across is not None:
            self.side_copy(step).wait()
            self.core_copy(step).start()

    def finish(self):
        if self.across is not None:
            for step in range(self.n):
                self.core_copy(step).wait()


class Reduce:
    def __init__(self, place, src, out, bufs):
        self.place, self.src, self.out, self.n = place, src, out, place.n
        self.r1, self.a1, self.r2, self.r3, self.sems = bufs
        self.size = src.shape[1] // 4

    @staticmethod
    def scratch(ways, rows, cols):
        return [
            pltpu.VMEM((ways, rows // 2, cols), bf16),
            pltpu.VMEM((ways, rows // 2, cols), bf16),
            pltpu.VMEM((ways, rows // 4, cols), bf16),
            pltpu.VMEM((ways - 1, rows // 4, cols), bf16),
            pltpu.SemaphoreType.DMA((2, ways + 5)),
        ]

    def half(self, which):
        return self.src.at[:, window(which, 2 * self.size)]

    def local(self):
        return pltpu.make_async_copy(self.half(self.place.core), self.a1, self.sems.at[0, self.n + 4])

    def core_copy(self):
        return send(self.half(1 - self.place.core), self.r1, self.sems, 0, self.place.to_core())

    def side_copy(self):
        theirs = self.a1.at[:, window(1 - self.place.side, self.size)]
        return send(theirs, self.r2, self.sems, self.n, self.place.to_side())

    def copy(self, step):
        return send(self.r2.at[self.place.at(step)], self.r3.at[step - 1], self.sems, step, self.place.to(step))

    def backs(self):
        got = self.out.at[window(self.place.quarter, self.size)]
        mates = (self.place.to_core(), self.place.to_side(), self.place.to_cross())
        return [send(got, got, self.sems, self.n + 1 + i, mate) for i, mate in enumerate(mates)]

    def start(self):
        self.core_copy().start()
        self.local().start()

    def over_sides(self):
        self.local().wait()
        self.core_copy().wait()

        @pl.loop(0, self.n)
        def _(i):
            self.a1[i] = (self.a1[i].astype(f32) + self.r1[i].astype(f32)).astype(bf16)

        self.side_copy().start()

    def over_shards(self):
        self.side_copy().wait()
        cut = window(self.place.side, self.size)

        @pl.loop(0, self.n)
        def _(i):
            self.r2[i] = (self.a1[i, cut].astype(f32) + self.r2[i].astype(f32)).astype(bf16)

        for step in range(1, self.n):
            self.copy(step).start()

    def settle(self):
        for step in range(1, self.n):
            self.copy(step).wait()
        whole = self.r2[self.place.f].astype(f32)
        for step in range(1, self.n):
            whole = whole + self.r3[step - 1].astype(f32)
        self.out[window(self.place.quarter, self.size)] = whole
        for back in self.backs():
            back.start()

    def finish(self):
        for back in self.backs():
            back.wait()

    stages = (start, over_sides, over_shards, settle, finish)


class ReduceSmall:
    def __init__(self, place, src, out, bufs):
        self.place, self.src, self.out, self.n = place, src, out, place.n
        self.r1, self.r2, self.r3, self.sems = bufs

    @staticmethod
    def scratch(ways, rows, cols):
        return [
            pltpu.VMEM((ways, rows, cols), f32),
            pltpu.VMEM((ways, rows, cols), f32),
            pltpu.VMEM((ways - 1, rows, cols), f32),
            pltpu.SemaphoreType.DMA((2, ways + 1)),
        ]

    def core_copy(self):
        return send(self.src, self.r1, self.sems, 0, self.place.to_core())

    def side_copy(self):
        return send(self.src, self.r2, self.sems, self.n, self.place.to_side())

    def copy(self, step):
        return send(self.src.at[self.place.at(step)], self.r3.at[step - 1], self.sems, step, self.place.to(step))

    def start(self):
        self.core_copy().start()

    def over_sides(self):
        self.core_copy().wait()
        self.src[...] += self.r1[...]
        self.side_copy().start()

    def over_shards(self):
        self.side_copy().wait()
        self.src[...] += self.r2[...]
        for step in range(1, self.n):
            self.copy(step).start()

    def settle(self):
        for step in range(1, self.n):
            self.copy(step).wait()
        whole = self.src[self.place.f]
        for step in range(1, self.n):
            whole = whole + self.r3[step - 1]
        self.out[...] = whole

    def finish(self):
        pass

    stages = (start, over_sides, over_shards, settle, finish)


def embed_tile(step, pix_ref, chan_ref, level, table, w, ind_ref, emb_ref, low_ref, qkv_ref, qt_ref, vt_ref, norm_ref):
    emb = mm_tn(one_hot_rows(pix_ref[...]), level) + mm_tn(chan_ref[...], table)
    emb_ref[...] = emb
    low = emb.astype(bf16)
    low_ref[...] = low
    qkv = mm(low, w)
    q = (qkv[:, :D] * HEAD_DIM**-0.5).astype(bf16)
    k = qkv[:, D : 2 * D].astype(bf16)
    v = qkv[:, 2 * D :].astype(bf16)
    qkv_ref[:, :D] = q
    qkv_ref[:, D : 2 * D] = k
    qkv_ref[:, 2 * D :] = v
    qt_ref[...] = q.T
    vt_ref[...] = v.T
    q = q.astype(f32)
    k = k.astype(f32)
    size_q = mm((q * q).astype(bf16), ind_ref[...]).max(0, keepdims=True)
    size_k = mm((k * k).astype(bf16), ind_ref[...]).max(0, keepdims=True)
    row = lax.broadcasted_iota(jnp.int32, (8, 128), 0)
    both = jnp.where(row == 0, size_q, jnp.where(row == 1, size_k, 0.0))
    norm_ref[...] = jnp.maximum(both, jnp.where(step == 0, 0.0, norm_ref[...]))


def embed_plain_kernel(pix_ref, chan_ref, level_ref, table_ref, w_ref, ind_ref, *outs):
    embed_tile(pl.program_id(0), pix_ref, chan_ref, level_ref[...], table_ref[...], w_ref[...], ind_ref, *outs)


def embed_outs():
    rows = lambda i: (i, 0)
    cols = lambda i: (0, i)
    specs = [
        pl.BlockSpec((BLOCK, D), rows),
        pl.BlockSpec((BLOCK, D), rows),
        pl.BlockSpec((BLOCK, 3 * D), rows),
        pl.BlockSpec((D, BLOCK), cols),
        pl.BlockSpec((D, BLOCK), cols),
        pl.BlockSpec((8, 128), lambda i: (0, 0)),
    ]
    shapes = [
        jax.ShapeDtypeStruct((SEQ, D), f32),
        jax.ShapeDtypeStruct((SEQ, D), bf16),
        jax.ShapeDtypeStruct((SEQ, 3 * D), bf16),
        jax.ShapeDtypeStruct((D, SEQ), bf16),
        jax.ShapeDtypeStruct((D, SEQ), bf16),
        jax.ShapeDtypeStruct((8, 128), f32),
    ]
    return specs, shapes


def head_columns():
    return (np.arange(D)[:, None] // HEAD_DIM == np.arange(128)[None, :]).astype(bf16)


def embed_plain(pix, chan, level, table, w_in):
    whole = lambda i: (0, 0)
    specs, shapes = embed_outs()
    return pl.pallas_call(
        embed_plain_kernel,
        grid=(SEQ // BLOCK,),
        in_specs=[
            pl.BlockSpec((1, BLOCK), lambda i: (0, i)),
            pl.BlockSpec((EXTRA, BLOCK), whole),
            pl.BlockSpec((LEVELS, D), whole),
            pl.BlockSpec((EXTRA, D), whole),
            pl.BlockSpec((D, 3 * D), whole),
            pl.BlockSpec((D, 128), whole),
        ],
        out_specs=specs,
        out_shape=shapes,
        compiler_params=params("arbitrary"),
    )(pix, chan, level, table, w_in, head_columns())


def half_lanes(even, odd):
    lane = lax.broadcasted_iota(jnp.int32, even.shape, 1)
    return jnp.where(lane < HEAD_DIM, even, pltpu.roll(odd, HEAD_DIM, 1))


def embed_gather_kernel(
    ways, pix_ref, chan_ref, ind_ref, level_ref, small_ref, win_ref, wo_ref,
    emb_ref, low_ref, qkv_ref, qt_ref, vt_ref, norm_ref, vec_ref, be_ref, w4_ref, wo_out,
    level_s, small_s, win_s, sem_level, sem_small, sem_in, sem_o, sem_w4,
):
    step = pl.program_id(0)
    last = SEQ // BLOCK - 1
    place = Place(ways)
    first = [
        Gather(place, small_ref, small_s, sem_small, None),
        Gather(place, level_ref, level_s, sem_level, 1),
        Gather(place, win_ref, win_s, sem_in, 0),
    ]
    later = Gather(place, wo_ref, wo_out, sem_o, 0)

    def copies():
        for i in range(3 * PAIRS):
            yield pltpu.make_async_copy(win_s.at[:, :, i * PAIR : (i + 1) * PAIR], w4_ref.at[i], sem_w4.at[i])

    @pl.when(step == 0)
    def _():
        place.hello()
        place.greeted()
        for g in (*first, later):
            g.start()
        for i in range(ways):
            for g in first:
                g.swap(i)
        for i in range(ways):
            for g in first:
                g.share(i)
        for i in range(ways // 2):
            both = [small_s[2 * i + odd].astype(f32) for odd in range(2)]
            vec_ref[:, i * 128 : (i + 1) * 128] = half_lanes(*both)
            for odd in range(2):
                for j in range(2):
                    at = ((2 * i + odd) * 2 + j) * 128
                    be_ref[0:1, at : at + 128] = both[odd][8 + j : 9 + j]
        for g in first:
            g.finish()
        for copy in copies():
            copy.start()

    table = vec_ref[...].astype(bf16)
    level = level_s[...].reshape(LEVELS, D)
    w = win_s[...].reshape(D, 3 * D)
    embed_tile(step, pix_ref, chan_ref, level, table, w, ind_ref, emb_ref, low_ref, qkv_ref, qt_ref, vt_ref, norm_ref)

    @pl.when(step == 0)
    def _():
        for i in range(ways):
            later.swap(i)

    @pl.when(step == last - 1)
    def _():
        for i in range(ways):
            later.share(i)

    @pl.when(step == last)
    def _():
        for copy in copies():
            copy.wait()
        later.finish()


def embed_gather(ways, pix, chan, level, small, w_in, wo):
    whole = lambda i: (0, 0)
    anywhere = pl.BlockSpec(memory_space=pl.ANY)
    specs, shapes = embed_outs()
    shards = [x[None] for x in (level, small, w_in, wo)]
    return pl.pallas_call(
        functools.partial(embed_gather_kernel, ways),
        grid=(SEQ // BLOCK,),
        in_specs=[
            pl.BlockSpec((1, BLOCK), lambda i: (0, i)),
            pl.BlockSpec((EXTRA, BLOCK), whole),
            pl.BlockSpec((D, 128), whole),
            *[anywhere] * 4,
        ],
        out_specs=[*specs, pl.BlockSpec((EXTRA, D), whole), pl.BlockSpec((8, FF), whole), *[anywhere] * 2],
        out_shape=[
            *shapes,
            jax.ShapeDtypeStruct((EXTRA, D), f32),
            jax.ShapeDtypeStruct((8, FF), f32),
            jax.ShapeDtypeStruct((3 * PAIRS, ways, D // ways, PAIR), bf16),
            jax.ShapeDtypeStruct((ways, *wo.shape), bf16),
        ],
        scratch_shapes=[
            *[pltpu.VMEM((ways, *x.shape), bf16) for x in (level, small, w_in)],
            *[Gather.semaphores(ways)] * 4,
            pltpu.SemaphoreType.DMA((3 * PAIRS,)),
        ],
        compiler_params=pltpu.CompilerParams(
            vmem_limit_bytes=VMEM_LIMIT, dimension_semantics=("arbitrary",), collective_id=0, has_side_effects=True
        ),
    )(pix, chan, head_columns(), *shards)


def units():
    found = []
    for band in range(BANDS):
        found += [(band, j) for j in range(max(0, band - REACH), band + 1)]
    return found


def lower_mask(keys, queries):
    key = lax.broadcasted_iota(jnp.int32, (keys, queries), 0)
    return key <= lax.broadcasted_iota(jnp.int32, (keys, queries), 1)


def spare_rows(x):
    row = lax.broadcasted_iota(jnp.int32, (HEAD_DIM, x.shape[1]), 0)
    hi, mid, low = split3(x)
    return jnp.where(row == 0, hi, jnp.where(row == 1, mid, jnp.where(row == 2, low, 0.0)))


class Fetch:
    def __init__(self, ways, sources, outs, sems):
        self.place = Place(ways)
        self.wide, self.narrow = [Gather(self.place, s, o, m, 0) for s, o, m in zip(sources, outs, sems)]

    def point(self, pair, name):
        every = range(self.place.n)
        half = self.place.n // 2
        plan = {
            (0, 0): [self.place.hello],
            (0, 3): [self.place.greeted, self.wide.start],
            (0, 8): [self.narrow.start],
            (1, 5): [functools.partial(self.wide.swap, i) for i in every],
            (2, 5): [functools.partial(self.narrow.swap, i) for i in every[:half]],
            (2, 8): [functools.partial(self.narrow.swap, i) for i in every[half:]],
            (3, 3): [functools.partial(self.wide.share, i) for i in every],
            (3, 9): [functools.partial(self.narrow.share, i) for i in every] + [self.wide.finish, self.narrow.finish],
        }
        for (when, where), steps in plan.items():
            if where == name:

                @pl.when(pair == when)
                def _():
                    for step in steps:
                        step()


def attend_kernel(ways, linked, *refs):
    q_ref, k_ref, vt_ref, *refs = refs
    sources, refs = (refs[:2], refs[2:]) if linked else (None, refs)
    o_ref, qe_ref, *refs = refs
    outs, refs = (refs[:2], refs[2:]) if linked else (None, refs)
    acc, lsum, probs, *sems = refs
    pair = pl.program_id(0)
    fetch = Fetch(ways, sources, outs, sems) if linked else None
    lane = lax.broadcasted_iota(jnp.int32, (BLOCK, PAIR), 1)

    def head_only(q, h, other):
        mine = (lane < HEAD_DIM) if h == 0 else (lane >= HEAD_DIM)
        return jnp.where(mine, q, other)

    for unit, (band, j) in enumerate(units()):
        if linked:
            fetch.point(pair, unit)
        here = slice(band * BLOCK, (band + 1) * BLOCK)
        first = j == max(0, band - REACH)
        q = q_ref[here, :]
        off = jnp.zeros_like(q)
        tiles = [(0, BLOCK, BLOCK)] if j < band else [(t * SUB, SUB, (t + 1) * SUB) for t in range(BLOCK // SUB)]
        for h in range(2):
            qm = head_only(q, h, off)
            for at, width, count in tiles:
                ts = slice(at, at + width)
                scores = mm_nt(k_ref[j * BLOCK : j * BLOCK + count, :], qm[ts])
                p = jnp.exp2(scores * LOG2E)
                if j == band:
                    diag = jnp.where(lower_mask(SUB, SUB), p[count - SUB :], 0.0)
                    p = diag if count == SUB else jnp.concatenate([p[: count - SUB], diag], 0)
                part = p.reshape(count // 8, 8, width).sum(0)
                if not first:
                    part += lsum[h, :, ts]
                lsum[h, :, ts] = part
                probs[h, :count, ts] = p.astype(bf16)
        ext = [None, None]
        for h in range(2):
            mine = slice(h * HEAD_DIM, (h + 1) * HEAD_DIM)
            for at, width, count in tiles:
                ts = slice(at, at + width)
                out = mm(vt_ref[mine, j * BLOCK : j * BLOCK + count], probs[h, :count, ts])
                if not first:
                    out += acc[mine, ts]
                acc[mine, ts] = out
            if j == band:
                whole = lsum[h].sum(0, keepdims=True)
                acc[mine, :] = acc[mine, :] / whole
                ext[1 - h] = spare_rows(-jnp.log(whole))
        if j == band:
            o_ref[here, :] = acc[...].T.astype(bf16)
            extra = jnp.concatenate(ext, 0).T.astype(bf16)
            qe_ref[here, :PAIR] = head_only(q, 0, extra)
            qe_ref[here, PAIR:] = head_only(q, 1, extra)
    if linked:
        fetch.point(pair, len(units()))


def attend(ways, qkv, vt, shards=None):
    linked = shards is not None
    anywhere = pl.BlockSpec(memory_space=pl.ANY)
    extra, outs, sems, compiler = [], [], [], params("arbitrary")
    if linked:
        extra = [x[None] for x in shards]
        outs = [jax.ShapeDtypeStruct((ways, *x.shape), bf16) for x in shards]
        sems = [Gather.semaphores(ways)] * 2
        compiler = pltpu.CompilerParams(
            vmem_limit_bytes=VMEM_LIMIT, dimension_semantics=("arbitrary",), collective_id=2, has_side_effects=True
        )
    return pl.pallas_call(
        functools.partial(attend_kernel, ways, linked),
        grid=(PAIRS,),
        in_specs=[
            pl.BlockSpec((SEQ, PAIR), lambda p: (0, p)),
            pl.BlockSpec((SEQ, PAIR), lambda p: (0, PAIRS + p)),
            pl.BlockSpec((PAIR, SEQ), lambda p: (p, 0)),
            *[anywhere] * len(extra),
        ],
        out_specs=[
            pl.BlockSpec((SEQ, PAIR), lambda p: (0, p)),
            pl.BlockSpec((SEQ, 2 * PAIR), lambda p: (0, p)),
            *[anywhere] * len(extra),
        ],
        out_shape=[
            jax.ShapeDtypeStruct((SEQ, D), bf16),
            jax.ShapeDtypeStruct((SEQ, 2 * D), bf16),
            *outs,
        ],
        scratch_shapes=[
            pltpu.VMEM((PAIR, BLOCK), f32),
            pltpu.VMEM((2, 8, BLOCK), f32),
            pltpu.VMEM((2, BLOCK, BLOCK), bf16),
            *sems,
        ],
        compiler_params=compiler,
    )(qkv, qkv, vt, *extra)


def repair_kernel(
    norm_ref, qkv_ref, vt_ref, _att, _qe, att_ref, qe_ref, q_s, k_s, vt_s, o_s, e_s, acc, top, lsum, sems
):
    bound = jnp.max(norm_ref[0:1] * norm_ref[1:2])

    @pl.when(jnp.logical_not(bound < SAFE * SAFE))
    def _():
        lane = lax.broadcasted_iota(jnp.int32, (BLOCK, PAIR), 1)
        chunk = 128

        @pl.loop(0, PAIRS)
        def _(pair):
            at = pl.multiple_of(pair * PAIR, PAIR)
            loads = [
                pltpu.make_async_copy(qkv_ref.at[:, pl.ds(at, PAIR)], q_s, sems.at[0]),
                pltpu.make_async_copy(qkv_ref.at[:, pl.ds(pl.multiple_of(at + D, PAIR), PAIR)], k_s, sems.at[1]),
                pltpu.make_async_copy(vt_ref.at[pl.ds(at, PAIR)], vt_s, sems.at[2]),
            ]
            for load in loads:
                load.start()
            for load in loads:
                load.wait()

            @pl.loop(0, BANDS)
            def _(band):
                here = pl.ds(pl.multiple_of(band * BLOCK, BLOCK), BLOCK)
                q = q_s[here, :]
                ext = [None, None]
                begin = jnp.maximum(band - REACH, 0) * (BLOCK // chunk)
                end = (band + 1) * (BLOCK // chunk)
                for h in range(2):
                    mine = slice(h * HEAD_DIM, (h + 1) * HEAD_DIM)
                    qm = jnp.where((lane < HEAD_DIM) if h == 0 else (lane >= HEAD_DIM), q, jnp.zeros_like(q))

                    def masked(i):
                        start = pl.multiple_of(i * chunk, chunk)
                        scores = mm_nt(k_s[pl.ds(start, chunk), :], qm)
                        key = lax.broadcasted_iota(jnp.int32, scores.shape, 0) + start
                        query = lax.broadcasted_iota(jnp.int32, scores.shape, 1) + band * BLOCK
                        return start, jnp.where(key <= query, scores, -1e30)

                    top[...] = jnp.full(top.shape, -1e30, f32)
                    lsum[...] = jnp.zeros_like(lsum)
                    acc[mine] = jnp.zeros((HEAD_DIM, BLOCK), f32)

                    @pl.loop(begin, end)
                    def _(i):
                        top[...] = jnp.maximum(top[...], masked(i)[1].max(0, keepdims=True))

                    @pl.loop(begin, end)
                    def _(i):
                        start, scores = masked(i)
                        p = jnp.exp2((scores - top[0:1]) * LOG2E)
                        lsum[...] += p.reshape(chunk // 8, 8, BLOCK).sum(0)
                        acc[mine] += mm(vt_s[mine, pl.ds(start, chunk)], p.astype(bf16))

                    whole = lsum[...].sum(0, keepdims=True)
                    acc[mine] = acc[mine] / whole
                    ext[1 - h] = spare_rows(-(top[0:1] + jnp.log(whole)))
                o_s[here, :] = acc[...].T.astype(bf16)
                extra = jnp.concatenate(ext, 0).T.astype(bf16)
                e_s[here, :PAIR] = jnp.where(lane < HEAD_DIM, q, extra)
                e_s[here, PAIR:] = jnp.where(lane < HEAD_DIM, extra, q)

            stores = [
                pltpu.make_async_copy(o_s, att_ref.at[:, pl.ds(at, PAIR)], sems.at[0]),
                pltpu.make_async_copy(
                    e_s, qe_ref.at[:, pl.ds(pl.multiple_of(2 * at, 2 * PAIR), 2 * PAIR)], sems.at[1]
                ),
            ]
            for store in stores:
                store.start()
            for store in stores:
                store.wait()


def repair(sizes, qkv, vt, att, qe):
    anywhere = pl.BlockSpec(memory_space=pl.ANY)
    return pl.pallas_call(
        repair_kernel,
        in_specs=[pl.BlockSpec(memory_space=pltpu.VMEM), *[anywhere] * 4],
        out_specs=[anywhere] * 2,
        out_shape=[jax.ShapeDtypeStruct(x.shape, x.dtype) for x in (att, qe)],
        scratch_shapes=[
            pltpu.VMEM((SEQ, PAIR), bf16),
            pltpu.VMEM((SEQ, PAIR), bf16),
            pltpu.VMEM((PAIR, SEQ), bf16),
            pltpu.VMEM((SEQ, PAIR), bf16),
            pltpu.VMEM((SEQ, 2 * PAIR), bf16),
            pltpu.VMEM((PAIR, BLOCK), f32),
            pltpu.VMEM((8, BLOCK), f32),
            pltpu.VMEM((8, BLOCK), f32),
            pltpu.SemaphoreType.DMA((3,)),
        ],
        input_output_aliases={3: 0, 4: 1},
        compiler_params=params(),
    )(sizes, qkv, vt, att, qe)


def mean(x):
    return jnp.mean(x, -1, keepdims=True)


def norm(x):
    centered = x - mean(x)
    factor = lax.rsqrt(mean(centered * centered) + EPS)
    return centered * factor, factor


def norm_back(scaled, normed, factor):
    return factor * (scaled - mean(scaled) - normed * mean(scaled * normed))


def total(x):
    return x.sum(0, keepdims=True)


def middle_kernel(
    att_ref, emb_ref, cot_ref, wo_ref, we_ref, ws_ref, vec_ref, be_ref, pick_ref,
    out_ref, go_ref, de_ref, dt_ref, gwo_out, gwe_out, gws_out, gvec_ref, gbe_ref, gwo_ref, gwe_ref, gws_ref,
):
    @pl.when(pl.program_id(0) == 0)
    def _():
        for ref in (gwo_ref, gwe_ref, gws_ref, gvec_ref, gbe_ref):
            ref[...] = jnp.zeros_like(ref)

    gain1, bias1, bs, gain2, bias2 = [vec_ref[i : i + 1, :] for i in range(5)]
    att = att_ref[...]
    cot = cot_ref[...]
    normed1, factor1 = norm(emb_ref[...] + mm(att, wo_ref[...]))
    hidden = normed1 * gain1 + bias1
    low = hidden.astype(bf16)
    preact = mm(low, we_ref[...]) + be_ref[0:1, :]
    sig = jax.nn.sigmoid(preact)
    activ = (preact * sig).astype(bf16)
    slope = sig * (1.0 + preact * (1.0 - sig))
    normed2, factor2 = norm(hidden + mm(activ, ws_ref[...]) + bs)
    out_ref[...] = (normed2 * gain2 + bias2).astype(bf16)
    gtwo = norm_back(cot * gain2, normed2, factor2)
    gbranch = gtwo.astype(bf16)
    gws_ref[...] += mm_tn(activ, gbranch)
    gpre = (mm_nt(gbranch, ws_ref[...]) * slope).astype(bf16)
    gbe_ref[0:1, :] += total(gpre.astype(f32))
    gwe_ref[...] += mm_tn(low, gpre)
    ghidden = gtwo + mm_nt(gpre, we_ref[...])
    gone = norm_back(ghidden * gain1, normed1, factor1)
    go_ref[...] = gone
    gatt_branch = gone.astype(bf16)
    gwo_ref[...] += mm_tn(att, gatt_branch)
    gatt = mm_nt(gatt_branch, wo_ref[...]).astype(bf16)
    dt_ref[...] = gatt.T
    gvec_ref[0:1, :] += total(ghidden * normed1)
    gvec_ref[1:2, :] += total(ghidden)
    gvec_ref[2:3, :] += total(gbranch.astype(f32))
    gvec_ref[3:4, :] += total(cot * normed2)
    gvec_ref[4:5, :] += total(cot)

    @pl.when(pl.program_id(0) == pl.num_programs(0) - 1)
    def _():
        gwo_out[...] = gwo_ref[...].astype(bf16)
        gwe_out[...] = gwe_ref[...].astype(bf16)
        gws_out[...] = gws_ref[...].astype(bf16)

    prod = gatt.astype(f32) * att.astype(f32)
    hi, mid, _ = split3(prod)
    pick = pick_ref[...]
    half = D // 2
    place = lax.broadcasted_iota(jnp.int32, (att.shape[0], half), 1) % HEAD_DIM
    lane = lax.broadcasted_iota(jnp.int32, (att.shape[0], PAIR), 1)
    for part in range(2):
        cols = slice(part * half, (part + 1) * half)
        inner = mm(hi[:, cols].astype(bf16), pick) + mm(mid[:, cols].astype(bf16), pick)
        a, b, c = split3(inner)
        ext = jnp.where(place == 0, a, jnp.where(place == 1, b, jnp.where(place == 2, c, 0.0))).astype(bf16)
        for i in range(2):
            pair = 2 * part + i
            e = ext[:, i * PAIR : (i + 1) * PAIR]
            d = gatt[:, pair * PAIR : (pair + 1) * PAIR]
            de_ref[:, 2 * pair * PAIR : (2 * pair + 1) * PAIR] = jnp.where(lane < HEAD_DIM, d, e)
            de_ref[:, (2 * pair + 1) * PAIR : (2 * pair + 2) * PAIR] = jnp.where(lane < HEAD_DIM, e, d)


def middle(att, emb, cot, wo, we, ws, vec, be):
    tile = 512
    half = D // 2
    src = np.arange(half)[:, None] // HEAD_DIM
    dst = np.arange(half)[None, :]
    other = (dst // HEAD_DIM) ^ 1
    pick = np.where((src == other) & (dst % HEAD_DIM < 3), -1.0, 0.0).astype(bf16)
    whole = lambda i: (0, 0)
    rows = lambda i: (i, 0)
    cols = lambda i: (0, i)
    one = pl.Buffered(1)
    return pl.pallas_call(
        middle_kernel,
        grid=(SEQ // tile,),
        in_specs=[
            pl.BlockSpec((tile, D), rows),
            pl.BlockSpec((tile, D), rows),
            pl.BlockSpec((tile, D), rows),
            pl.BlockSpec((D, D), whole, pipeline_mode=one),
            pl.BlockSpec((D, FF), whole, pipeline_mode=one),
            pl.BlockSpec((FF, D), whole, pipeline_mode=one),
            pl.BlockSpec((EXTRA, D), whole),
            pl.BlockSpec((8, FF), whole),
            pl.BlockSpec((half, half), whole),
        ],
        out_specs=[
            pl.BlockSpec((tile, D), rows),
            pl.BlockSpec((tile, D), rows),
            pl.BlockSpec((tile, 2 * D), rows),
            pl.BlockSpec((D, tile), cols),
            pl.BlockSpec((D, D), whole, pipeline_mode=one),
            pl.BlockSpec((D, FF), whole, pipeline_mode=one),
            pl.BlockSpec((FF, D), whole, pipeline_mode=one),
            pl.BlockSpec((8, D), whole),
            pl.BlockSpec((8, FF), whole),
        ],
        out_shape=[
            jax.ShapeDtypeStruct((SEQ, D), bf16),
            jax.ShapeDtypeStruct((SEQ, D), f32),
            jax.ShapeDtypeStruct((SEQ, 2 * D), bf16),
            jax.ShapeDtypeStruct((D, SEQ), bf16),
            jax.ShapeDtypeStruct((D, D), bf16),
            jax.ShapeDtypeStruct((D, FF), bf16),
            jax.ShapeDtypeStruct((FF, D), bf16),
            jax.ShapeDtypeStruct((8, D), f32),
            jax.ShapeDtypeStruct((8, FF), f32),
        ],
        scratch_shapes=[pltpu.VMEM((D, D), f32), pltpu.VMEM((D, FF), f32), pltpu.VMEM((FF, D), f32)],
        compiler_params=params("arbitrary"),
    )(att, emb, cot, wo, we, ws, vec, be, pick)


def back_kernel(ways, linked, *refs):
    refs = list(refs)
    take = lambda count: [refs.pop(0) for _ in range(count)]
    qe_ref, k_ref, v_ref, de_ref, qt_ref, dt_ref, low_ref, w_ref, pix_ref, chan_ref, go_ref = take(11)
    given = take(5) if linked else None
    outs = take(6 if linked else 3)
    ke, ve, km, probs, slopes, dkt, dvt, dqa, grads, gemb, sem = take(11)
    pair = pl.program_id(0)
    copy = pltpu.make_async_copy(go_ref, gemb, sem)
    sums = Sums(ways, given, outs, refs) if linked else None

    def point(name):
        if linked:
            sums.point(pair, name)

    @pl.when(pair == 0)
    def _():
        copy.start()

    point("begin")
    lane = lax.broadcasted_iota(jnp.int32, (BLOCK, PAIR), 1)
    for band in range(BANDS):
        here = slice(band * BLOCK, (band + 1) * BLOCK)
        k = k_ref[here, :]
        v = v_ref[here, :]
        one = jnp.ones_like(k)
        zero = jnp.zeros_like(k)
        right = jnp.where(lane < HEAD_DIM + 3, one, zero)
        left = jnp.where(lane < 3, one, zero)
        ke[0, here] = jnp.where(lane < HEAD_DIM, k, right)
        ke[1, here] = jnp.where(lane < HEAD_DIM, left, k)
        ve[0, here] = jnp.where(lane < HEAD_DIM, v, right)
        ve[1, here] = jnp.where(lane < HEAD_DIM, left, v)
        km[0, here] = jnp.where(lane < HEAD_DIM, k, zero)
        km[1, here] = jnp.where(lane < HEAD_DIM, zero, k)
    for unit, (band, j) in enumerate(units()):
        point(unit)
        t0 = band * BLOCK
        k0 = j * BLOCK
        first = j == max(0, band - REACH)
        tiles = [(0, BLOCK)] if j < band else [(i * SUB, SUB) for i in range(BLOCK // SUB)]
        for h in range(2):
            mine = slice(h * HEAD_DIM, (h + 1) * HEAD_DIM)
            lanes = slice(h * PAIR, (h + 1) * PAIR)
            for at, count in tiles:
                ts = slice(t0 + at, t0 + BLOCK)
                ks = slice(k0 + at, k0 + at + count)
                scores = mm_nt(qe_ref[ts, lanes], ke[h, ks])
                p = jnp.exp2(scores * LOG2E)
                if j == band:
                    t = lax.broadcasted_iota(jnp.int32, p.shape, 0)
                    p = jnp.where(lax.broadcasted_iota(jnp.int32, p.shape, 1) <= t, p, 0.0)
                dp = mm_nt(de_ref[ts, lanes], ve[h, ks])
                cols = slice(at, at + count)
                probs[h, at:, cols] = p.astype(bf16)
                slopes[h, at:, cols] = (p * dp).astype(bf16)
                dv = mm(dt_ref[mine, ts], probs[h, at:, cols])
                dk = mm(qt_ref[mine, ts], slopes[h, at:, cols])
                if j == band:
                    dvt[mine, ks] = dv
                    dkt[mine, ks] = dk
                else:
                    dvt[mine, ks] += dv
                    dkt[mine, ks] += dk
        if j < band:
            dq = mm(slopes[0], km[0, k0 : k0 + BLOCK]) + mm(slopes[1], km[1, k0 : k0 + BLOCK])
            if first:
                dqa[...] = dq
            else:
                dqa[...] += dq
        else:
            for i in range(BLOCK // SUB):
                count = (i + 1) * SUB
                rows = slice(i * SUB, count)
                dq = mm(slopes[0, rows, :count], km[0, k0 : k0 + count])
                dq += mm(slopes[1, rows, :count], km[1, k0 : k0 + count])
                if not first:
                    dq += dqa[rows]
                grads[t0 + i * SUB : t0 + count, :PAIR] = (dq * HEAD_DIM**-0.5).astype(bf16)
    for band in range(BANDS):
        here = slice(band * BLOCK, (band + 1) * BLOCK)
        grads[here, PAIR : 2 * PAIR] = dkt[:, here].T.astype(bf16)
        grads[here, 2 * PAIR :] = dvt[:, here].T.astype(bf16)

    gw = mm_tn(low_ref[...], grads[...]).astype(bf16)
    if linked:
        sums.take_pair(pair, gw)
        point("ready")
    else:
        outs[0][0] = gw

    @pl.when(pair == 0)
    def _():
        copy.wait()

    w = jnp.concatenate([w_ref[0, 0], w_ref[1, 0], w_ref[2, 0]], 1)
    for band in range(BANDS):
        here = slice(band * BLOCK, (band + 1) * BLOCK)
        gemb[here] += mm_nt(grads[here, :], w)
    point("end")

    @pl.when(pair == PAIRS - 1)
    def _():
        table = None
        for band in range(BANDS):
            here = slice(band * BLOCK, (band + 1) * BLOCK)
            rows = jnp.concatenate([one_hot_rows(pix_ref[:, here]), chan_ref[...]], 0)
            part = mm(rows, gemb[here].astype(bf16))
            table = part if band == 0 else table + part
        count = LEVELS // ways
        for f in range(ways):
            mine = table[f * count : (f + 1) * count].astype(bf16)
            to = sums.lev_src.at[f] if linked else outs[1].at[f]
            to[:count] = mine[:, : D // 2]
            to[count:] = mine[:, D // 2 :]
        if linked:
            sums.last(table[LEVELS : LEVELS + 8])
        else:
            outs[2][...] = table[LEVELS:]


def back(ways, qe, qkv, de, qt, dt, low, w4, pix, chan, gone, given=None):
    one = pl.Buffered(1)
    rows = D // ways
    linked = given is not None
    anywhere = pl.BlockSpec(memory_space=pl.ANY)
    out_specs = [
        pl.BlockSpec((1, D, 3 * PAIR), lambda p: (p, 0, 0)),
        pl.BlockSpec((ways, 2 * LEVELS // ways, D // 2), lambda p: (0, 0, 0)),
        pl.BlockSpec((EXTRA, D), lambda p: (0, 0)),
    ]
    out_shape = [
        jax.ShapeDtypeStruct((PAIRS, D, 3 * PAIR), bf16),
        jax.ShapeDtypeStruct((ways, 2 * LEVELS // ways, D // 2), bf16),
        jax.ShapeDtypeStruct((EXTRA, D), f32),
    ]
    extra, extra_specs, extra_scratch = [], [], []
    compiler = params("arbitrary")
    if linked:
        split = lambda x: x.reshape(ways, x.shape[0] // ways, x.shape[1])
        gwo, gwe, gws, gvec, gbe = given
        extra = [split(gwo), split(gwe), split(gws), gvec, gbe]
        extra_specs = [anywhere] * 3
        extra_specs += [pl.BlockSpec(x.shape, lambda p: (0, 0)) for x in (gvec, gbe)]
        shapes = [(rows, D), (rows, FF), (FF // ways, D), (rows, 3 * D), (LEVELS // ways, D), (EXTRA, 128)]
        out_specs = [pl.BlockSpec(shape, lambda p: (0, 0), pipeline_mode=one) for shape in shapes]
        out_shape = [jax.ShapeDtypeStruct(shape, f32) for shape in shapes]
        extra_scratch = Sums.scratch(ways)
        compiler = pltpu.CompilerParams(
            vmem_limit_bytes=VMEM_LIMIT, dimension_semantics=("arbitrary",), collective_id=1, has_side_effects=True
        )
    return pl.pallas_call(
        functools.partial(back_kernel, ways, linked),
        grid=(PAIRS,),
        in_specs=[
            pl.BlockSpec((SEQ, 2 * PAIR), lambda p: (0, p)),
            pl.BlockSpec((SEQ, PAIR), lambda p: (0, PAIRS + p)),
            pl.BlockSpec((SEQ, PAIR), lambda p: (0, 2 * PAIRS + p)),
            pl.BlockSpec((SEQ, 2 * PAIR), lambda p: (0, p)),
            pl.BlockSpec((PAIR, SEQ), lambda p: (p, 0)),
            pl.BlockSpec((PAIR, SEQ), lambda p: (p, 0)),
            pl.BlockSpec((SEQ, D), lambda p: (0, 0), pipeline_mode=one),
            pl.BlockSpec((3, 1, D, PAIR), lambda p: (0, p, 0, 0)),
            pl.BlockSpec((1, SEQ), lambda p: (0, 0)),
            pl.BlockSpec((EXTRA, BLOCK), lambda p: (0, 0)),
            anywhere,
            *extra_specs,
        ],
        out_specs=out_specs,
        out_shape=out_shape,
        scratch_shapes=[
            pltpu.VMEM((2, SEQ, PAIR), bf16),
            pltpu.VMEM((2, SEQ, PAIR), bf16),
            pltpu.VMEM((2, SEQ, PAIR), bf16),
            pltpu.VMEM((2, BLOCK, BLOCK), bf16),
            pltpu.VMEM((2, BLOCK, BLOCK), bf16),
            pltpu.VMEM((PAIR, SEQ), f32),
            pltpu.VMEM((PAIR, SEQ), f32),
            pltpu.VMEM((BLOCK, PAIR), f32),
            pltpu.VMEM((SEQ, 3 * PAIR), bf16),
            pltpu.VMEM((SEQ, D), f32),
            pltpu.SemaphoreType.DMA,
            *extra_scratch,
        ],
        compiler_params=compiler,
    )(qe, qkv, qkv, de, qt, dt, low, w4, pix, chan, gone, *extra)


class Sums:
    EARLY = ((0, 3), (0, "ready"), (1, "ready"), (2, "ready"), (3, 3))
    NEXT = ((0, "ready"), (1, 3), (1, "ready"), (2, "ready"), (3, "ready"))

    @staticmethod
    def sizes(ways):
        rows = D // ways
        return [(FF // ways, D), (rows, FF), (rows, D)] + [(rows, 3 * PAIR)] * PAIRS + [(2 * LEVELS // ways, D // 2)]

    @staticmethod
    def scratch(ways):
        sizes = Sums.sizes(ways)
        scratch = [pltpu.VMEM(size, f32) for size in sizes]
        scratch += [pltpu.VMEM((PAIRS, ways, *sizes[3]), bf16), pltpu.VMEM((ways, *sizes[-1]), bf16)]
        scratch += [pltpu.VMEM((ways, EXTRA, 128), f32), pltpu.VMEM((EXTRA, 128), f32)]
        for size in sizes:
            scratch += Reduce.scratch(ways, *size)
        return scratch + ReduceSmall.scratch(ways, EXTRA, 128)

    def __init__(self, ways, given, outs, scratch):
        self.ways, self.outs = ways, outs
        self.place = Place(ways)
        wo, we, ws, self.gvec, self.gbe = given
        scratch = list(scratch)
        take = lambda count: [scratch.pop(0) for _ in range(count)]
        self.results = take(4 + PAIRS)
        self.in_src, self.lev_src = take(2)
        self.small_src, self.small_out = take(2)
        sources = [ws, we, wo, *[self.in_src.at[p] for p in range(PAIRS)], self.lev_src]
        chunks = [Reduce(self.place, s, r, take(5)) for s, r in zip(sources, self.results)]
        self.early, self.pairs, self.lev = chunks[:3], chunks[3:-1], chunks[-1]
        self.small = ReduceSmall(self.place, self.small_src, self.small_out, take(4))

    def point(self, pair, name):
        @pl.when(pair == 0)
        def _():
            if name == "begin":
                self.place.hello()
            if name == 3:
                self.place.greeted()

        for stage, (when, where) in enumerate(self.EARLY):
            if where == name:

                @pl.when(pair == when)
                def _():
                    for chunk in self.early:
                        chunk.stages[stage](chunk)

        for p, chunk in enumerate(self.pairs):
            for stage, (after, where) in enumerate(self.NEXT):
                if where == name and p + after < PAIRS:

                    @pl.when(pair == p + after)
                    def _():
                        chunk.stages[stage](chunk)

    def take_pair(self, pair, gw):
        self.in_src[pair] = gw.reshape(self.in_src.shape[1:])

    def last(self, channels):
        comb = self.gvec[...] + channels
        self.small_src[...] = jnp.zeros_like(self.small_src)
        for f in range(self.place.n):
            cols = comb[:, f // 2 * 128 : (f // 2 + 1) * 128]
            self.small_src[f, 0:8] = cols if f % 2 == 0 else pltpu.roll(cols, HEAD_DIM, 1)
            for j in range(2):
                at = (f * 2 + j) * 128
                self.small_src[f, 8 + j : 9 + j] = self.gbe[0:1, at : at + 128]
        done = {chunk: sum(p + after < PAIRS for after, _ in self.NEXT) for p, chunk in enumerate(self.pairs)}
        done.update({self.lev: 0, self.small: 0})
        while any(at < len(Reduce.stages) for at in done.values()):
            for chunk, at in done.items():
                if at < len(Reduce.stages):
                    chunk.stages[at](chunk)
                    done[chunk] = at + 1
        o_out, e_out, s_out, in_out, lev_out, small_out = self.outs
        s_out[...], e_out[...], o_out[...] = [x[...] for x in self.results[:3]]
        for p in range(PAIRS):
            for part in range(3):
                at = (part * PAIRS + p) * PAIR
                in_out[:, at : at + PAIR] = self.results[3 + p][:, part * PAIR : (part + 1) * PAIR]
        half = lev_out.shape[0]
        lev_out[:, : D // 2] = self.results[-1][:half]
        lev_out[:, D // 2 :] = self.results[-1][half:]
        small_out[...] = self.small_out[...]


def place_kernel(o, e, s, win, lev, small, *outs):
    names = ("lev", "chan", "win", "o", "gain1", "bias1", "e", "eb", "s", "sb", "gain2", "bias2")
    to = dict(zip(names, outs))
    for name, ref in (("lev", lev), ("win", win), ("o", o), ("e", e), ("s", s)):
        to[name][...] = ref[...]
    each = to["chan"].shape[1]
    to["chan"][...] = small[5:8, :each]
    for i, name in enumerate(("gain1", "bias1", "sb", "gain2", "bias2")):
        to[name][...] = small[i : i + 1, :each]
    for i in range(2):
        to["eb"][:, i * 128 : (i + 1) * 128] = small[8 + i : 9 + i]


def place_results(ways, o, e, s, win, lev, small):
    each = D // ways
    vec = (1, each)
    shapes = [
        lev.shape, (CHANNELS, each), win.shape, o.shape, vec, vec, e.shape, (1, FF // ways), s.shape, vec, vec, vec,
    ]
    outs = pl.pallas_call(
        place_kernel,
        out_shape=[jax.ShapeDtypeStruct(shape, f32) for shape in shapes],
        compiler_params=params(),
    )(o, e, s, win, lev, small)
    return [x.reshape(-1) if x.shape[0] == 1 else x for x in outs]


def channel_rows():
    pos = np.arange(BLOCK) % CHANNELS + 5
    return (np.arange(EXTRA)[:, None] == pos[None, :]).astype(bf16)


def image(ways, pix, cot, chan, embedded, weights, shards=None):
    emb, low, qkv, qt, vt, sizes = embedded
    w4, wo, vec, be, we, ws = weights
    att, qe, *fetched = attend(ways, qkv, vt, shards)
    if shards is not None:
        we, ws = [x.reshape(-1, x.shape[2]) for x in fetched]
    att, qe = repair(sizes, qkv, vt, att, qe)
    out, gone, de, dt, *grads = middle(att, emb, cot, wo, we, ws, vec, be)
    if shards is not None:
        return out, *back(ways, qe, qkv, de, qt, dt, low, w4, pix, chan, gone, grads)
    return out, *grads, *back(ways, qe, qkv, de, qt, dt, low, w4, pix, chan, gone)


def pack_small(vectors, channels, bias):
    size = bias.shape[0] // 128
    rows = jnp.concatenate([jnp.stack(vectors), channels])
    rows = jnp.pad(rows, ((0, 0), (0, 128 - rows.shape[1])))
    return jnp.concatenate([rows, bias.reshape(size, 128), jnp.zeros((EXTRA - 8 - size, 128), bf16)])


def body(
    ways, pixels, level_table, channel_table, attend_in, attend_out, first_gain, first_bias, expand_weight,
    expand_bias, shrink_weight, shrink_bias, second_gain, second_bias, cotangent,
):
    chan = channel_rows()
    vectors = (first_gain, first_bias, shrink_bias, second_gain, second_bias)
    small = pack_small(vectors, channel_table, expand_bias)
    *embedded, vec, be, w4, wo = embed_gather(ways, pixels, chan, level_table, small, attend_in, attend_out)
    weights = (w4.reshape(3, PAIRS, D, PAIR), wo.reshape(D, D), vec, be, None, None)
    shards = (expand_weight, shrink_weight)
    out, *sums = image(ways, pixels, cotangent[0], chan, embedded, weights, shards)
    return out[None], *place_results(ways, *sums)


def plain_body(
    ways, pixels, level_table, channel_table, attend_in, attend_out, first_gain, first_bias, expand_weight,
    expand_bias, shrink_weight, shrink_bias, second_gain, second_bias, cotangent,
):
    gather = lambda x, axis=0: lax.all_gather(x, "fsdp", axis=axis, tiled=True)
    vectors = jnp.stack((first_gain, first_bias, shrink_bias, second_gain, second_bias))
    chan = channel_rows()
    small = gather(jnp.concatenate([vectors, channel_table]), 1)
    table = jnp.pad(small, ((0, EXTRA - 8), (0, 0)))
    level = gather(level_table)
    w_in = gather(attend_in)
    be = jnp.pad(gather(expand_bias).astype(f32)[None], ((0, 7), (0, 0)))
    w4 = w_in.reshape(D, 3, PAIRS, PAIR).transpose(1, 2, 0, 3)
    weights = (w4, gather(attend_out), table.astype(f32), be, gather(expand_weight), gather(shrink_weight))
    outs = []
    sums = None
    for i in range(pixels.shape[0]):
        pix = pixels[i : i + 1]
        got = image(ways, pix, cotangent[i], chan, embed_plain(pix, chan, level, table, w_in), weights)
        outs.append(got[0])
        grads = [x.astype(f32) for x in got[1:]]
        sums = grads if sums is None else [a + b for a, b in zip(sums, grads)]
    gwo, gwe, gws, gvec, gbe, gw, glev, gchan = sums
    gwin = gw.reshape(PAIRS, D, 3, PAIR).transpose(1, 2, 0, 3).reshape(D, 3 * D)
    count = LEVELS // ways
    glev = glev.reshape(ways, 2, count, D // 2).transpose(0, 2, 1, 3).reshape(LEVELS, D)

    def scatter(x, axis=0):
        return lax.psum(lax.psum_scatter(x, "fsdp", scatter_dimension=axis, tiled=True), "dp")

    small = scatter(gvec + gchan[:8], 1)
    return (
        jnp.stack(outs), scatter(glev), small[5:8], scatter(gwin), scatter(gwo), small[0], small[1], scatter(gwe),
        scatter(gbe[0]), scatter(gws), small[2], small[3], small[4],
    )


def solution(mesh):
    row = P("fsdp", None)
    vector = P("fsdp")
    shared = P(("fsdp", "dp"), None, None)
    weights = (
        row, P(None, "fsdp"), row, row, vector, vector, row, vector, row, vector, vector, vector,
    )
    ways = mesh.shape["fsdp"]
    fits = ways == 8 and mesh.shape["dp"] == 4

    def program(pixels, *rest):
        return (body if fits and pixels.shape[0] == 1 else plain_body)(ways, pixels, *rest)

    return jax.shard_map(
        program,
        mesh=mesh,
        in_specs=(P(("fsdp", "dp"), None), *weights, shared),
        out_specs=(shared, *weights),
        check_vma=False,
    )
```

```python
import functools

import jax
import jax.numpy as jnp
import numpy as np
from jax import lax
from jax.experimental import pallas as pl
from jax.experimental.pallas import tpu as pltpu
from jax.sharding import PartitionSpec as P

D = 512
HEADS = 8
HEAD_DIM = 64
FF = 2048
LEVELS = 256
CHANNELS = 3
SEQ = 3072
BLOCK = 768
BANDS = SEQ // BLOCK
PAIRS = HEADS // 2
PAIR = 2 * HEAD_DIM
REACH = 2
SUB = 256
EXTRA = 16
EPS = 1e-6
LOG2E = 1.4426950408889634
SAFE = 60.0

f32 = jnp.float32
bf16 = jnp.bfloat16
NT = (((1,), (1,)), ((), ()))
TN = (((0,), (0,)), ((), ()))
VMEM_LIMIT = 60 * 2**20


def mm(a, b):
    return jnp.dot(a, b, preferred_element_type=f32)


def mm_nt(a, b):
    return lax.dot_general(a, b, NT, preferred_element_type=f32)


def mm_tn(a, b):
    return lax.dot_general(a, b, TN, preferred_element_type=f32)


def params(*semantics):
    return pltpu.CompilerParams(
        vmem_limit_bytes=VMEM_LIMIT, dimension_semantics=semantics or None
    )


def one_hot_rows(pix):
    width = pix.shape[1]
    return (lax.broadcasted_iota(jnp.int32, (LEVELS, width), 0) == pix).astype(bf16)


def split3(x):
    hi = x.astype(bf16).astype(f32)
    rest = x - hi
    mid = rest.astype(bf16).astype(f32)
    return hi, mid, rest - mid


class Place:
    def __init__(self, ways):
        self.n = ways
        self.f = lax.axis_index("fsdp")
        self.d = lax.axis_index("dp")
        self.core = self.d % 2
        self.side = self.d // 2
        self.quarter = self.core * 2 + self.side

    def at(self, step):
        return (self.f + step) % self.n

    def to(self, step):
        return {"fsdp": self.at(step), "dp": self.d}

    def to_core(self):
        return {"fsdp": self.f, "dp": self.d + 1 - 2 * self.core}

    def to_side(self):
        return {"fsdp": self.f, "dp": self.d + 2 - 4 * self.side}

    def to_cross(self):
        return {"fsdp": self.f, "dp": 3 - self.d}

    def mates(self):
        return [self.to_core(), self.to_side(), self.to_cross()] + [self.to(step) for step in range(1, self.n)]

    def hello(self):
        barrier = pltpu.get_barrier_semaphore()
        for mate in self.mates():
            pl.semaphore_signal(barrier, inc=1, device_id=mate, device_id_type=pl.DeviceIdType.MESH)

    def greeted(self):
        pl.semaphore_wait(pltpu.get_barrier_semaphore(), self.n + 2)


def send(src, dst, sems, i, device):
    return pltpu.make_async_remote_copy(
        src_ref=src,
        dst_ref=dst,
        send_sem=sems.at[0, i],
        recv_sem=sems.at[1, i],
        device_id=device,
        device_id_type=pl.DeviceIdType.MESH,
    )


def window(which, size, count=1):
    return pl.ds(pl.multiple_of(which * size, size), size * count)


class Gather:
    def __init__(self, place, src, dst, sems, across):
        self.place, self.src, self.dst, self.sems = place, src, dst, sems
        self.across, self.n = across, place.n

    @staticmethod
    def semaphores(ways):
        return pltpu.SemaphoreType.DMA((2, 3 * ways + 1))

    def part(self, ref, f, start, count):
        if self.across is None:
            return ref.at[f]
        cut = window(start, self.dst.shape[1 + self.across] // 4, count)
        return ref.at[f, cut] if self.across == 0 else ref.at[f, :, cut]

    def mine(self):
        return self.part(self.dst, self.place.f, self.place.quarter, 1)

    def source(self):
        return self.part(self.src, 0, self.place.quarter, 1)

    def local(self):
        return pltpu.make_async_copy(self.source(), self.mine(), self.sems.at[0, 3 * self.n])

    def copy(self, step):
        return send(self.source(), self.mine(), self.sems, step, self.place.to(step))

    def side_copy(self, step):
        got = self.part(self.dst, self.place.at(self.n - step), self.place.quarter, 1)
        return send(got, got, self.sems, self.n + step, self.place.to_side())

    def core_copy(self, step):
        got = self.part(self.dst, self.place.at(self.n - step), self.place.core * 2, 2)
        return send(got, got, self.sems, 2 * self.n + step, self.place.to_core())

    def start(self):
        self.local().start()
        for step in range(1, self.n):
            self.copy(step).start()

    def swap(self, step):
        if step:
            self.copy(step).wait()
        else:
            self.local().wait()
        if self.across is not None:
            self.side_copy(step).start()

    def share(self, step):
        if self.across is not None:
            self.side_copy(step).wait()
            self.core_copy(step).start()

    def finish(self):
        if self.across is not None:
            for step in range(self.n):
                self.core_copy(step).wait()


class Reduce:
    def __init__(self, place, src, out, bufs):
        self.place, self.src, self.out, self.n = place, src, out, place.n
        self.r1, self.a1, self.r2, self.r3, self.sems = bufs
        self.size = src.shape[1] // 4

    @staticmethod
    def scratch(ways, rows, cols):
        return [
            pltpu.VMEM((ways, rows // 2, cols), bf16),
            pltpu.VMEM((ways, rows // 2, cols), bf16),
            pltpu.VMEM((ways, rows // 4, cols), bf16),
            pltpu.VMEM((ways - 1, rows // 4, cols), bf16),
            pltpu.SemaphoreType.DMA((2, ways + 5)),
        ]

    def half(self, which):
        return self.src.at[:, window(which, 2 * self.size)]

    def local(self):
        return pltpu.make_async_copy(self.half(self.place.core), self.a1, self.sems.at[0, self.n + 4])

    def core_copy(self):
        return send(self.half(1 - self.place.core), self.r1, self.sems, 0, self.place.to_core())

    def side_copy(self):
        theirs = self.a1.at[:, window(1 - self.place.side, self.size)]
        return send(theirs, self.r2, self.sems, self.n, self.place.to_side())

    def copy(self, step):
        return send(self.r2.at[self.place.at(step)], self.r3.at[step - 1], self.sems, step, self.place.to(step))

    def backs(self):
        got = self.out.at[window(self.place.quarter, self.size)]
        mates = (self.place.to_core(), self.place.to_side(), self.place.to_cross())
        return [send(got, got, self.sems, self.n + 1 + i, mate) for i, mate in enumerate(mates)]

    def start(self):
        self.core_copy().start()
        self.local().start()

    def over_sides(self):
        self.local().wait()
        self.core_copy().wait()

        @pl.loop(0, self.n)
        def _(i):
            self.a1[i] = (self.a1[i].astype(f32) + self.r1[i].astype(f32)).astype(bf16)

        self.side_copy().start()

    def over_shards(self):
        self.side_copy().wait()
        cut = window(self.place.side, self.size)

        @pl.loop(0, self.n)
        def _(i):
            self.r2[i] = (self.a1[i, cut].astype(f32) + self.r2[i].astype(f32)).astype(bf16)

        for step in range(1, self.n):
            self.copy(step).start()

    def settle(self):
        for step in range(1, self.n):
            self.copy(step).wait()
        whole = self.r2[self.place.f].astype(f32)
        for step in range(1, self.n):
            whole = whole + self.r3[step - 1].astype(f32)
        self.out[window(self.place.quarter, self.size)] = whole
        for back in self.backs():
            back.start()

    def finish(self):
        for back in self.backs():
            back.wait()

    stages = (start, over_sides, over_shards, settle, finish)


class ReduceSmall:
    def __init__(self, place, src, out, bufs):
        self.place, self.src, self.out, self.n = place, src, out, place.n
        self.r1, self.r2, self.r3, self.sems = bufs

    @staticmethod
    def scratch(ways, rows, cols):
        return [
            pltpu.VMEM((ways, rows, cols), f32),
            pltpu.VMEM((ways, rows, cols), f32),
            pltpu.VMEM((ways - 1, rows, cols), f32),
            pltpu.SemaphoreType.DMA((2, ways + 1)),
        ]

    def core_copy(self):
        return send(self.src, self.r1, self.sems, 0, self.place.to_core())

    def side_copy(self):
        return send(self.src, self.r2, self.sems, self.n, self.place.to_side())

    def copy(self, step):
        return send(self.src.at[self.place.at(step)], self.r3.at[step - 1], self.sems, step, self.place.to(step))

    def start(self):
        self.core_copy().start()

    def over_sides(self):
        self.core_copy().wait()
        self.src[...] += self.r1[...]
        self.side_copy().start()

    def over_shards(self):
        self.side_copy().wait()
        self.src[...] += self.r2[...]
        for step in range(1, self.n):
            self.copy(step).start()

    def settle(self):
        for step in range(1, self.n):
            self.copy(step).wait()
        whole = self.src[self.place.f]
        for step in range(1, self.n):
            whole = whole + self.r3[step - 1]
        self.out[...] = whole

    def finish(self):
        pass

    stages = (start, over_sides, over_shards, settle, finish)


def embed_tile(step, pix_ref, chan_ref, level, table, w, ind_ref, emb_ref, low_ref, qkv_ref, qt_ref, vt_ref, norm_ref):
    emb = mm_tn(one_hot_rows(pix_ref[...]), level) + mm_tn(chan_ref[...], table)
    emb_ref[...] = emb
    low = emb.astype(bf16)
    low_ref[...] = low
    qkv = mm(low, w)
    q = (qkv[:, :D] * HEAD_DIM**-0.5).astype(bf16)
    k = qkv[:, D : 2 * D].astype(bf16)
    v = qkv[:, 2 * D :].astype(bf16)
    qkv_ref[:, :D] = q
    qkv_ref[:, D : 2 * D] = k
    qkv_ref[:, 2 * D :] = v
    qt_ref[...] = q.T
    vt_ref[...] = v.T
    q = q.astype(f32)
    k = k.astype(f32)
    size_q = mm((q * q).astype(bf16), ind_ref[...]).max(0, keepdims=True)
    size_k = mm((k * k).astype(bf16), ind_ref[...]).max(0, keepdims=True)
    row = lax.broadcasted_iota(jnp.int32, (8, 128), 0)
    both = jnp.where(row == 0, size_q, jnp.where(row == 1, size_k, 0.0))
    norm_ref[...] = jnp.maximum(both, jnp.where(step == 0, 0.0, norm_ref[...]))


def embed_plain_kernel(pix_ref, chan_ref, level_ref, table_ref, w_ref, ind_ref, *outs):
    embed_tile(pl.program_id(0), pix_ref, chan_ref, level_ref[...], table_ref[...], w_ref[...], ind_ref, *outs)


def embed_outs():
    rows = lambda i: (i, 0)
    cols = lambda i: (0, i)
    specs = [
        pl.BlockSpec((BLOCK, D), rows),
        pl.BlockSpec((BLOCK, D), rows),
        pl.BlockSpec((BLOCK, 3 * D), rows),
        pl.BlockSpec((D, BLOCK), cols),
        pl.BlockSpec((D, BLOCK), cols),
        pl.BlockSpec((8, 128), lambda i: (0, 0)),
    ]
    shapes = [
        jax.ShapeDtypeStruct((SEQ, D), f32),
        jax.ShapeDtypeStruct((SEQ, D), bf16),
        jax.ShapeDtypeStruct((SEQ, 3 * D), bf16),
        jax.ShapeDtypeStruct((D, SEQ), bf16),
        jax.ShapeDtypeStruct((D, SEQ), bf16),
        jax.ShapeDtypeStruct((8, 128), f32),
    ]
    return specs, shapes


def head_columns():
    return (np.arange(D)[:, None] // HEAD_DIM == np.arange(128)[None, :]).astype(bf16)


def embed_plain(pix, chan, level, table, w_in):
    whole = lambda i: (0, 0)
    specs, shapes = embed_outs()
    return pl.pallas_call(
        embed_plain_kernel,
        grid=(SEQ // BLOCK,),
        in_specs=[
            pl.BlockSpec((1, BLOCK), lambda i: (0, i)),
            pl.BlockSpec((EXTRA, BLOCK), whole),
            pl.BlockSpec((LEVELS, D), whole),
            pl.BlockSpec((EXTRA, D), whole),
            pl.BlockSpec((D, 3 * D), whole),
            pl.BlockSpec((D, 128), whole),
        ],
        out_specs=specs,
        out_shape=shapes,
        compiler_params=params("arbitrary"),
    )(pix, chan, level, table, w_in, head_columns())


def half_lanes(even, odd):
    lane = lax.broadcasted_iota(jnp.int32, even.shape, 1)
    return jnp.where(lane < HEAD_DIM, even, pltpu.roll(odd, HEAD_DIM, 1))


def embed_gather_kernel(
    ways, pix_ref, chan_ref, ind_ref, level_ref, small_ref, win_ref, wo_ref,
    emb_ref, low_ref, qkv_ref, qt_ref, vt_ref, norm_ref, vec_ref, be_ref, w4_ref, wo_out,
    level_s, small_s, win_s, sem_level, sem_small, sem_in, sem_o, sem_w4,
):
    step = pl.program_id(0)
    last = SEQ // BLOCK - 1
    place = Place(ways)
    first = [
        Gather(place, small_ref, small_s, sem_small, None),
        Gather(place, level_ref, level_s, sem_level, 1),
        Gather(place, win_ref, win_s, sem_in, 0),
    ]
    later = Gather(place, wo_ref, wo_out, sem_o, 0)

    def copies():
        for i in range(3 * PAIRS):
            yield pltpu.make_async_copy(win_s.at[:, :, i * PAIR : (i + 1) * PAIR], w4_ref.at[i], sem_w4.at[i])

    @pl.when(step == 0)
    def _():
        place.hello()
        place.greeted()
        for g in (*first, later):
            g.start()
        for i in range(ways):
            for g in first:
                g.swap(i)
        for i in range(ways):
            for g in first:
                g.share(i)
        for i in range(ways // 2):
            both = [small_s[2 * i + odd].astype(f32) for odd in range(2)]
            vec_ref[:, i * 128 : (i + 1) * 128] = half_lanes(*both)
            for odd in range(2):
                for j in range(2):
                    at = ((2 * i + odd) * 2 + j) * 128
                    be_ref[0:1, at : at + 128] = both[odd][8 + j : 9 + j]
        for g in first:
            g.finish()
        for copy in copies():
            copy.start()

    table = vec_ref[...].astype(bf16)
    level = level_s[...].reshape(LEVELS, D)
    w = win_s[...].reshape(D, 3 * D)
    embed_tile(step, pix_ref, chan_ref, level, table, w, ind_ref, emb_ref, low_ref, qkv_ref, qt_ref, vt_ref, norm_ref)

    @pl.when(step == 0)
    def _():
        for i in range(ways):
            later.swap(i)

    @pl.when(step == last - 1)
    def _():
        for i in range(ways):
            later.share(i)

    @pl.when(step == last)
    def _():
        for copy in copies():
            copy.wait()
        later.finish()


def embed_gather(ways, pix, chan, level, small, w_in, wo):
    whole = lambda i: (0, 0)
    anywhere = pl.BlockSpec(memory_space=pl.ANY)
    specs, shapes = embed_outs()
    shards = [x[None] for x in (level, small, w_in, wo)]
    return pl.pallas_call(
        functools.partial(embed_gather_kernel, ways),
        grid=(SEQ // BLOCK,),
        in_specs=[
            pl.BlockSpec((1, BLOCK), lambda i: (0, i)),
            pl.BlockSpec((EXTRA, BLOCK), whole),
            pl.BlockSpec((D, 128), whole),
            *[anywhere] * 4,
        ],
        out_specs=[*specs, pl.BlockSpec((EXTRA, D), whole), pl.BlockSpec((8, FF), whole), *[anywhere] * 2],
        out_shape=[
            *shapes,
            jax.ShapeDtypeStruct((EXTRA, D), f32),
            jax.ShapeDtypeStruct((8, FF), f32),
            jax.ShapeDtypeStruct((3 * PAIRS, ways, D // ways, PAIR), bf16),
            jax.ShapeDtypeStruct((ways, *wo.shape), bf16),
        ],
        scratch_shapes=[
            *[pltpu.VMEM((ways, *x.shape), bf16) for x in (level, small, w_in)],
            *[Gather.semaphores(ways)] * 4,
            pltpu.SemaphoreType.DMA((3 * PAIRS,)),
        ],
        compiler_params=pltpu.CompilerParams(
            vmem_limit_bytes=VMEM_LIMIT, dimension_semantics=("arbitrary",), collective_id=0, has_side_effects=True
        ),
    )(pix, chan, head_columns(), *shards)


def units():
    found = []
    for band in range(BANDS):
        found += [(band, j) for j in range(max(0, band - REACH), band + 1)]
    return found


def lower_mask(keys, queries):
    key = lax.broadcasted_iota(jnp.int32, (keys, queries), 0)
    return key <= lax.broadcasted_iota(jnp.int32, (keys, queries), 1)


def spare_rows(x):
    row = lax.broadcasted_iota(jnp.int32, (HEAD_DIM, x.shape[1]), 0)
    hi, mid, low = split3(x)
    return jnp.where(row == 0, hi, jnp.where(row == 1, mid, jnp.where(row == 2, low, 0.0)))


class Fetch:
    def __init__(self, ways, sources, outs, sems):
        self.place = Place(ways)
        self.wide, self.narrow = [Gather(self.place, s, o, m, 0) for s, o, m in zip(sources, outs, sems)]

    def point(self, pair, name):
        every = range(self.place.n)
        half = self.place.n // 2
        plan = {
            (0, 0): [self.place.hello],
            (0, 3): [self.place.greeted, self.wide.start],
            (0, 8): [self.narrow.start],
            (1, 5): [functools.partial(self.wide.swap, i) for i in every],
            (2, 5): [functools.partial(self.narrow.swap, i) for i in every[:half]],
            (2, 8): [functools.partial(self.narrow.swap, i) for i in every[half:]],
            (3, 3): [functools.partial(self.wide.share, i) for i in every],
            (3, 9): [functools.partial(self.narrow.share, i) for i in every] + [self.wide.finish, self.narrow.finish],
        }
        for (when, where), steps in plan.items():
            if where == name:

                @pl.when(pair == when)
                def _():
                    for step in steps:
                        step()


def attend_kernel(ways, linked, *refs):
    q_ref, k_ref, vt_ref, *refs = refs
    sources, refs = (refs[:2], refs[2:]) if linked else (None, refs)
    o_ref, qe_ref, *refs = refs
    outs, refs = (refs[:2], refs[2:]) if linked else (None, refs)
    acc, lsum, probs, *sems = refs
    pair = pl.program_id(0)
    fetch = Fetch(ways, sources, outs, sems) if linked else None
    lane = lax.broadcasted_iota(jnp.int32, (BLOCK, PAIR), 1)

    def head_only(q, h, other):
        mine = (lane < HEAD_DIM) if h == 0 else (lane >= HEAD_DIM)
        return jnp.where(mine, q, other)

    for unit, (band, j) in enumerate(units()):
        if linked:
            fetch.point(pair, unit)
        here = slice(band * BLOCK, (band + 1) * BLOCK)
        first = j == max(0, band - REACH)
        q = q_ref[here, :]
        off = jnp.zeros_like(q)
        tiles = [(0, BLOCK, BLOCK)] if j < band else [(t * SUB, SUB, (t + 1) * SUB) for t in range(BLOCK // SUB)]
        for h in range(2):
            qm = head_only(q, h, off)
            for at, width, count in tiles:
                ts = slice(at, at + width)
                scores = mm_nt(k_ref[j * BLOCK : j * BLOCK + count, :], qm[ts])
                p = jnp.exp2(scores * LOG2E)
                if j == band:
                    diag = jnp.where(lower_mask(SUB, SUB), p[count - SUB :], 0.0)
                    p = diag if count == SUB else jnp.concatenate([p[: count - SUB], diag], 0)
                part = p.reshape(count // 8, 8, width).sum(0)
                if not first:
                    part += lsum[h, :, ts]
                lsum[h, :, ts] = part
                probs[h, :count, ts] = p.astype(bf16)
        ext = [None, None]
        for h in range(2):
            mine = slice(h * HEAD_DIM, (h + 1) * HEAD_DIM)
            for at, width, count in tiles:
                ts = slice(at, at + width)
                out = mm(vt_ref[mine, j * BLOCK : j * BLOCK + count], probs[h, :count, ts])
                if not first:
                    out += acc[mine, ts]
                acc[mine, ts] = out
            if j == band:
                whole = lsum[h].sum(0, keepdims=True)
                acc[mine, :] = acc[mine, :] / whole
                ext[1 - h] = spare_rows(-jnp.log(whole))
        if j == band:
            o_ref[here, :] = acc[...].T.astype(bf16)
            extra = jnp.concatenate(ext, 0).T.astype(bf16)
            qe_ref[here, :PAIR] = head_only(q, 0, extra)
            qe_ref[here, PAIR:] = head_only(q, 1, extra)
    if linked:
        fetch.point(pair, len(units()))


def attend(ways, qkv, vt, shards=None):
    linked = shards is not None
    anywhere = pl.BlockSpec(memory_space=pl.ANY)
    extra, outs, sems, compiler = [], [], [], params("arbitrary")
    if linked:
        extra = [x[None] for x in shards]
        outs = [jax.ShapeDtypeStruct((ways, *x.shape), bf16) for x in shards]
        sems = [Gather.semaphores(ways)] * 2
        compiler = pltpu.CompilerParams(
            vmem_limit_bytes=VMEM_LIMIT, dimension_semantics=("arbitrary",), collective_id=2, has_side_effects=True
        )
    return pl.pallas_call(
        functools.partial(attend_kernel, ways, linked),
        grid=(PAIRS,),
        in_specs=[
            pl.BlockSpec((SEQ, PAIR), lambda p: (0, p)),
            pl.BlockSpec((SEQ, PAIR), lambda p: (0, PAIRS + p)),
            pl.BlockSpec((PAIR, SEQ), lambda p: (p, 0)),
            *[anywhere] * len(extra),
        ],
        out_specs=[
            pl.BlockSpec((SEQ, PAIR), lambda p: (0, p)),
            pl.BlockSpec((SEQ, 2 * PAIR), lambda p: (0, p)),
            *[anywhere] * len(extra),
        ],
        out_shape=[
            jax.ShapeDtypeStruct((SEQ, D), bf16),
            jax.ShapeDtypeStruct((SEQ, 2 * D), bf16),
            *outs,
        ],
        scratch_shapes=[
            pltpu.VMEM((PAIR, BLOCK), f32),
            pltpu.VMEM((2, 8, BLOCK), f32),
            pltpu.VMEM((2, BLOCK, BLOCK), bf16),
            *sems,
        ],
        compiler_params=compiler,
    )(qkv, qkv, vt, *extra)


def repair_kernel(
    norm_ref, qkv_ref, vt_ref, _att, _qe, att_ref, qe_ref, q_s, k_s, vt_s, o_s, e_s, acc, top, lsum, sems
):
    bound = jnp.max(norm_ref[0:1] * norm_ref[1:2])

    @pl.when(jnp.logical_not(bound < SAFE * SAFE))
    def _():
        lane = lax.broadcasted_iota(jnp.int32, (BLOCK, PAIR), 1)
        chunk = 128

        @pl.loop(0, PAIRS)
        def _(pair):
            at = pl.multiple_of(pair * PAIR, PAIR)
            loads = [
                pltpu.make_async_copy(qkv_ref.at[:, pl.ds(at, PAIR)], q_s, sems.at[0]),
                pltpu.make_async_copy(qkv_ref.at[:, pl.ds(pl.multiple_of(at + D, PAIR), PAIR)], k_s, sems.at[1]),
                pltpu.make_async_copy(vt_ref.at[pl.ds(at, PAIR)], vt_s, sems.at[2]),
            ]
            for load in loads:
                load.start()
            for load in loads:
                load.wait()

            @pl.loop(0, BANDS)
            def _(band):
                here = pl.ds(pl.multiple_of(band * BLOCK, BLOCK), BLOCK)
                q = q_s[here, :]
                ext = [None, None]
                begin = jnp.maximum(band - REACH, 0) * (BLOCK // chunk)
                end = (band + 1) * (BLOCK // chunk)
                for h in range(2):
                    mine = slice(h * HEAD_DIM, (h + 1) * HEAD_DIM)
                    qm = jnp.where((lane < HEAD_DIM) if h == 0 else (lane >= HEAD_DIM), q, jnp.zeros_like(q))

                    def masked(i):
                        start = pl.multiple_of(i * chunk, chunk)
                        scores = mm_nt(k_s[pl.ds(start, chunk), :], qm)
                        key = lax.broadcasted_iota(jnp.int32, scores.shape, 0) + start
                        query = lax.broadcasted_iota(jnp.int32, scores.shape, 1) + band * BLOCK
                        return start, jnp.where(key <= query, scores, -1e30)

                    top[...] = jnp.full(top.shape, -1e30, f32)
                    lsum[...] = jnp.zeros_like(lsum)
                    acc[mine] = jnp.zeros((HEAD_DIM, BLOCK), f32)

                    @pl.loop(begin, end)
                    def _(i):
                        top[...] = jnp.maximum(top[...], masked(i)[1].max(0, keepdims=True))

                    @pl.loop(begin, end)
                    def _(i):
                        start, scores = masked(i)
                        p = jnp.exp2((scores - top[0:1]) * LOG2E)
                        lsum[...] += p.reshape(chunk // 8, 8, BLOCK).sum(0)
                        acc[mine] += mm(vt_s[mine, pl.ds(start, chunk)], p.astype(bf16))

                    whole = lsum[...].sum(0, keepdims=True)
                    acc[mine] = acc[mine] / whole
                    ext[1 - h] = spare_rows(-(top[0:1] + jnp.log(whole)))
                o_s[here, :] = acc[...].T.astype(bf16)
                extra = jnp.concatenate(ext, 0).T.astype(bf16)
                e_s[here, :PAIR] = jnp.where(lane < HEAD_DIM, q, extra)
                e_s[here, PAIR:] = jnp.where(lane < HEAD_DIM, extra, q)

            stores = [
                pltpu.make_async_copy(o_s, att_ref.at[:, pl.ds(at, PAIR)], sems.at[0]),
                pltpu.make_async_copy(
                    e_s, qe_ref.at[:, pl.ds(pl.multiple_of(2 * at, 2 * PAIR), 2 * PAIR)], sems.at[1]
                ),
            ]
            for store in stores:
                store.start()
            for store in stores:
                store.wait()


def repair(sizes, qkv, vt, att, qe):
    anywhere = pl.BlockSpec(memory_space=pl.ANY)
    return pl.pallas_call(
        repair_kernel,
        in_specs=[pl.BlockSpec(memory_space=pltpu.VMEM), *[anywhere] * 4],
        out_specs=[anywhere] * 2,
        out_shape=[jax.ShapeDtypeStruct(x.shape, x.dtype) for x in (att, qe)],
        scratch_shapes=[
            pltpu.VMEM((SEQ, PAIR), bf16),
            pltpu.VMEM((SEQ, PAIR), bf16),
            pltpu.VMEM((PAIR, SEQ), bf16),
            pltpu.VMEM((SEQ, PAIR), bf16),
            pltpu.VMEM((SEQ, 2 * PAIR), bf16),
            pltpu.VMEM((PAIR, BLOCK), f32),
            pltpu.VMEM((8, BLOCK), f32),
            pltpu.VMEM((8, BLOCK), f32),
            pltpu.SemaphoreType.DMA((3,)),
        ],
        input_output_aliases={3: 0, 4: 1},
        compiler_params=params(),
    )(sizes, qkv, vt, att, qe)


def mean(x):
    return jnp.mean(x, -1, keepdims=True)


def norm(x):
    centered = x - mean(x)
    factor = lax.rsqrt(mean(centered * centered) + EPS)
    return centered * factor, factor


def norm_back(scaled, normed, factor):
    return factor * (scaled - mean(scaled) - normed * mean(scaled * normed))


def total(x):
    return x.sum(0, keepdims=True)


def middle_kernel(
    att_ref, emb_ref, cot_ref, wo_ref, we_ref, ws_ref, vec_ref, be_ref, pick_ref,
    out_ref, go_ref, de_ref, dt_ref, gwo_out, gwe_out, gws_out, gvec_ref, gbe_ref, gwo_ref, gwe_ref, gws_ref,
):
    @pl.when(pl.program_id(0) == 0)
    def _():
        for ref in (gwo_ref, gwe_ref, gws_ref, gvec_ref, gbe_ref):
            ref[...] = jnp.zeros_like(ref)

    gain1, bias1, bs, gain2, bias2 = [vec_ref[i : i + 1, :] for i in range(5)]
    att = att_ref[...]
    cot = cot_ref[...]
    normed1, factor1 = norm(emb_ref[...] + mm(att, wo_ref[...]))
    hidden = normed1 * gain1 + bias1
    low = hidden.astype(bf16)
    preact = mm(low, we_ref[...]) + be_ref[0:1, :]
    sig = jax.nn.sigmoid(preact)
    activ = (preact * sig).astype(bf16)
    slope = sig * (1.0 + preact * (1.0 - sig))
    normed2, factor2 = norm(hidden + mm(activ, ws_ref[...]) + bs)
    out_ref[...] = (normed2 * gain2 + bias2).astype(bf16)
    gtwo = norm_back(cot * gain2, normed2, factor2)
    gbranch = gtwo.astype(bf16)
    gws_ref[...] += mm_tn(activ, gbranch)
    gpre = (mm_nt(gbranch, ws_ref[...]) * slope).astype(bf16)
    gbe_ref[0:1, :] += total(gpre.astype(f32))
    gwe_ref[...] += mm_tn(low, gpre)
    ghidden = gtwo + mm_nt(gpre, we_ref[...])
    gone = norm_back(ghidden * gain1, normed1, factor1)
    go_ref[...] = gone
    gatt_branch = gone.astype(bf16)
    gwo_ref[...] += mm_tn(att, gatt_branch)
    gatt = mm_nt(gatt_branch, wo_ref[...]).astype(bf16)
    dt_ref[...] = gatt.T
    gvec_ref[0:1, :] += total(ghidden * normed1)
    gvec_ref[1:2, :] += total(ghidden)
    gvec_ref[2:3, :] += total(gbranch.astype(f32))
    gvec_ref[3:4, :] += total(cot * normed2)
    gvec_ref[4:5, :] += total(cot)

    @pl.when(pl.program_id(0) == pl.num_programs(0) - 1)
    def _():
        gwo_out[...] = gwo_ref[...].astype(bf16)
        gwe_out[...] = gwe_ref[...].astype(bf16)
        gws_out[...] = gws_ref[...].astype(bf16)

    prod = gatt.astype(f32) * att.astype(f32)
    hi, mid, _ = split3(prod)
    pick = pick_ref[...]
    half = D // 2
    place = lax.broadcasted_iota(jnp.int32, (att.shape[0], half), 1) % HEAD_DIM
    lane = lax.broadcasted_iota(jnp.int32, (att.shape[0], PAIR), 1)
    for part in range(2):
        cols = slice(part * half, (part + 1) * half)
        inner = mm(hi[:, cols].astype(bf16), pick) + mm(mid[:, cols].astype(bf16), pick)
        a, b, c = split3(inner)
        ext = jnp.where(place == 0, a, jnp.where(place == 1, b, jnp.where(place == 2, c, 0.0))).astype(bf16)
        for i in range(2):
            pair = 2 * part + i
            e = ext[:, i * PAIR : (i + 1) * PAIR]
            d = gatt[:, pair * PAIR : (pair + 1) * PAIR]
            de_ref[:, 2 * pair * PAIR : (2 * pair + 1) * PAIR] = jnp.where(lane < HEAD_DIM, d, e)
            de_ref[:, (2 * pair + 1) * PAIR : (2 * pair + 2) * PAIR] = jnp.where(lane < HEAD_DIM, e, d)


def middle(att, emb, cot, wo, we, ws, vec, be):
    tile = 768
    half = D // 2
    src = np.arange(half)[:, None] // HEAD_DIM
    dst = np.arange(half)[None, :]
    other = (dst // HEAD_DIM) ^ 1
    pick = np.where((src == other) & (dst % HEAD_DIM < 3), -1.0, 0.0).astype(bf16)
    whole = lambda i: (0, 0)
    rows = lambda i: (i, 0)
    cols = lambda i: (0, i)
    one = pl.Buffered(1)
    return pl.pallas_call(
        middle_kernel,
        grid=(SEQ // tile,),
        in_specs=[
            pl.BlockSpec((tile, D), rows),
            pl.BlockSpec((tile, D), rows),
            pl.BlockSpec((tile, D), rows),
            pl.BlockSpec((D, D), whole, pipeline_mode=one),
            pl.BlockSpec((D, FF), whole, pipeline_mode=one),
            pl.BlockSpec((FF, D), whole, pipeline_mode=one),
            pl.BlockSpec((EXTRA, D), whole),
            pl.BlockSpec((8, FF), whole),
            pl.BlockSpec((half, half), whole),
        ],
        out_specs=[
            pl.BlockSpec((tile, D), rows),
            pl.BlockSpec((tile, D), rows),
            pl.BlockSpec((tile, 2 * D), rows),
            pl.BlockSpec((D, tile), cols),
            pl.BlockSpec((D, D), whole, pipeline_mode=one),
            pl.BlockSpec((D, FF), whole, pipeline_mode=one),
            pl.BlockSpec((FF, D), whole, pipeline_mode=one),
            pl.BlockSpec((8, D), whole),
            pl.BlockSpec((8, FF), whole),
        ],
        out_shape=[
            jax.ShapeDtypeStruct((SEQ, D), bf16),
            jax.ShapeDtypeStruct((SEQ, D), f32),
            jax.ShapeDtypeStruct((SEQ, 2 * D), bf16),
            jax.ShapeDtypeStruct((D, SEQ), bf16),
            jax.ShapeDtypeStruct((D, D), bf16),
            jax.ShapeDtypeStruct((D, FF), bf16),
            jax.ShapeDtypeStruct((FF, D), bf16),
            jax.ShapeDtypeStruct((8, D), f32),
            jax.ShapeDtypeStruct((8, FF), f32),
        ],
        scratch_shapes=[pltpu.VMEM((D, D), f32), pltpu.VMEM((D, FF), f32), pltpu.VMEM((FF, D), f32)],
        compiler_params=params("arbitrary"),
    )(att, emb, cot, wo, we, ws, vec, be, pick)


def back_kernel(ways, linked, *refs):
    refs = list(refs)
    take = lambda count: [refs.pop(0) for _ in range(count)]
    qe_ref, k_ref, v_ref, de_ref, qt_ref, dt_ref, low_ref, w_ref, pix_ref, chan_ref, go_ref = take(11)
    given = take(5) if linked else None
    outs = take(6 if linked else 3)
    ke, ve, km, probs, slopes, dkt, dvt, dqa, grads, gemb, sem = take(11)
    pair = pl.program_id(0)
    copy = pltpu.make_async_copy(go_ref, gemb, sem)
    sums = Sums(ways, given, outs, refs) if linked else None

    def point(name):
        if linked:
            sums.point(pair, name)

    @pl.when(pair == 0)
    def _():
        copy.start()

    point("begin")
    lane = lax.broadcasted_iota(jnp.int32, (BLOCK, PAIR), 1)
    for band in range(BANDS):
        here = slice(band * BLOCK, (band + 1) * BLOCK)
        k = k_ref[here, :]
        v = v_ref[here, :]
        one = jnp.ones_like(k)
        zero = jnp.zeros_like(k)
        right = jnp.where(lane < HEAD_DIM + 3, one, zero)
        left = jnp.where(lane < 3, one, zero)
        ke[0, here] = jnp.where(lane < HEAD_DIM, k, right)
        ke[1, here] = jnp.where(lane < HEAD_DIM, left, k)
        ve[0, here] = jnp.where(lane < HEAD_DIM, v, right)
        ve[1, here] = jnp.where(lane < HEAD_DIM, left, v)
        km[0, here] = jnp.where(lane < HEAD_DIM, k, zero)
        km[1, here] = jnp.where(lane < HEAD_DIM, zero, k)
    for unit, (band, j) in enumerate(units()):
        point(unit)
        t0 = band * BLOCK
        k0 = j * BLOCK
        first = j == max(0, band - REACH)
        tiles = [(0, BLOCK)] if j < band else [(i * SUB, SUB) for i in range(BLOCK // SUB)]
        for h in range(2):
            mine = slice(h * HEAD_DIM, (h + 1) * HEAD_DIM)
            lanes = slice(h * PAIR, (h + 1) * PAIR)
            for at, count in tiles:
                ts = slice(t0 + at, t0 + BLOCK)
                ks = slice(k0 + at, k0 + at + count)
                scores = mm_nt(qe_ref[ts, lanes], ke[h, ks])
                p = jnp.exp2(scores * LOG2E)
                if j == band:
                    t = lax.broadcasted_iota(jnp.int32, p.shape, 0)
                    p = jnp.where(lax.broadcasted_iota(jnp.int32, p.shape, 1) <= t, p, 0.0)
                dp = mm_nt(de_ref[ts, lanes], ve[h, ks])
                cols = slice(at, at + count)
                probs[h, at:, cols] = p.astype(bf16)
                slopes[h, at:, cols] = (p * dp).astype(bf16)
        for h in range(2):
            mine = slice(h * HEAD_DIM, (h + 1) * HEAD_DIM)
            for at, count in tiles:
                ts = slice(t0 + at, t0 + BLOCK)
                ks = slice(k0 + at, k0 + at + count)
                cols = slice(at, at + count)
                dv = mm(dt_ref[mine, ts], probs[h, at:, cols])
                dk = mm(qt_ref[mine, ts], slopes[h, at:, cols])
                if j == band:
                    dvt[mine, ks] = dv
                    dkt[mine, ks] = dk
                else:
                    dvt[mine, ks] += dv
                    dkt[mine, ks] += dk
        if j < band:
            dq = mm(slopes[0], km[0, k0 : k0 + BLOCK]) + mm(slopes[1], km[1, k0 : k0 + BLOCK])
            if first:
                dqa[...] = dq
            else:
                dqa[...] += dq
        else:
            for i in range(BLOCK // SUB):
                count = (i + 1) * SUB
                rows = slice(i * SUB, count)
                dq = mm(slopes[0, rows, :count], km[0, k0 : k0 + count])
                dq += mm(slopes[1, rows, :count], km[1, k0 : k0 + count])
                if not first:
                    dq += dqa[rows]
                grads[t0 + i * SUB : t0 + count, :PAIR] = (dq * HEAD_DIM**-0.5).astype(bf16)
    for band in range(BANDS):
        here = slice(band * BLOCK, (band + 1) * BLOCK)
        grads[here, PAIR : 2 * PAIR] = dkt[:, here].T.astype(bf16)
        grads[here, 2 * PAIR :] = dvt[:, here].T.astype(bf16)

    gw = mm_tn(low_ref[...], grads[...]).astype(bf16)
    if linked:
        sums.take_pair(pair, gw)
        point("ready")
    else:
        outs[0][0] = gw

    @pl.when(pair == 0)
    def _():
        copy.wait()

    w = jnp.concatenate([w_ref[0, 0], w_ref[1, 0], w_ref[2, 0]], 1)
    for band in range(BANDS):
        here = slice(band * BLOCK, (band + 1) * BLOCK)
        gemb[here] += mm_nt(grads[here, :], w)
    point("end")

    @pl.when(pair == PAIRS - 1)
    def _():
        table = None
        for band in range(BANDS):
            here = slice(band * BLOCK, (band + 1) * BLOCK)
            rows = jnp.concatenate([one_hot_rows(pix_ref[:, here]), chan_ref[...]], 0)
            part = mm(rows, gemb[here].astype(bf16))
            table = part if band == 0 else table + part
        count = LEVELS // ways
        for f in range(ways):
            mine = table[f * count : (f + 1) * count].astype(bf16)
            to = sums.lev_src.at[f] if linked else outs[1].at[f]
            to[:count] = mine[:, : D // 2]
            to[count:] = mine[:, D // 2 :]
        if linked:
            sums.last(table[LEVELS : LEVELS + 8])
        else:
            outs[2][...] = table[LEVELS:]


def back(ways, qe, qkv, de, qt, dt, low, w4, pix, chan, gone, given=None):
    one = pl.Buffered(1)
    rows = D // ways
    linked = given is not None
    anywhere = pl.BlockSpec(memory_space=pl.ANY)
    out_specs = [
        pl.BlockSpec((1, D, 3 * PAIR), lambda p: (p, 0, 0)),
        pl.BlockSpec((ways, 2 * LEVELS // ways, D // 2), lambda p: (0, 0, 0)),
        pl.BlockSpec((EXTRA, D), lambda p: (0, 0)),
    ]
    out_shape = [
        jax.ShapeDtypeStruct((PAIRS, D, 3 * PAIR), bf16),
        jax.ShapeDtypeStruct((ways, 2 * LEVELS // ways, D // 2), bf16),
        jax.ShapeDtypeStruct((EXTRA, D), f32),
    ]
    extra, extra_specs, extra_scratch = [], [], []
    compiler = params("arbitrary")
    if linked:
        split = lambda x: x.reshape(ways, x.shape[0] // ways, x.shape[1])
        gwo, gwe, gws, gvec, gbe = given
        extra = [split(gwo), split(gwe), split(gws), gvec, gbe]
        extra_specs = [anywhere] * 3
        extra_specs += [pl.BlockSpec(x.shape, lambda p: (0, 0)) for x in (gvec, gbe)]
        shapes = [(rows, D), (rows, FF), (FF // ways, D), (rows, 3 * D), (LEVELS // ways, D), (EXTRA, 128)]
        out_specs = [pl.BlockSpec(shape, lambda p: (0, 0), pipeline_mode=one) for shape in shapes]
        out_shape = [jax.ShapeDtypeStruct(shape, f32) for shape in shapes]
        extra_scratch = Sums.scratch(ways)
        compiler = pltpu.CompilerParams(
            vmem_limit_bytes=VMEM_LIMIT, dimension_semantics=("arbitrary",), collective_id=1, has_side_effects=True
        )
    return pl.pallas_call(
        functools.partial(back_kernel, ways, linked),
        grid=(PAIRS,),
        in_specs=[
            pl.BlockSpec((SEQ, 2 * PAIR), lambda p: (0, p)),
            pl.BlockSpec((SEQ, PAIR), lambda p: (0, PAIRS + p)),
            pl.BlockSpec((SEQ, PAIR), lambda p: (0, 2 * PAIRS + p)),
            pl.BlockSpec((SEQ, 2 * PAIR), lambda p: (0, p)),
            pl.BlockSpec((PAIR, SEQ), lambda p: (p, 0)),
            pl.BlockSpec((PAIR, SEQ), lambda p: (p, 0)),
            pl.BlockSpec((SEQ, D), lambda p: (0, 0), pipeline_mode=one),
            pl.BlockSpec((3, 1, D, PAIR), lambda p: (0, p, 0, 0)),
            pl.BlockSpec((1, SEQ), lambda p: (0, 0)),
            pl.BlockSpec((EXTRA, BLOCK), lambda p: (0, 0)),
            anywhere,
            *extra_specs,
        ],
        out_specs=out_specs,
        out_shape=out_shape,
        scratch_shapes=[
            pltpu.VMEM((2, SEQ, PAIR), bf16),
            pltpu.VMEM((2, SEQ, PAIR), bf16),
            pltpu.VMEM((2, SEQ, PAIR), bf16),
            pltpu.VMEM((2, BLOCK, BLOCK), bf16),
            pltpu.VMEM((2, BLOCK, BLOCK), bf16),
            pltpu.VMEM((PAIR, SEQ), f32),
            pltpu.VMEM((PAIR, SEQ), f32),
            pltpu.VMEM((BLOCK, PAIR), f32),
            pltpu.VMEM((SEQ, 3 * PAIR), bf16),
            pltpu.VMEM((SEQ, D), f32),
            pltpu.SemaphoreType.DMA,
            *extra_scratch,
        ],
        compiler_params=compiler,
    )(qe, qkv, qkv, de, qt, dt, low, w4, pix, chan, gone, *extra)


class Sums:
    EARLY = ((0, 3), (0, "ready"), (1, "ready"), (2, "ready"), (3, 3))
    NEXT = ((0, "ready"), (1, 3), (1, "ready"), (2, "ready"), (3, "ready"))

    @staticmethod
    def sizes(ways):
        rows = D // ways
        return [(FF // ways, D), (rows, FF), (rows, D)] + [(rows, 3 * PAIR)] * PAIRS + [(2 * LEVELS // ways, D // 2)]

    @staticmethod
    def scratch(ways):
        sizes = Sums.sizes(ways)
        scratch = [pltpu.VMEM(size, f32) for size in sizes]
        scratch += [pltpu.VMEM((PAIRS, ways, *sizes[3]), bf16), pltpu.VMEM((ways, *sizes[-1]), bf16)]
        scratch += [pltpu.VMEM((ways, EXTRA, 128), f32), pltpu.VMEM((EXTRA, 128), f32)]
        for size in sizes:
            scratch += Reduce.scratch(ways, *size)
        return scratch + ReduceSmall.scratch(ways, EXTRA, 128)

    def __init__(self, ways, given, outs, scratch):
        self.ways, self.outs = ways, outs
        self.place = Place(ways)
        wo, we, ws, self.gvec, self.gbe = given
        scratch = list(scratch)
        take = lambda count: [scratch.pop(0) for _ in range(count)]
        self.results = take(4 + PAIRS)
        self.in_src, self.lev_src = take(2)
        self.small_src, self.small_out = take(2)
        sources = [ws, we, wo, *[self.in_src.at[p] for p in range(PAIRS)], self.lev_src]
        chunks = [Reduce(self.place, s, r, take(5)) for s, r in zip(sources, self.results)]
        self.early, self.pairs, self.lev = chunks[:3], chunks[3:-1], chunks[-1]
        self.small = ReduceSmall(self.place, self.small_src, self.small_out, take(4))

    def point(self, pair, name):
        @pl.when(pair == 0)
        def _():
            if name == "begin":
                self.place.hello()
            if name == 3:
                self.place.greeted()

        for stage, (when, where) in enumerate(self.EARLY):
            if where == name:

                @pl.when(pair == when)
                def _():
                    for chunk in self.early:
                        chunk.stages[stage](chunk)

        for p, chunk in enumerate(self.pairs):
            for stage, (after, where) in enumerate(self.NEXT):
                if where == name and p + after < PAIRS:

                    @pl.when(pair == p + after)
                    def _():
                        chunk.stages[stage](chunk)

    def take_pair(self, pair, gw):
        self.in_src[pair] = gw.reshape(self.in_src.shape[1:])

    def last(self, channels):
        comb = self.gvec[...] + channels
        self.small_src[...] = jnp.zeros_like(self.small_src)
        for f in range(self.place.n):
            cols = comb[:, f // 2 * 128 : (f // 2 + 1) * 128]
            self.small_src[f, 0:8] = cols if f % 2 == 0 else pltpu.roll(cols, HEAD_DIM, 1)
            for j in range(2):
                at = (f * 2 + j) * 128
                self.small_src[f, 8 + j : 9 + j] = self.gbe[0:1, at : at + 128]
        done = {chunk: sum(p + after < PAIRS for after, _ in self.NEXT) for p, chunk in enumerate(self.pairs)}
        done.update({self.lev: 0, self.small: 0})
        while any(at < len(Reduce.stages) for at in done.values()):
            for chunk, at in done.items():
                if at < len(Reduce.stages):
                    chunk.stages[at](chunk)
                    done[chunk] = at + 1
        o_out, e_out, s_out, in_out, lev_out, small_out = self.outs
        s_out[...], e_out[...], o_out[...] = [x[...] for x in self.results[:3]]
        for p in range(PAIRS):
            for part in range(3):
                at = (part * PAIRS + p) * PAIR
                in_out[:, at : at + PAIR] = self.results[3 + p][:, part * PAIR : (part + 1) * PAIR]
        half = lev_out.shape[0]
        lev_out[:, : D // 2] = self.results[-1][:half]
        lev_out[:, D // 2 :] = self.results[-1][half:]
        small_out[...] = self.small_out[...]


def place_kernel(o, e, s, win, lev, small, *outs):
    names = ("lev", "chan", "win", "o", "gain1", "bias1", "e", "eb", "s", "sb", "gain2", "bias2")
    to = dict(zip(names, outs))
    for name, ref in (("lev", lev), ("win", win), ("o", o), ("e", e), ("s", s)):
        to[name][...] = ref[...]
    each = to["chan"].shape[1]
    to["chan"][...] = small[5:8, :each]
    for i, name in enumerate(("gain1", "bias1", "sb", "gain2", "bias2")):
        to[name][...] = small[i : i + 1, :each]
    for i in range(2):
        to["eb"][:, i * 128 : (i + 1) * 128] = small[8 + i : 9 + i]


def place_results(ways, o, e, s, win, lev, small):
    each = D // ways
    vec = (1, each)
    shapes = [
        lev.shape, (CHANNELS, each), win.shape, o.shape, vec, vec, e.shape, (1, FF // ways), s.shape, vec, vec, vec,
    ]
    outs = pl.pallas_call(
        place_kernel,
        out_shape=[jax.ShapeDtypeStruct(shape, f32) for shape in shapes],
        compiler_params=params(),
    )(o, e, s, win, lev, small)
    return [x.reshape(-1) if x.shape[0] == 1 else x for x in outs]


def channel_rows():
    pos = np.arange(BLOCK) % CHANNELS + 5
    return (np.arange(EXTRA)[:, None] == pos[None, :]).astype(bf16)


def image(ways, pix, cot, chan, embedded, weights, shards=None):
    emb, low, qkv, qt, vt, sizes = embedded
    w4, wo, vec, be, we, ws = weights
    att, qe, *fetched = attend(ways, qkv, vt, shards)
    if shards is not None:
        we, ws = [x.reshape(-1, x.shape[2]) for x in fetched]
    att, qe = repair(sizes, qkv, vt, att, qe)
    out, gone, de, dt, *grads = middle(att, emb, cot, wo, we, ws, vec, be)
    if shards is not None:
        return out, *back(ways, qe, qkv, de, qt, dt, low, w4, pix, chan, gone, grads)
    return out, *grads, *back(ways, qe, qkv, de, qt, dt, low, w4, pix, chan, gone)


def pack_small(vectors, channels, bias):
    size = bias.shape[0] // 128
    rows = jnp.concatenate([jnp.stack(vectors), channels])
    rows = jnp.pad(rows, ((0, 0), (0, 128 - rows.shape[1])))
    return jnp.concatenate([rows, bias.reshape(size, 128), jnp.zeros((EXTRA - 8 - size, 128), bf16)])


def body(
    ways, pixels, level_table, channel_table, attend_in, attend_out, first_gain, first_bias, expand_weight,
    expand_bias, shrink_weight, shrink_bias, second_gain, second_bias, cotangent,
):
    chan = channel_rows()
    vectors = (first_gain, first_bias, shrink_bias, second_gain, second_bias)
    small = pack_small(vectors, channel_table, expand_bias)
    *embedded, vec, be, w4, wo = embed_gather(ways, pixels, chan, level_table, small, attend_in, attend_out)
    weights = (w4.reshape(3, PAIRS, D, PAIR), wo.reshape(D, D), vec, be, None, None)
    shards = (expand_weight, shrink_weight)
    out, *sums = image(ways, pixels, cotangent[0], chan, embedded, weights, shards)
    return out[None], *place_results(ways, *sums)


def plain_body(
    ways, pixels, level_table, channel_table, attend_in, attend_out, first_gain, first_bias, expand_weight,
    expand_bias, shrink_weight, shrink_bias, second_gain, second_bias, cotangent,
):
    gather = lambda x, axis=0: lax.all_gather(x, "fsdp", axis=axis, tiled=True)
    vectors = jnp.stack((first_gain, first_bias, shrink_bias, second_gain, second_bias))
    chan = channel_rows()
    small = gather(jnp.concatenate([vectors, channel_table]), 1)
    table = jnp.pad(small, ((0, EXTRA - 8), (0, 0)))
    level = gather(level_table)
    w_in = gather(attend_in)
    be = jnp.pad(gather(expand_bias).astype(f32)[None], ((0, 7), (0, 0)))
    w4 = w_in.reshape(D, 3, PAIRS, PAIR).transpose(1, 2, 0, 3)
    weights = (w4, gather(attend_out), table.astype(f32), be, gather(expand_weight), gather(shrink_weight))
    outs = []
    sums = None
    for i in range(pixels.shape[0]):
        pix = pixels[i : i + 1]
        got = image(ways, pix, cotangent[i], chan, embed_plain(pix, chan, level, table, w_in), weights)
        outs.append(got[0])
        grads = [x.astype(f32) for x in got[1:]]
        sums = grads if sums is None else [a + b for a, b in zip(sums, grads)]
    gwo, gwe, gws, gvec, gbe, gw, glev, gchan = sums
    gwin = gw.reshape(PAIRS, D, 3, PAIR).transpose(1, 2, 0, 3).reshape(D, 3 * D)
    count = LEVELS // ways
    glev = glev.reshape(ways, 2, count, D // 2).transpose(0, 2, 1, 3).reshape(LEVELS, D)

    def scatter(x, axis=0):
        return lax.psum(lax.psum_scatter(x, "fsdp", scatter_dimension=axis, tiled=True), "dp")

    small = scatter(gvec + gchan[:8], 1)
    return (
        jnp.stack(outs), scatter(glev), small[5:8], scatter(gwin), scatter(gwo), small[0], small[1], scatter(gwe),
        scatter(gbe[0]), scatter(gws), small[2], small[3], small[4],
    )


def solution(mesh):
    row = P("fsdp", None)
    vector = P("fsdp")
    shared = P(("fsdp", "dp"), None, None)
    weights = (
        row, P(None, "fsdp"), row, row, vector, vector, row, vector, row, vector, vector, vector,
    )
    ways = mesh.shape["fsdp"]
    fits = ways == 8 and mesh.shape["dp"] == 4

    def program(pixels, *rest):
        return (body if fits and pixels.shape[0] == 1 else plain_body)(ways, pixels, *rest)

    return jax.shard_map(
        program,
        mesh=mesh,
        in_specs=(P(("fsdp", "dp"), None), *weights, shared),
        out_specs=(shared, *weights),
        check_vma=False,
    )
```

```python
import functools

import jax
import jax.numpy as jnp
import numpy as np
from jax import lax
from jax.experimental import pallas as pl
from jax.experimental.pallas import tpu as pltpu
from jax.sharding import PartitionSpec as P

D = 512
HEADS = 8
HEAD_DIM = 64
FF = 2048
LEVELS = 256
CHANNELS = 3
SEQ = 3072
BLOCK = 768
BANDS = SEQ // BLOCK
PAIRS = HEADS // 2
PAIR = 2 * HEAD_DIM
REACH = 2
SUB = 256
EXTRA = 16
EPS = 1e-6
LOG2E = 1.4426950408889634
SAFE = 60.0

f32 = jnp.float32
bf16 = jnp.bfloat16
NT = (((1,), (1,)), ((), ()))
TN = (((0,), (0,)), ((), ()))
VMEM_LIMIT = 60 * 2**20


def mm(a, b):
    return jnp.dot(a, b, preferred_element_type=f32)


def mm_nt(a, b):
    return lax.dot_general(a, b, NT, preferred_element_type=f32)


def mm_tn(a, b):
    return lax.dot_general(a, b, TN, preferred_element_type=f32)


def params(*semantics):
    return pltpu.CompilerParams(
        vmem_limit_bytes=VMEM_LIMIT, dimension_semantics=semantics or None
    )


def one_hot_rows(pix):
    width = pix.shape[1]
    return (lax.broadcasted_iota(jnp.int32, (LEVELS, width), 0) == pix).astype(bf16)


def split3(x):
    hi = x.astype(bf16).astype(f32)
    rest = x - hi
    mid = rest.astype(bf16).astype(f32)
    return hi, mid, rest - mid


class Place:
    def __init__(self, ways):
        self.n = ways
        self.f = lax.axis_index("fsdp")
        self.d = lax.axis_index("dp")
        self.core = self.d % 2
        self.side = self.d // 2
        self.quarter = self.core * 2 + self.side

    def at(self, step):
        return (self.f + step) % self.n

    def to(self, step):
        return {"fsdp": self.at(step), "dp": self.d}

    def to_core(self):
        return {"fsdp": self.f, "dp": self.d + 1 - 2 * self.core}

    def to_side(self):
        return {"fsdp": self.f, "dp": self.d + 2 - 4 * self.side}

    def to_cross(self):
        return {"fsdp": self.f, "dp": 3 - self.d}

    def mates(self):
        return [self.to_core(), self.to_side(), self.to_cross()] + [self.to(step) for step in range(1, self.n)]

    def hello(self):
        barrier = pltpu.get_barrier_semaphore()
        for mate in self.mates():
            pl.semaphore_signal(barrier, inc=1, device_id=mate, device_id_type=pl.DeviceIdType.MESH)

    def greeted(self):
        pl.semaphore_wait(pltpu.get_barrier_semaphore(), self.n + 2)


def send(src, dst, sems, i, device):
    return pltpu.make_async_remote_copy(
        src_ref=src,
        dst_ref=dst,
        send_sem=sems.at[0, i],
        recv_sem=sems.at[1, i],
        device_id=device,
        device_id_type=pl.DeviceIdType.MESH,
    )


def window(which, size, count=1):
    return pl.ds(pl.multiple_of(which * size, size), size * count)


class Gather:
    def __init__(self, place, src, dst, sems, across):
        self.place, self.src, self.dst, self.sems = place, src, dst, sems
        self.across, self.n = across, place.n

    @staticmethod
    def semaphores(ways):
        return pltpu.SemaphoreType.DMA((2, 3 * ways + 1))

    def part(self, ref, f, start, count):
        if self.across is None:
            return ref.at[f]
        cut = window(start, self.dst.shape[1 + self.across] // 4, count)
        return ref.at[f, cut] if self.across == 0 else ref.at[f, :, cut]

    def mine(self):
        return self.part(self.dst, self.place.f, self.place.quarter, 1)

    def source(self):
        return self.part(self.src, 0, self.place.quarter, 1)

    def local(self):
        return pltpu.make_async_copy(self.source(), self.mine(), self.sems.at[0, 3 * self.n])

    def copy(self, step):
        return send(self.source(), self.mine(), self.sems, step, self.place.to(step))

    def side_copy(self, step):
        got = self.part(self.dst, self.place.at(self.n - step), self.place.quarter, 1)
        return send(got, got, self.sems, self.n + step, self.place.to_side())

    def core_copy(self, step):
        got = self.part(self.dst, self.place.at(self.n - step), self.place.core * 2, 2)
        return send(got, got, self.sems, 2 * self.n + step, self.place.to_core())

    def start(self):
        self.local().start()
        for step in range(1, self.n):
            self.copy(step).start()

    def swap(self, step):
        if step:
            self.copy(step).wait()
        else:
            self.local().wait()
        if self.across is not None:
            self.side_copy(step).start()

    def share(self, step):
        if self.across is not None:
            self.side_copy(step).wait()
            self.core_copy(step).start()

    def finish(self):
        if self.across is not None:
            for step in range(self.n):
                self.core_copy(step).wait()


class Reduce:
    def __init__(self, place, src, out, bufs):
        self.place, self.src, self.out, self.n = place, src, out, place.n
        self.r1, self.a1, self.r2, self.r3, self.sems = bufs
        self.size = src.shape[1] // 4

    @staticmethod
    def scratch(ways, rows, cols):
        return [
            pltpu.VMEM((ways, rows // 2, cols), bf16),
            pltpu.VMEM((ways, rows // 2, cols), bf16),
            pltpu.VMEM((ways, rows // 4, cols), bf16),
            pltpu.VMEM((ways - 1, rows // 4, cols), bf16),
            pltpu.SemaphoreType.DMA((2, ways + 5)),
        ]

    def half(self, which):
        return self.src.at[:, window(which, 2 * self.size)]

    def local(self):
        return pltpu.make_async_copy(self.half(self.place.core), self.a1, self.sems.at[0, self.n + 4])

    def core_copy(self):
        return send(self.half(1 - self.place.core), self.r1, self.sems, 0, self.place.to_core())

    def side_copy(self):
        theirs = self.a1.at[:, window(1 - self.place.side, self.size)]
        return send(theirs, self.r2, self.sems, self.n, self.place.to_side())

    def copy(self, step):
        return send(self.r2.at[self.place.at(step)], self.r3.at[step - 1], self.sems, step, self.place.to(step))

    def backs(self):
        got = self.out.at[window(self.place.quarter, self.size)]
        mates = (self.place.to_core(), self.place.to_side(), self.place.to_cross())
        return [send(got, got, self.sems, self.n + 1 + i, mate) for i, mate in enumerate(mates)]

    def start(self):
        self.core_copy().start()
        self.local().start()

    def over_sides(self):
        self.local().wait()
        self.core_copy().wait()

        @pl.loop(0, self.n)
        def _(i):
            self.a1[i] = (self.a1[i].astype(f32) + self.r1[i].astype(f32)).astype(bf16)

        self.side_copy().start()

    def over_shards(self):
        self.side_copy().wait()
        cut = window(self.place.side, self.size)

        @pl.loop(0, self.n)
        def _(i):
            self.r2[i] = (self.a1[i, cut].astype(f32) + self.r2[i].astype(f32)).astype(bf16)

        for step in range(1, self.n):
            self.copy(step).start()

    def settle(self):
        for step in range(1, self.n):
            self.copy(step).wait()
        whole = self.r2[self.place.f].astype(f32)
        for step in range(1, self.n):
            whole = whole + self.r3[step - 1].astype(f32)
        self.out[window(self.place.quarter, self.size)] = whole
        for back in self.backs():
            back.start()

    def finish(self):
        for back in self.backs():
            back.wait()

    stages = (start, over_sides, over_shards, settle, finish)


class ReduceSmall:
    def __init__(self, place, src, out, bufs):
        self.place, self.src, self.out, self.n = place, src, out, place.n
        self.r1, self.r2, self.r3, self.sems = bufs

    @staticmethod
    def scratch(ways, rows, cols):
        return [
            pltpu.VMEM((ways, rows, cols), f32),
            pltpu.VMEM((ways, rows, cols), f32),
            pltpu.VMEM((ways - 1, rows, cols), f32),
            pltpu.SemaphoreType.DMA((2, ways + 1)),
        ]

    def core_copy(self):
        return send(self.src, self.r1, self.sems, 0, self.place.to_core())

    def side_copy(self):
        return send(self.src, self.r2, self.sems, self.n, self.place.to_side())

    def copy(self, step):
        return send(self.src.at[self.place.at(step)], self.r3.at[step - 1], self.sems, step, self.place.to(step))

    def start(self):
        self.core_copy().start()

    def over_sides(self):
        self.core_copy().wait()
        self.src[...] += self.r1[...]
        self.side_copy().start()

    def over_shards(self):
        self.side_copy().wait()
        self.src[...] += self.r2[...]
        for step in range(1, self.n):
            self.copy(step).start()

    def settle(self):
        for step in range(1, self.n):
            self.copy(step).wait()
        whole = self.src[self.place.f]
        for step in range(1, self.n):
            whole = whole + self.r3[step - 1]
        self.out[...] = whole

    def finish(self):
        pass

    stages = (start, over_sides, over_shards, settle, finish)


def embed_tile(step, pix_ref, chan_ref, level, table, w, ind_ref, emb_ref, low_ref, qkv_ref, qt_ref, vt_ref, norm_ref):
    emb = mm_tn(one_hot_rows(pix_ref[...]), level) + mm_tn(chan_ref[...], table)
    emb_ref[...] = emb
    low = emb.astype(bf16)
    low_ref[...] = low
    qkv = mm(low, w)
    q = (qkv[:, :D] * HEAD_DIM**-0.5).astype(bf16)
    k = qkv[:, D : 2 * D].astype(bf16)
    v = qkv[:, 2 * D :].astype(bf16)
    qkv_ref[:, :D] = q
    qkv_ref[:, D : 2 * D] = k
    qkv_ref[:, 2 * D :] = v
    qt_ref[...] = q.T
    vt_ref[...] = v.T
    q = q.astype(f32)
    k = k.astype(f32)
    size_q = mm((q * q).astype(bf16), ind_ref[...]).max(0, keepdims=True)
    size_k = mm((k * k).astype(bf16), ind_ref[...]).max(0, keepdims=True)
    row = lax.broadcasted_iota(jnp.int32, (8, 128), 0)
    both = jnp.where(row == 0, size_q, jnp.where(row == 1, size_k, 0.0))
    norm_ref[...] = jnp.maximum(both, jnp.where(step == 0, 0.0, norm_ref[...]))


def embed_plain_kernel(pix_ref, chan_ref, level_ref, table_ref, w_ref, ind_ref, *outs):
    embed_tile(pl.program_id(0), pix_ref, chan_ref, level_ref[...], table_ref[...], w_ref[...], ind_ref, *outs)


def embed_outs():
    rows = lambda i: (i, 0)
    cols = lambda i: (0, i)
    specs = [
        pl.BlockSpec((BLOCK, D), rows),
        pl.BlockSpec((BLOCK, D), rows),
        pl.BlockSpec((BLOCK, 3 * D), rows),
        pl.BlockSpec((D, BLOCK), cols),
        pl.BlockSpec((D, BLOCK), cols),
        pl.BlockSpec((8, 128), lambda i: (0, 0)),
    ]
    shapes = [
        jax.ShapeDtypeStruct((SEQ, D), f32),
        jax.ShapeDtypeStruct((SEQ, D), bf16),
        jax.ShapeDtypeStruct((SEQ, 3 * D), bf16),
        jax.ShapeDtypeStruct((D, SEQ), bf16),
        jax.ShapeDtypeStruct((D, SEQ), bf16),
        jax.ShapeDtypeStruct((8, 128), f32),
    ]
    return specs, shapes


def head_columns():
    return (np.arange(D)[:, None] // HEAD_DIM == np.arange(128)[None, :]).astype(bf16)


def embed_plain(pix, chan, level, table, w_in):
    whole = lambda i: (0, 0)
    specs, shapes = embed_outs()
    return pl.pallas_call(
        embed_plain_kernel,
        grid=(SEQ // BLOCK,),
        in_specs=[
            pl.BlockSpec((1, BLOCK), lambda i: (0, i)),
            pl.BlockSpec((EXTRA, BLOCK), whole),
            pl.BlockSpec((LEVELS, D), whole),
            pl.BlockSpec((EXTRA, D), whole),
            pl.BlockSpec((D, 3 * D), whole),
            pl.BlockSpec((D, 128), whole),
        ],
        out_specs=specs,
        out_shape=shapes,
        compiler_params=params("arbitrary"),
    )(pix, chan, level, table, w_in, head_columns())


def half_lanes(even, odd):
    lane = lax.broadcasted_iota(jnp.int32, even.shape, 1)
    return jnp.where(lane < HEAD_DIM, even, pltpu.roll(odd, HEAD_DIM, 1))


def embed_gather_kernel(
    ways, pix_ref, chan_ref, ind_ref, level_ref, small_ref, win_ref, wo_ref,
    emb_ref, low_ref, qkv_ref, qt_ref, vt_ref, norm_ref, vec_ref, be_ref, w4_ref, wo_out,
    level_s, small_s, win_s, sem_level, sem_small, sem_in, sem_o, sem_w4,
):
    step = pl.program_id(0)
    last = SEQ // BLOCK - 1
    place = Place(ways)
    first = [
        Gather(place, small_ref, small_s, sem_small, None),
        Gather(place, level_ref, level_s, sem_level, 1),
        Gather(place, win_ref, win_s, sem_in, 0),
    ]
    later = Gather(place, wo_ref, wo_out, sem_o, 0)

    def copies():
        for i in range(3 * PAIRS):
            yield pltpu.make_async_copy(win_s.at[:, :, i * PAIR : (i + 1) * PAIR], w4_ref.at[i], sem_w4.at[i])

    @pl.when(step == 0)
    def _():
        place.hello()
        place.greeted()
        for g in (*first, later):
            g.start()
        for i in range(ways):
            for g in first:
                g.swap(i)
        for i in range(ways):
            for g in first:
                g.share(i)
        for i in range(ways // 2):
            both = [small_s[2 * i + odd].astype(f32) for odd in range(2)]
            vec_ref[:, i * 128 : (i + 1) * 128] = half_lanes(*both)
            for odd in range(2):
                for j in range(2):
                    at = ((2 * i + odd) * 2 + j) * 128
                    be_ref[0:1, at : at + 128] = both[odd][8 + j : 9 + j]
        for g in first:
            g.finish()
        for copy in copies():
            copy.start()

    table = vec_ref[...].astype(bf16)
    level = level_s[...].reshape(LEVELS, D)
    w = win_s[...].reshape(D, 3 * D)
    embed_tile(step, pix_ref, chan_ref, level, table, w, ind_ref, emb_ref, low_ref, qkv_ref, qt_ref, vt_ref, norm_ref)

    @pl.when(step == 0)
    def _():
        for i in range(ways):
            later.swap(i)

    @pl.when(step == last - 1)
    def _():
        for i in range(ways):
            later.share(i)

    @pl.when(step == last)
    def _():
        for copy in copies():
            copy.wait()
        later.finish()


def embed_gather(ways, pix, chan, level, small, w_in, wo):
    whole = lambda i: (0, 0)
    anywhere = pl.BlockSpec(memory_space=pl.ANY)
    specs, shapes = embed_outs()
    shards = [x[None] for x in (level, small, w_in, wo)]
    return pl.pallas_call(
        functools.partial(embed_gather_kernel, ways),
        grid=(SEQ // BLOCK,),
        in_specs=[
            pl.BlockSpec((1, BLOCK), lambda i: (0, i)),
            pl.BlockSpec((EXTRA, BLOCK), whole),
            pl.BlockSpec((D, 128), whole),
            *[anywhere] * 4,
        ],
        out_specs=[*specs, pl.BlockSpec((EXTRA, D), whole), pl.BlockSpec((8, FF), whole), *[anywhere] * 2],
        out_shape=[
            *shapes,
            jax.ShapeDtypeStruct((EXTRA, D), f32),
            jax.ShapeDtypeStruct((8, FF), f32),
            jax.ShapeDtypeStruct((3 * PAIRS, ways, D // ways, PAIR), bf16),
            jax.ShapeDtypeStruct((ways, *wo.shape), bf16),
        ],
        scratch_shapes=[
            *[pltpu.VMEM((ways, *x.shape), bf16) for x in (level, small, w_in)],
            *[Gather.semaphores(ways)] * 4,
            pltpu.SemaphoreType.DMA((3 * PAIRS,)),
        ],
        compiler_params=pltpu.CompilerParams(
            vmem_limit_bytes=VMEM_LIMIT, dimension_semantics=("arbitrary",), collective_id=0, has_side_effects=True
        ),
    )(pix, chan, head_columns(), *shards)


def units():
    found = []
    for band in range(BANDS):
        found += [(band, j) for j in range(max(0, band - REACH), band + 1)]
    return found


def lower_mask(keys, queries):
    key = lax.broadcasted_iota(jnp.int32, (keys, queries), 0)
    return key <= lax.broadcasted_iota(jnp.int32, (keys, queries), 1)


def spare_rows(x):
    row = lax.broadcasted_iota(jnp.int32, (HEAD_DIM, x.shape[1]), 0)
    hi, mid, low = split3(x)
    return jnp.where(row == 0, hi, jnp.where(row == 1, mid, jnp.where(row == 2, low, 0.0)))


class Fetch:
    def __init__(self, ways, sources, outs, sems):
        self.place = Place(ways)
        self.wide, self.narrow = [Gather(self.place, s, o, m, 0) for s, o, m in zip(sources, outs, sems)]

    def point(self, pair, name):
        half = self.place.n // 2
        steps_of = lambda method, parts: [functools.partial(method, i) for i in parts]
        near, far = range(half), range(half, self.place.n)
        wide, narrow = self.wide, self.narrow
        plan = {
            (0, 0): [self.place.hello],
            (0, 5): [self.place.greeted, wide.start, narrow.start],
            (1, 5): steps_of(wide.swap, near),
            (1, 9): steps_of(wide.swap, far),
            (2, 5): steps_of(narrow.swap, near),
            (2, 9): steps_of(narrow.swap, far) + steps_of(wide.share, near),
            (3, 5): steps_of(wide.share, far) + steps_of(narrow.share, near),
            (3, 9): steps_of(narrow.share, far) + [wide.finish, narrow.finish],
        }
        for (when, where), steps in plan.items():
            if where == name:

                @pl.when(pair == when)
                def _():
                    for step in steps:
                        step()


def attend_kernel(ways, linked, *refs):
    q_ref, k_ref, vt_ref, *refs = refs
    sources, refs = (refs[:2], refs[2:]) if linked else (None, refs)
    o_ref, qe_ref, *refs = refs
    outs, refs = (refs[:2], refs[2:]) if linked else (None, refs)
    acc, lsum, probs, *sems = refs
    pair = pl.program_id(0)
    fetch = Fetch(ways, sources, outs, sems) if linked else None
    lane = lax.broadcasted_iota(jnp.int32, (BLOCK, PAIR), 1)

    def head_only(q, h, other):
        mine = (lane < HEAD_DIM) if h == 0 else (lane >= HEAD_DIM)
        return jnp.where(mine, q, other)

    for unit, (band, j) in enumerate(units()):
        if linked:
            fetch.point(pair, unit)
        here = slice(band * BLOCK, (band + 1) * BLOCK)
        first = j == max(0, band - REACH)
        q = q_ref[here, :]
        off = jnp.zeros_like(q)
        tiles = [(0, BLOCK, BLOCK)] if j < band else [(t * SUB, SUB, (t + 1) * SUB) for t in range(BLOCK // SUB)]
        for h in range(2):
            qm = head_only(q, h, off)
            for at, width, count in tiles:
                ts = slice(at, at + width)
                scores = mm_nt(k_ref[j * BLOCK : j * BLOCK + count, :], qm[ts])
                p = jnp.exp2(scores * LOG2E)
                if j == band:
                    diag = jnp.where(lower_mask(SUB, SUB), p[count - SUB :], 0.0)
                    p = diag if count == SUB else jnp.concatenate([p[: count - SUB], diag], 0)
                part = p.reshape(count // 8, 8, width).sum(0)
                if not first:
                    part += lsum[h, :, ts]
                lsum[h, :, ts] = part
                probs[h, :count, ts] = p.astype(bf16)
        ext = [None, None]
        for h in range(2):
            mine = slice(h * HEAD_DIM, (h + 1) * HEAD_DIM)
            for at, width, count in tiles:
                ts = slice(at, at + width)
                out = mm(vt_ref[mine, j * BLOCK : j * BLOCK + count], probs[h, :count, ts])
                if not first:
                    out += acc[mine, ts]
                acc[mine, ts] = out
            if j == band:
                whole = lsum[h].sum(0, keepdims=True)
                acc[mine, :] = acc[mine, :] / whole
                ext[1 - h] = spare_rows(-jnp.log(whole))
        if j == band:
            o_ref[here, :] = acc[...].T.astype(bf16)
            extra = jnp.concatenate(ext, 0).T.astype(bf16)
            qe_ref[here, :PAIR] = head_only(q, 0, extra)
            qe_ref[here, PAIR:] = head_only(q, 1, extra)
    if linked:
        fetch.point(pair, len(units()))


def attend(ways, qkv, vt, shards=None):
    linked = shards is not None
    anywhere = pl.BlockSpec(memory_space=pl.ANY)
    extra, outs, sems, compiler = [], [], [], params("arbitrary")
    if linked:
        extra = [x[None] for x in shards]
        outs = [jax.ShapeDtypeStruct((ways, *x.shape), bf16) for x in shards]
        sems = [Gather.semaphores(ways)] * 2
        compiler = pltpu.CompilerParams(
            vmem_limit_bytes=VMEM_LIMIT, dimension_semantics=("arbitrary",), collective_id=2, has_side_effects=True
        )
    return pl.pallas_call(
        functools.partial(attend_kernel, ways, linked),
        grid=(PAIRS,),
        in_specs=[
            pl.BlockSpec((SEQ, PAIR), lambda p: (0, p)),
            pl.BlockSpec((SEQ, PAIR), lambda p: (0, PAIRS + p)),
            pl.BlockSpec((PAIR, SEQ), lambda p: (p, 0)),
            *[anywhere] * len(extra),
        ],
        out_specs=[
            pl.BlockSpec((SEQ, PAIR), lambda p: (0, p)),
            pl.BlockSpec((SEQ, 2 * PAIR), lambda p: (0, p)),
            *[anywhere] * len(extra),
        ],
        out_shape=[
            jax.ShapeDtypeStruct((SEQ, D), bf16),
            jax.ShapeDtypeStruct((SEQ, 2 * D), bf16),
            *outs,
        ],
        scratch_shapes=[
            pltpu.VMEM((PAIR, BLOCK), f32),
            pltpu.VMEM((2, 8, BLOCK), f32),
            pltpu.VMEM((2, BLOCK, BLOCK), bf16),
            *sems,
        ],
        compiler_params=compiler,
    )(qkv, qkv, vt, *extra)


def repair_kernel(
    norm_ref, qkv_ref, vt_ref, _att, _qe, att_ref, qe_ref, q_s, k_s, vt_s, o_s, e_s, acc, top, lsum, sems
):
    bound = jnp.max(norm_ref[0:1] * norm_ref[1:2])

    @pl.when(jnp.logical_not(bound < SAFE * SAFE))
    def _():
        lane = lax.broadcasted_iota(jnp.int32, (BLOCK, PAIR), 1)
        chunk = 128

        @pl.loop(0, PAIRS)
        def _(pair):
            at = pl.multiple_of(pair * PAIR, PAIR)
            loads = [
                pltpu.make_async_copy(qkv_ref.at[:, pl.ds(at, PAIR)], q_s, sems.at[0]),
                pltpu.make_async_copy(qkv_ref.at[:, pl.ds(pl.multiple_of(at + D, PAIR), PAIR)], k_s, sems.at[1]),
                pltpu.make_async_copy(vt_ref.at[pl.ds(at, PAIR)], vt_s, sems.at[2]),
            ]
            for load in loads:
                load.start()
            for load in loads:
                load.wait()

            @pl.loop(0, BANDS)
            def _(band):
                here = pl.ds(pl.multiple_of(band * BLOCK, BLOCK), BLOCK)
                q = q_s[here, :]
                ext = [None, None]
                begin = jnp.maximum(band - REACH, 0) * (BLOCK // chunk)
                end = (band + 1) * (BLOCK // chunk)
                for h in range(2):
                    mine = slice(h * HEAD_DIM, (h + 1) * HEAD_DIM)
                    qm = jnp.where((lane < HEAD_DIM) if h == 0 else (lane >= HEAD_DIM), q, jnp.zeros_like(q))

                    def masked(i):
                        start = pl.multiple_of(i * chunk, chunk)
                        scores = mm_nt(k_s[pl.ds(start, chunk), :], qm)
                        key = lax.broadcasted_iota(jnp.int32, scores.shape, 0) + start
                        query = lax.broadcasted_iota(jnp.int32, scores.shape, 1) + band * BLOCK
                        return start, jnp.where(key <= query, scores, -1e30)

                    top[...] = jnp.full(top.shape, -1e30, f32)
                    lsum[...] = jnp.zeros_like(lsum)
                    acc[mine] = jnp.zeros((HEAD_DIM, BLOCK), f32)

                    @pl.loop(begin, end)
                    def _(i):
                        top[...] = jnp.maximum(top[...], masked(i)[1].max(0, keepdims=True))

                    @pl.loop(begin, end)
                    def _(i):
                        start, scores = masked(i)
                        p = jnp.exp2((scores - top[0:1]) * LOG2E)
                        lsum[...] += p.reshape(chunk // 8, 8, BLOCK).sum(0)
                        acc[mine] += mm(vt_s[mine, pl.ds(start, chunk)], p.astype(bf16))

                    whole = lsum[...].sum(0, keepdims=True)
                    acc[mine] = acc[mine] / whole
                    ext[1 - h] = spare_rows(-(top[0:1] + jnp.log(whole)))
                o_s[here, :] = acc[...].T.astype(bf16)
                extra = jnp.concatenate(ext, 0).T.astype(bf16)
                e_s[here, :PAIR] = jnp.where(lane < HEAD_DIM, q, extra)
                e_s[here, PAIR:] = jnp.where(lane < HEAD_DIM, extra, q)

            stores = [
                pltpu.make_async_copy(o_s, att_ref.at[:, pl.ds(at, PAIR)], sems.at[0]),
                pltpu.make_async_copy(
                    e_s, qe_ref.at[:, pl.ds(pl.multiple_of(2 * at, 2 * PAIR), 2 * PAIR)], sems.at[1]
                ),
            ]
            for store in stores:
                store.start()
            for store in stores:
                store.wait()


def repair(sizes, qkv, vt, att, qe):
    anywhere = pl.BlockSpec(memory_space=pl.ANY)
    return pl.pallas_call(
        repair_kernel,
        in_specs=[pl.BlockSpec(memory_space=pltpu.VMEM), *[anywhere] * 4],
        out_specs=[anywhere] * 2,
        out_shape=[jax.ShapeDtypeStruct(x.shape, x.dtype) for x in (att, qe)],
        scratch_shapes=[
            pltpu.VMEM((SEQ, PAIR), bf16),
            pltpu.VMEM((SEQ, PAIR), bf16),
            pltpu.VMEM((PAIR, SEQ), bf16),
            pltpu.VMEM((SEQ, PAIR), bf16),
            pltpu.VMEM((SEQ, 2 * PAIR), bf16),
            pltpu.VMEM((PAIR, BLOCK), f32),
            pltpu.VMEM((8, BLOCK), f32),
            pltpu.VMEM((8, BLOCK), f32),
            pltpu.SemaphoreType.DMA((3,)),
        ],
        input_output_aliases={3: 0, 4: 1},
        compiler_params=params(),
    )(sizes, qkv, vt, att, qe)


def mean(x):
    return jnp.mean(x, -1, keepdims=True)


def norm(x):
    centered = x - mean(x)
    factor = lax.rsqrt(mean(centered * centered) + EPS)
    return centered * factor, factor


def norm_back(scaled, normed, factor):
    return factor * (scaled - mean(scaled) - normed * mean(scaled * normed))


def total(x):
    return x.sum(0, keepdims=True)


def middle_kernel(
    att_ref, emb_ref, cot_ref, wo_ref, we_ref, ws_ref, vec_ref, be_ref, pick_ref,
    out_ref, go_ref, de_ref, dt_ref, gwo_out, gwe_out, gws_out, gvec_ref, gbe_ref, gwo_ref, gwe_ref, gws_ref,
):
    @pl.when(pl.program_id(0) == 0)
    def _():
        for ref in (gwo_ref, gwe_ref, gws_ref, gvec_ref, gbe_ref):
            ref[...] = jnp.zeros_like(ref)

    gain1, bias1, bs, gain2, bias2 = [vec_ref[i : i + 1, :] for i in range(5)]
    att = att_ref[...]
    cot = cot_ref[...]
    normed1, factor1 = norm(emb_ref[...] + mm(att, wo_ref[...]))
    hidden = normed1 * gain1 + bias1
    low = hidden.astype(bf16)
    preact = mm(low, we_ref[...]) + be_ref[0:1, :]
    sig = jax.nn.sigmoid(preact)
    activ = (preact * sig).astype(bf16)
    slope = sig * (1.0 + preact * (1.0 - sig))
    normed2, factor2 = norm(hidden + mm(activ, ws_ref[...]) + bs)
    out_ref[...] = (normed2 * gain2 + bias2).astype(bf16)
    gtwo = norm_back(cot * gain2, normed2, factor2)
    gbranch = gtwo.astype(bf16)
    gws_ref[...] += mm_tn(activ, gbranch)
    gpre = (mm_nt(gbranch, ws_ref[...]) * slope).astype(bf16)
    gbe_ref[0:1, :] += total(gpre.astype(f32))
    gwe_ref[...] += mm_tn(low, gpre)
    ghidden = gtwo + mm_nt(gpre, we_ref[...])
    gone = norm_back(ghidden * gain1, normed1, factor1)
    go_ref[...] = gone
    gatt_branch = gone.astype(bf16)
    gwo_ref[...] += mm_tn(att, gatt_branch)
    gatt = mm_nt(gatt_branch, wo_ref[...]).astype(bf16)
    dt_ref[...] = gatt.T
    gvec_ref[0:1, :] += total(ghidden * normed1)
    gvec_ref[1:2, :] += total(ghidden)
    gvec_ref[2:3, :] += total(gbranch.astype(f32))
    gvec_ref[3:4, :] += total(cot * normed2)
    gvec_ref[4:5, :] += total(cot)

    @pl.when(pl.program_id(0) == pl.num_programs(0) - 1)
    def _():
        gwo_out[...] = gwo_ref[...].astype(bf16)
        gwe_out[...] = gwe_ref[...].astype(bf16)
        gws_out[...] = gws_ref[...].astype(bf16)

    prod = gatt.astype(f32) * att.astype(f32)
    hi, mid, _ = split3(prod)
    pick = pick_ref[...]
    half = D // 2
    place = lax.broadcasted_iota(jnp.int32, (att.shape[0], half), 1) % HEAD_DIM
    lane = lax.broadcasted_iota(jnp.int32, (att.shape[0], PAIR), 1)
    for part in range(2):
        cols = slice(part * half, (part + 1) * half)
        inner = mm(hi[:, cols].astype(bf16), pick) + mm(mid[:, cols].astype(bf16), pick)
        a, b, c = split3(inner)
        ext = jnp.where(place == 0, a, jnp.where(place == 1, b, jnp.where(place == 2, c, 0.0))).astype(bf16)
        for i in range(2):
            pair = 2 * part + i
            e = ext[:, i * PAIR : (i + 1) * PAIR]
            d = gatt[:, pair * PAIR : (pair + 1) * PAIR]
            de_ref[:, 2 * pair * PAIR : (2 * pair + 1) * PAIR] = jnp.where(lane < HEAD_DIM, d, e)
            de_ref[:, (2 * pair + 1) * PAIR : (2 * pair + 2) * PAIR] = jnp.where(lane < HEAD_DIM, e, d)


def middle(att, emb, cot, wo, we, ws, vec, be):
    tile = 768
    half = D // 2
    src = np.arange(half)[:, None] // HEAD_DIM
    dst = np.arange(half)[None, :]
    other = (dst // HEAD_DIM) ^ 1
    pick = np.where((src == other) & (dst % HEAD_DIM < 3), -1.0, 0.0).astype(bf16)
    whole = lambda i: (0, 0)
    rows = lambda i: (i, 0)
    cols = lambda i: (0, i)
    one = pl.Buffered(1)
    return pl.pallas_call(
        middle_kernel,
        grid=(SEQ // tile,),
        in_specs=[
            pl.BlockSpec((tile, D), rows),
            pl.BlockSpec((tile, D), rows),
            pl.BlockSpec((tile, D), rows),
            pl.BlockSpec((D, D), whole, pipeline_mode=one),
            pl.BlockSpec((D, FF), whole, pipeline_mode=one),
            pl.BlockSpec((FF, D), whole, pipeline_mode=one),
            pl.BlockSpec((EXTRA, D), whole),
            pl.BlockSpec((8, FF), whole),
            pl.BlockSpec((half, half), whole),
        ],
        out_specs=[
            pl.BlockSpec((tile, D), rows),
            pl.BlockSpec((tile, D), rows),
            pl.BlockSpec((tile, 2 * D), rows),
            pl.BlockSpec((D, tile), cols),
            pl.BlockSpec((D, D), whole, pipeline_mode=one),
            pl.BlockSpec((D, FF), whole, pipeline_mode=one),
            pl.BlockSpec((FF, D), whole, pipeline_mode=one),
            pl.BlockSpec((8, D), whole),
            pl.BlockSpec((8, FF), whole),
        ],
        out_shape=[
            jax.ShapeDtypeStruct((SEQ, D), bf16),
            jax.ShapeDtypeStruct((SEQ, D), f32),
            jax.ShapeDtypeStruct((SEQ, 2 * D), bf16),
            jax.ShapeDtypeStruct((D, SEQ), bf16),
            jax.ShapeDtypeStruct((D, D), bf16),
            jax.ShapeDtypeStruct((D, FF), bf16),
            jax.ShapeDtypeStruct((FF, D), bf16),
            jax.ShapeDtypeStruct((8, D), f32),
            jax.ShapeDtypeStruct((8, FF), f32),
        ],
        scratch_shapes=[pltpu.VMEM((D, D), f32), pltpu.VMEM((D, FF), f32), pltpu.VMEM((FF, D), f32)],
        compiler_params=params("arbitrary"),
    )(att, emb, cot, wo, we, ws, vec, be, pick)


def back_kernel(ways, linked, *refs):
    refs = list(refs)
    take = lambda count: [refs.pop(0) for _ in range(count)]
    qe_ref, k_ref, v_ref, de_ref, qt_ref, dt_ref, low_ref, w_ref, pix_ref, chan_ref, go_ref = take(11)
    given = take(5) if linked else None
    outs = take(6 if linked else 3)
    ke, ve, km, probs, slopes, dkt, dvt, dqa, grads, gemb, sem = take(11)
    pair = pl.program_id(0)
    copy = pltpu.make_async_copy(go_ref, gemb, sem)
    sums = Sums(ways, given, outs, refs) if linked else None

    def point(name):
        if linked:
            sums.point(pair, name)

    @pl.when(pair == 0)
    def _():
        copy.start()

    point("begin")
    lane = lax.broadcasted_iota(jnp.int32, (BLOCK, PAIR), 1)
    for band in range(BANDS):
        here = slice(band * BLOCK, (band + 1) * BLOCK)
        k = k_ref[here, :]
        v = v_ref[here, :]
        one = jnp.ones_like(k)
        zero = jnp.zeros_like(k)
        right = jnp.where(lane < HEAD_DIM + 3, one, zero)
        left = jnp.where(lane < 3, one, zero)
        ke[0, here] = jnp.where(lane < HEAD_DIM, k, right)
        ke[1, here] = jnp.where(lane < HEAD_DIM, left, k)
        ve[0, here] = jnp.where(lane < HEAD_DIM, v, right)
        ve[1, here] = jnp.where(lane < HEAD_DIM, left, v)
        km[0, here] = jnp.where(lane < HEAD_DIM, k, zero)
        km[1, here] = jnp.where(lane < HEAD_DIM, zero, k)
    for unit, (band, j) in enumerate(units()):
        point(unit)
        t0 = band * BLOCK
        k0 = j * BLOCK
        first = j == max(0, band - REACH)
        tiles = [(0, BLOCK)] if j < band else [(i * SUB, SUB) for i in range(BLOCK // SUB)]
        for h in range(2):
            mine = slice(h * HEAD_DIM, (h + 1) * HEAD_DIM)
            lanes = slice(h * PAIR, (h + 1) * PAIR)
            for at, count in tiles:
                ts = slice(t0 + at, t0 + BLOCK)
                ks = slice(k0 + at, k0 + at + count)
                scores = mm_nt(qe_ref[ts, lanes], ke[h, ks])
                p = jnp.exp2(scores * LOG2E)
                if j == band:
                    t = lax.broadcasted_iota(jnp.int32, p.shape, 0)
                    p = jnp.where(lax.broadcasted_iota(jnp.int32, p.shape, 1) <= t, p, 0.0)
                dp = mm_nt(de_ref[ts, lanes], ve[h, ks])
                cols = slice(at, at + count)
                probs[h, at:, cols] = p.astype(bf16)
                slopes[h, at:, cols] = (p * dp).astype(bf16)
        for h in range(2):
            mine = slice(h * HEAD_DIM, (h + 1) * HEAD_DIM)
            for at, count in tiles:
                ts = slice(t0 + at, t0 + BLOCK)
                ks = slice(k0 + at, k0 + at + count)
                cols = slice(at, at + count)
                dv = mm(dt_ref[mine, ts], probs[h, at:, cols])
                dk = mm(qt_ref[mine, ts], slopes[h, at:, cols])
                if j == band:
                    dvt[mine, ks] = dv
                    dkt[mine, ks] = dk
                else:
                    dvt[mine, ks] += dv
                    dkt[mine, ks] += dk
        if j < band:
            dq = mm(slopes[0], km[0, k0 : k0 + BLOCK]) + mm(slopes[1], km[1, k0 : k0 + BLOCK])
            if first:
                dqa[...] = dq
            else:
                dqa[...] += dq
        else:
            for i in range(BLOCK // SUB):
                count = (i + 1) * SUB
                rows = slice(i * SUB, count)
                dq = mm(slopes[0, rows, :count], km[0, k0 : k0 + count])
                dq += mm(slopes[1, rows, :count], km[1, k0 : k0 + count])
                if not first:
                    dq += dqa[rows]
                grads[t0 + i * SUB : t0 + count, :PAIR] = (dq * HEAD_DIM**-0.5).astype(bf16)
    for band in range(BANDS):
        here = slice(band * BLOCK, (band + 1) * BLOCK)
        grads[here, PAIR : 2 * PAIR] = dkt[:, here].T.astype(bf16)
        grads[here, 2 * PAIR :] = dvt[:, here].T.astype(bf16)

    gw = mm_tn(low_ref[...], grads[...]).astype(bf16)
    if linked:
        sums.take_pair(pair, gw)
        point("ready")
    else:
        outs[0][0] = gw

    @pl.when(pair == 0)
    def _():
        copy.wait()

    w = jnp.concatenate([w_ref[0, 0], w_ref[1, 0], w_ref[2, 0]], 1)
    for band in range(BANDS):
        here = slice(band * BLOCK, (band + 1) * BLOCK)
        gemb[here] += mm_nt(grads[here, :], w)
    point("end")

    @pl.when(pair == PAIRS - 1)
    def _():
        table = None
        for band in range(BANDS):
            here = slice(band * BLOCK, (band + 1) * BLOCK)
            rows = jnp.concatenate([one_hot_rows(pix_ref[:, here]), chan_ref[...]], 0)
            part = mm(rows, gemb[here].astype(bf16))
            table = part if band == 0 else table + part
        count = LEVELS // ways
        for f in range(ways):
            mine = table[f * count : (f + 1) * count].astype(bf16)
            to = sums.lev_src.at[f] if linked else outs[1].at[f]
            to[:count] = mine[:, : D // 2]
            to[count:] = mine[:, D // 2 :]
        if linked:
            sums.last(table[LEVELS : LEVELS + 8])
        else:
            outs[2][...] = table[LEVELS:]


def back(ways, qe, qkv, de, qt, dt, low, w4, pix, chan, gone, given=None):
    one = pl.Buffered(1)
    rows = D // ways
    linked = given is not None
    anywhere = pl.BlockSpec(memory_space=pl.ANY)
    out_specs = [
        pl.BlockSpec((1, D, 3 * PAIR), lambda p: (p, 0, 0)),
        pl.BlockSpec((ways, 2 * LEVELS // ways, D // 2), lambda p: (0, 0, 0)),
        pl.BlockSpec((EXTRA, D), lambda p: (0, 0)),
    ]
    out_shape = [
        jax.ShapeDtypeStruct((PAIRS, D, 3 * PAIR), bf16),
        jax.ShapeDtypeStruct((ways, 2 * LEVELS // ways, D // 2), bf16),
        jax.ShapeDtypeStruct((EXTRA, D), f32),
    ]
    extra, extra_specs, extra_scratch = [], [], []
    compiler = params("arbitrary")
    if linked:
        split = lambda x: x.reshape(ways, x.shape[0] // ways, x.shape[1])
        gwo, gwe, gws, gvec, gbe = given
        extra = [split(gwo), split(gwe), split(gws), gvec, gbe]
        extra_specs = [anywhere] * 3
        extra_specs += [pl.BlockSpec(x.shape, lambda p: (0, 0)) for x in (gvec, gbe)]
        shapes = [(rows, D), (rows, FF), (FF // ways, D), (rows, 3 * D), (LEVELS // ways, D), (EXTRA, 128)]
        out_specs = [pl.BlockSpec(shape, lambda p: (0, 0), pipeline_mode=one) for shape in shapes]
        out_shape = [jax.ShapeDtypeStruct(shape, f32) for shape in shapes]
        extra_scratch = Sums.scratch(ways)
        compiler = pltpu.CompilerParams(
            vmem_limit_bytes=VMEM_LIMIT, dimension_semantics=("arbitrary",), collective_id=1, has_side_effects=True
        )
    return pl.pallas_call(
        functools.partial(back_kernel, ways, linked),
        grid=(PAIRS,),
        in_specs=[
            pl.BlockSpec((SEQ, 2 * PAIR), lambda p: (0, p)),
            pl.BlockSpec((SEQ, PAIR), lambda p: (0, PAIRS + p)),
            pl.BlockSpec((SEQ, PAIR), lambda p: (0, 2 * PAIRS + p)),
            pl.BlockSpec((SEQ, 2 * PAIR), lambda p: (0, p)),
            pl.BlockSpec((PAIR, SEQ), lambda p: (p, 0)),
            pl.BlockSpec((PAIR, SEQ), lambda p: (p, 0)),
            pl.BlockSpec((SEQ, D), lambda p: (0, 0), pipeline_mode=one),
            pl.BlockSpec((3, 1, D, PAIR), lambda p: (0, p, 0, 0)),
            pl.BlockSpec((1, SEQ), lambda p: (0, 0)),
            pl.BlockSpec((EXTRA, BLOCK), lambda p: (0, 0)),
            anywhere,
            *extra_specs,
        ],
        out_specs=out_specs,
        out_shape=out_shape,
        scratch_shapes=[
            pltpu.VMEM((2, SEQ, PAIR), bf16),
            pltpu.VMEM((2, SEQ, PAIR), bf16),
            pltpu.VMEM((2, SEQ, PAIR), bf16),
            pltpu.VMEM((2, BLOCK, BLOCK), bf16),
            pltpu.VMEM((2, BLOCK, BLOCK), bf16),
            pltpu.VMEM((PAIR, SEQ), f32),
            pltpu.VMEM((PAIR, SEQ), f32),
            pltpu.VMEM((BLOCK, PAIR), f32),
            pltpu.VMEM((SEQ, 3 * PAIR), bf16),
            pltpu.VMEM((SEQ, D), f32),
            pltpu.SemaphoreType.DMA,
            *extra_scratch,
        ],
        compiler_params=compiler,
    )(qe, qkv, qkv, de, qt, dt, low, w4, pix, chan, gone, *extra)


class Sums:
    EARLY = ((0, 3), (0, "ready"), (1, "ready"), (2, "ready"), (3, 3))
    NEXT = ((0, "ready"), (1, 3), (1, "ready"), (2, "ready"), (3, "ready"))

    @staticmethod
    def sizes(ways):
        rows = D // ways
        return [(FF // ways, D), (rows, FF), (rows, D)] + [(rows, 3 * PAIR)] * PAIRS + [(2 * LEVELS // ways, D // 2)]

    @staticmethod
    def scratch(ways):
        sizes = Sums.sizes(ways)
        scratch = [pltpu.VMEM(size, f32) for size in sizes]
        scratch += [pltpu.VMEM((PAIRS, ways, *sizes[3]), bf16), pltpu.VMEM((ways, *sizes[-1]), bf16)]
        scratch += [pltpu.VMEM((ways, EXTRA, 128), f32), pltpu.VMEM((EXTRA, 128), f32)]
        for size in sizes:
            scratch += Reduce.scratch(ways, *size)
        return scratch + ReduceSmall.scratch(ways, EXTRA, 128)

    def __init__(self, ways, given, outs, scratch):
        self.ways, self.outs = ways, outs
        self.place = Place(ways)
        wo, we, ws, self.gvec, self.gbe = given
        scratch = list(scratch)
        take = lambda count: [scratch.pop(0) for _ in range(count)]
        self.results = take(4 + PAIRS)
        self.in_src, self.lev_src = take(2)
        self.small_src, self.small_out = take(2)
        sources = [ws, we, wo, *[self.in_src.at[p] for p in range(PAIRS)], self.lev_src]
        chunks = [Reduce(self.place, s, r, take(5)) for s, r in zip(sources, self.results)]
        self.early, self.pairs, self.lev = chunks[:3], chunks[3:-1], chunks[-1]
        self.small = ReduceSmall(self.place, self.small_src, self.small_out, take(4))

    def point(self, pair, name):
        @pl.when(pair == 0)
        def _():
            if name == "begin":
                self.place.hello()
            if name == 3:
                self.place.greeted()

        for stage, (when, where) in enumerate(self.EARLY):
            if where == name:

                @pl.when(pair == when)
                def _():
                    for chunk in self.early:
                        chunk.stages[stage](chunk)

        for p, chunk in reversed(list(enumerate(self.pairs))):
            for stage, (after, where) in enumerate(self.NEXT):
                if where == name and p + after < PAIRS:

                    @pl.when(pair == p + after)
                    def _():
                        chunk.stages[stage](chunk)

    def take_pair(self, pair, gw):
        self.in_src[pair] = gw.reshape(self.in_src.shape[1:])

    def last(self, channels):
        comb = self.gvec[...] + channels
        self.small_src[...] = jnp.zeros_like(self.small_src)
        for f in range(self.place.n):
            cols = comb[:, f // 2 * 128 : (f // 2 + 1) * 128]
            self.small_src[f, 0:8] = cols if f % 2 == 0 else pltpu.roll(cols, HEAD_DIM, 1)
            for j in range(2):
                at = (f * 2 + j) * 128
                self.small_src[f, 8 + j : 9 + j] = self.gbe[0:1, at : at + 128]
        done = {chunk: sum(p + after < PAIRS for after, _ in self.NEXT) for p, chunk in enumerate(self.pairs)}
        done.update({self.lev: 0, self.small: 0})
        while any(at < len(Reduce.stages) for at in done.values()):
            for chunk, at in reversed(list(done.items())):
                if at < len(Reduce.stages):
                    chunk.stages[at](chunk)
                    done[chunk] = at + 1
        o_out, e_out, s_out, in_out, lev_out, small_out = self.outs
        s_out[...], e_out[...], o_out[...] = [x[...] for x in self.results[:3]]
        for p in range(PAIRS):
            for part in range(3):
                at = (part * PAIRS + p) * PAIR
                in_out[:, at : at + PAIR] = self.results[3 + p][:, part * PAIR : (part + 1) * PAIR]
        half = lev_out.shape[0]
        lev_out[:, : D // 2] = self.results[-1][:half]
        lev_out[:, D // 2 :] = self.results[-1][half:]
        small_out[...] = self.small_out[...]


def place_kernel(o, e, s, win, lev, small, *outs):
    names = ("lev", "chan", "win", "o", "gain1", "bias1", "e", "eb", "s", "sb", "gain2", "bias2")
    to = dict(zip(names, outs))
    for name, ref in (("lev", lev), ("win", win), ("o", o), ("e", e), ("s", s)):
        to[name][...] = ref[...]
    each = to["chan"].shape[1]
    to["chan"][...] = small[5:8, :each]
    for i, name in enumerate(("gain1", "bias1", "sb", "gain2", "bias2")):
        to[name][...] = small[i : i + 1, :each]
    for i in range(2):
        to["eb"][:, i * 128 : (i + 1) * 128] = small[8 + i : 9 + i]


def place_results(ways, o, e, s, win, lev, small):
    each = D // ways
    vec = (1, each)
    shapes = [
        lev.shape, (CHANNELS, each), win.shape, o.shape, vec, vec, e.shape, (1, FF // ways), s.shape, vec, vec, vec,
    ]
    outs = pl.pallas_call(
        place_kernel,
        out_shape=[jax.ShapeDtypeStruct(shape, f32) for shape in shapes],
        compiler_params=params(),
    )(o, e, s, win, lev, small)
    return [x.reshape(-1) if x.shape[0] == 1 else x for x in outs]


def channel_rows():
    pos = np.arange(BLOCK) % CHANNELS + 5
    return (np.arange(EXTRA)[:, None] == pos[None, :]).astype(bf16)


def image(ways, pix, cot, chan, embedded, weights, shards=None):
    emb, low, qkv, qt, vt, sizes = embedded
    w4, wo, vec, be, we, ws = weights
    att, qe, *fetched = attend(ways, qkv, vt, shards)
    if shards is not None:
        we, ws = [x.reshape(-1, x.shape[2]) for x in fetched]
    att, qe = repair(sizes, qkv, vt, att, qe)
    out, gone, de, dt, *grads = middle(att, emb, cot, wo, we, ws, vec, be)
    if shards is not None:
        return out, *back(ways, qe, qkv, de, qt, dt, low, w4, pix, chan, gone, grads)
    return out, *grads, *back(ways, qe, qkv, de, qt, dt, low, w4, pix, chan, gone)


def pack_small(vectors, channels, bias):
    size = bias.shape[0] // 128
    rows = jnp.concatenate([jnp.stack(vectors), channels])
    rows = jnp.pad(rows, ((0, 0), (0, 128 - rows.shape[1])))
    return jnp.concatenate([rows, bias.reshape(size, 128), jnp.zeros((EXTRA - 8 - size, 128), bf16)])


def body(
    ways, pixels, level_table, channel_table, attend_in, attend_out, first_gain, first_bias, expand_weight,
    expand_bias, shrink_weight, shrink_bias, second_gain, second_bias, cotangent,
):
    chan = channel_rows()
    vectors = (first_gain, first_bias, shrink_bias, second_gain, second_bias)
    small = pack_small(vectors, channel_table, expand_bias)
    *embedded, vec, be, w4, wo = embed_gather(ways, pixels, chan, level_table, small, attend_in, attend_out)
    weights = (w4.reshape(3, PAIRS, D, PAIR), wo.reshape(D, D), vec, be, None, None)
    shards = (expand_weight, shrink_weight)
    out, *sums = image(ways, pixels, cotangent[0], chan, embedded, weights, shards)
    return out[None], *place_results(ways, *sums)


def plain_body(
    ways, pixels, level_table, channel_table, attend_in, attend_out, first_gain, first_bias, expand_weight,
    expand_bias, shrink_weight, shrink_bias, second_gain, second_bias, cotangent,
):
    gather = lambda x, axis=0: lax.all_gather(x, "fsdp", axis=axis, tiled=True)
    vectors = jnp.stack((first_gain, first_bias, shrink_bias, second_gain, second_bias))
    chan = channel_rows()
    small = gather(jnp.concatenate([vectors, channel_table]), 1)
    table = jnp.pad(small, ((0, EXTRA - 8), (0, 0)))
    level = gather(level_table)
    w_in = gather(attend_in)
    be = jnp.pad(gather(expand_bias).astype(f32)[None], ((0, 7), (0, 0)))
    w4 = w_in.reshape(D, 3, PAIRS, PAIR).transpose(1, 2, 0, 3)
    weights = (w4, gather(attend_out), table.astype(f32), be, gather(expand_weight), gather(shrink_weight))
    outs = []
    sums = None
    for i in range(pixels.shape[0]):
        pix = pixels[i : i + 1]
        got = image(ways, pix, cotangent[i], chan, embed_plain(pix, chan, level, table, w_in), weights)
        outs.append(got[0])
        grads = [x.astype(f32) for x in got[1:]]
        sums = grads if sums is None else [a + b for a, b in zip(sums, grads)]
    gwo, gwe, gws, gvec, gbe, gw, glev, gchan = sums
    gwin = gw.reshape(PAIRS, D, 3, PAIR).transpose(1, 2, 0, 3).reshape(D, 3 * D)
    count = LEVELS // ways
    glev = glev.reshape(ways, 2, count, D // 2).transpose(0, 2, 1, 3).reshape(LEVELS, D)

    def scatter(x, axis=0):
        return lax.psum(lax.psum_scatter(x, "fsdp", scatter_dimension=axis, tiled=True), "dp")

    small = scatter(gvec + gchan[:8], 1)
    return (
        jnp.stack(outs), scatter(glev), small[5:8], scatter(gwin), scatter(gwo), small[0], small[1], scatter(gwe),
        scatter(gbe[0]), scatter(gws), small[2], small[3], small[4],
    )


def solution(mesh):
    row = P("fsdp", None)
    vector = P("fsdp")
    shared = P(("fsdp", "dp"), None, None)
    weights = (
        row, P(None, "fsdp"), row, row, vector, vector, row, vector, row, vector, vector, vector,
    )
    ways = mesh.shape["fsdp"]
    fits = ways == 8 and mesh.shape["dp"] == 4

    def program(pixels, *rest):
        return (body if fits and pixels.shape[0] == 1 else plain_body)(ways, pixels, *rest)

    return jax.shard_map(
        program,
        mesh=mesh,
        in_specs=(P(("fsdp", "dp"), None), *weights, shared),
        out_specs=(shared, *weights),
        check_vma=False,
    )
```

```python
import functools

import jax
import jax.numpy as jnp
import numpy as np
from jax import lax
from jax.experimental import pallas as pl
from jax.experimental.pallas import tpu as pltpu
from jax.sharding import PartitionSpec as P

D = 512
HEADS = 8
HEAD_DIM = 64
FF = 2048
LEVELS = 256
CHANNELS = 3
SEQ = 3072
BLOCK = 768
BANDS = SEQ // BLOCK
PAIRS = HEADS // 2
PAIR = 2 * HEAD_DIM
REACH = 2
SUB = 256
EXTRA = 16
EPS = 1e-6
LOG2E = 1.4426950408889634
SAFE = 60.0

f32 = jnp.float32
bf16 = jnp.bfloat16
NT = (((1,), (1,)), ((), ()))
TN = (((0,), (0,)), ((), ()))
VMEM_LIMIT = 60 * 2**20


def mm(a, b):
    return jnp.dot(a, b, preferred_element_type=f32)


def mm_nt(a, b):
    return lax.dot_general(a, b, NT, preferred_element_type=f32)


def mm_tn(a, b):
    return lax.dot_general(a, b, TN, preferred_element_type=f32)


def params(*semantics):
    return pltpu.CompilerParams(
        vmem_limit_bytes=VMEM_LIMIT, dimension_semantics=semantics or None
    )


def one_hot_rows(pix):
    width = pix.shape[1]
    return (lax.broadcasted_iota(jnp.int32, (LEVELS, width), 0) == pix).astype(bf16)


def split3(x):
    hi = x.astype(bf16).astype(f32)
    rest = x - hi
    mid = rest.astype(bf16).astype(f32)
    return hi, mid, rest - mid


class Place:
    def __init__(self, ways):
        self.n = ways
        self.f = lax.axis_index("fsdp")
        self.d = lax.axis_index("dp")
        self.core = self.d % 2
        self.side = self.d // 2
        self.quarter = self.core * 2 + self.side

    def at(self, step):
        return (self.f + step) % self.n

    def to(self, step):
        return {"fsdp": self.at(step), "dp": self.d}

    def to_core(self):
        return {"fsdp": self.f, "dp": self.d + 1 - 2 * self.core}

    def to_side(self):
        return {"fsdp": self.f, "dp": self.d + 2 - 4 * self.side}

    def to_cross(self):
        return {"fsdp": self.f, "dp": 3 - self.d}

    def mates(self):
        return [self.to_core(), self.to_side(), self.to_cross()] + [self.to(step) for step in range(1, self.n)]

    def hello(self):
        barrier = pltpu.get_barrier_semaphore()
        for mate in self.mates():
            pl.semaphore_signal(barrier, inc=1, device_id=mate, device_id_type=pl.DeviceIdType.MESH)

    def greeted(self):
        pl.semaphore_wait(pltpu.get_barrier_semaphore(), self.n + 2)


def send(src, dst, sems, i, device):
    return pltpu.make_async_remote_copy(
        src_ref=src,
        dst_ref=dst,
        send_sem=sems.at[0, i],
        recv_sem=sems.at[1, i],
        device_id=device,
        device_id_type=pl.DeviceIdType.MESH,
    )


def window(which, size, count=1):
    return pl.ds(pl.multiple_of(which * size, size), size * count)


class Gather:
    def __init__(self, place, src, dst, sems, across):
        self.place, self.src, self.dst, self.sems = place, src, dst, sems
        self.across, self.n = across, place.n

    @staticmethod
    def semaphores(ways):
        return pltpu.SemaphoreType.DMA((2, 3 * ways + 1))

    def part(self, ref, f, start, count):
        if self.across is None:
            return ref.at[f]
        cut = window(start, self.dst.shape[1 + self.across] // 4, count)
        return ref.at[f, cut] if self.across == 0 else ref.at[f, :, cut]

    def mine(self):
        return self.part(self.dst, self.place.f, self.place.quarter, 1)

    def source(self):
        return self.part(self.src, 0, self.place.quarter, 1)

    def local(self):
        return pltpu.make_async_copy(self.source(), self.mine(), self.sems.at[0, 3 * self.n])

    def copy(self, step):
        return send(self.source(), self.mine(), self.sems, step, self.place.to(step))

    def side_copy(self, step):
        got = self.part(self.dst, self.place.at(self.n - step), self.place.quarter, 1)
        return send(got, got, self.sems, self.n + step, self.place.to_side())

    def core_copy(self, step):
        got = self.part(self.dst, self.place.at(self.n - step), self.place.core * 2, 2)
        return send(got, got, self.sems, 2 * self.n + step, self.place.to_core())

    def start(self):
        self.local().start()
        for step in range(1, self.n):
            self.copy(step).start()

    def swap(self, step):
        if step:
            self.copy(step).wait()
        else:
            self.local().wait()
        if self.across is not None:
            self.side_copy(step).start()

    def share(self, step):
        if self.across is not None:
            self.side_copy(step).wait()
            self.core_copy(step).start()

    def finish(self):
        if self.across is not None:
            for step in range(self.n):
                self.core_copy(step).wait()


class Reduce:
    def __init__(self, place, src, out, bufs):
        self.place, self.src, self.out, self.n = place, src, out, place.n
        self.r1, self.a1, self.r2, self.r3, self.sems = bufs
        self.size = src.shape[1] // 4

    @staticmethod
    def scratch(ways, rows, cols):
        return [
            pltpu.VMEM((ways, rows // 2, cols), bf16),
            pltpu.VMEM((ways, rows // 2, cols), bf16),
            pltpu.VMEM((ways, rows // 4, cols), bf16),
            pltpu.VMEM((ways - 1, rows // 4, cols), bf16),
            pltpu.SemaphoreType.DMA((2, ways + 5)),
        ]

    def half(self, which):
        return self.src.at[:, window(which, 2 * self.size)]

    def local(self):
        return pltpu.make_async_copy(self.half(self.place.core), self.a1, self.sems.at[0, self.n + 4])

    def core_copy(self):
        return send(self.half(1 - self.place.core), self.r1, self.sems, 0, self.place.to_core())

    def side_copy(self):
        theirs = self.a1.at[:, window(1 - self.place.side, self.size)]
        return send(theirs, self.r2, self.sems, self.n, self.place.to_side())

    def copy(self, step):
        return send(self.r2.at[self.place.at(step)], self.r3.at[step - 1], self.sems, step, self.place.to(step))

    def backs(self):
        got = self.out.at[window(self.place.quarter, self.size)]
        mates = (self.place.to_core(), self.place.to_side(), self.place.to_cross())
        return [send(got, got, self.sems, self.n + 1 + i, mate) for i, mate in enumerate(mates)]

    def start(self):
        self.core_copy().start()
        self.local().start()

    def over_sides(self):
        self.local().wait()
        self.core_copy().wait()

        @pl.loop(0, self.n)
        def _(i):
            self.a1[i] = (self.a1[i].astype(f32) + self.r1[i].astype(f32)).astype(bf16)

        self.side_copy().start()

    def over_shards(self):
        self.side_copy().wait()
        cut = window(self.place.side, self.size)

        @pl.loop(0, self.n)
        def _(i):
            self.r2[i] = (self.a1[i, cut].astype(f32) + self.r2[i].astype(f32)).astype(bf16)

        for step in range(1, self.n):
            self.copy(step).start()

    def settle(self):
        for step in range(1, self.n):
            self.copy(step).wait()
        whole = self.r2[self.place.f].astype(f32)
        for step in range(1, self.n):
            whole = whole + self.r3[step - 1].astype(f32)
        self.out[window(self.place.quarter, self.size)] = whole
        for back in self.backs():
            back.start()

    def finish(self):
        for back in self.backs():
            back.wait()

    stages = (start, over_sides, over_shards, settle, finish)


class ReduceSmall:
    def __init__(self, place, src, out, bufs):
        self.place, self.src, self.out, self.n = place, src, out, place.n
        self.r1, self.r2, self.r3, self.sems = bufs

    @staticmethod
    def scratch(ways, rows, cols):
        return [
            pltpu.VMEM((ways, rows, cols), f32),
            pltpu.VMEM((ways, rows, cols), f32),
            pltpu.VMEM((ways - 1, rows, cols), f32),
            pltpu.SemaphoreType.DMA((2, ways + 1)),
        ]

    def core_copy(self):
        return send(self.src, self.r1, self.sems, 0, self.place.to_core())

    def side_copy(self):
        return send(self.src, self.r2, self.sems, self.n, self.place.to_side())

    def copy(self, step):
        return send(self.src.at[self.place.at(step)], self.r3.at[step - 1], self.sems, step, self.place.to(step))

    def start(self):
        self.core_copy().start()

    def over_sides(self):
        self.core_copy().wait()
        self.src[...] += self.r1[...]
        self.side_copy().start()

    def over_shards(self):
        self.side_copy().wait()
        self.src[...] += self.r2[...]
        for step in range(1, self.n):
            self.copy(step).start()

    def settle(self):
        for step in range(1, self.n):
            self.copy(step).wait()
        whole = self.src[self.place.f]
        for step in range(1, self.n):
            whole = whole + self.r3[step - 1]
        self.out[...] = whole

    def finish(self):
        pass

    stages = (start, over_sides, over_shards, settle, finish)


def embed_tile(step, pix_ref, chan_ref, level, table, w, ind_ref, emb_ref, low_ref, qkv_ref, qt_ref, vt_ref, norm_ref):
    emb = mm_tn(one_hot_rows(pix_ref[...]), level) + mm_tn(chan_ref[...], table)
    emb_ref[...] = emb
    low = emb.astype(bf16)
    low_ref[...] = low
    qkv = mm(low, w)
    q = (qkv[:, :D] * HEAD_DIM**-0.5).astype(bf16)
    k = qkv[:, D : 2 * D].astype(bf16)
    v = qkv[:, 2 * D :].astype(bf16)
    qkv_ref[:, :D] = q
    qkv_ref[:, D : 2 * D] = k
    qkv_ref[:, 2 * D :] = v
    qt_ref[...] = q.T
    vt_ref[...] = v.T
    q = q.astype(f32)
    k = k.astype(f32)
    size_q = mm((q * q).astype(bf16), ind_ref[...]).max(0, keepdims=True)
    size_k = mm((k * k).astype(bf16), ind_ref[...]).max(0, keepdims=True)
    row = lax.broadcasted_iota(jnp.int32, (8, 128), 0)
    both = jnp.where(row == 0, size_q, jnp.where(row == 1, size_k, 0.0))
    norm_ref[...] = jnp.maximum(both, jnp.where(step == 0, 0.0, norm_ref[...]))


def embed_plain_kernel(pix_ref, chan_ref, level_ref, table_ref, w_ref, ind_ref, *outs):
    embed_tile(pl.program_id(0), pix_ref, chan_ref, level_ref[...], table_ref[...], w_ref[...], ind_ref, *outs)


def embed_outs():
    rows = lambda i: (i, 0)
    cols = lambda i: (0, i)
    specs = [
        pl.BlockSpec((BLOCK, D), rows),
        pl.BlockSpec((BLOCK, D), rows),
        pl.BlockSpec((BLOCK, 3 * D), rows),
        pl.BlockSpec((D, BLOCK), cols),
        pl.BlockSpec((D, BLOCK), cols),
        pl.BlockSpec((8, 128), lambda i: (0, 0)),
    ]
    shapes = [
        jax.ShapeDtypeStruct((SEQ, D), f32),
        jax.ShapeDtypeStruct((SEQ, D), bf16),
        jax.ShapeDtypeStruct((SEQ, 3 * D), bf16),
        jax.ShapeDtypeStruct((D, SEQ), bf16),
        jax.ShapeDtypeStruct((D, SEQ), bf16),
        jax.ShapeDtypeStruct((8, 128), f32),
    ]
    return specs, shapes


def head_columns():
    return (np.arange(D)[:, None] // HEAD_DIM == np.arange(128)[None, :]).astype(bf16)


def embed_plain(pix, chan, level, table, w_in):
    whole = lambda i: (0, 0)
    specs, shapes = embed_outs()
    return pl.pallas_call(
        embed_plain_kernel,
        grid=(SEQ // BLOCK,),
        in_specs=[
            pl.BlockSpec((1, BLOCK), lambda i: (0, i)),
            pl.BlockSpec((EXTRA, BLOCK), whole),
            pl.BlockSpec((LEVELS, D), whole),
            pl.BlockSpec((EXTRA, D), whole),
            pl.BlockSpec((D, 3 * D), whole),
            pl.BlockSpec((D, 128), whole),
        ],
        out_specs=specs,
        out_shape=shapes,
        compiler_params=params("arbitrary"),
    )(pix, chan, level, table, w_in, head_columns())


def half_lanes(even, odd):
    lane = lax.broadcasted_iota(jnp.int32, even.shape, 1)
    return jnp.where(lane < HEAD_DIM, even, pltpu.roll(odd, HEAD_DIM, 1))


def embed_gather_kernel(
    ways, pix_ref, chan_ref, ind_ref, level_ref, small_ref, win_ref, wo_ref,
    emb_ref, low_ref, qkv_ref, qt_ref, vt_ref, norm_ref, vec_ref, be_ref, w4_ref, wo_out,
    level_s, small_s, win_s, sem_level, sem_small, sem_in, sem_o, sem_w4,
):
    step = pl.program_id(0)
    last = SEQ // BLOCK - 1
    place = Place(ways)
    first = [
        Gather(place, small_ref, small_s, sem_small, None),
        Gather(place, level_ref, level_s, sem_level, 1),
        Gather(place, win_ref, win_s, sem_in, 0),
    ]
    later = Gather(place, wo_ref, wo_out, sem_o, 0)

    def copies():
        for i in range(3 * PAIRS):
            yield pltpu.make_async_copy(win_s.at[:, :, i * PAIR : (i + 1) * PAIR], w4_ref.at[i], sem_w4.at[i])

    @pl.when(step == 0)
    def _():
        place.hello()
        place.greeted()
        for g in (*first, later):
            g.start()
        for i in range(ways):
            for g in first:
                g.swap(i)
        for i in range(ways):
            for g in first:
                g.share(i)
        for i in range(ways // 2):
            both = [small_s[2 * i + odd].astype(f32) for odd in range(2)]
            vec_ref[:, i * 128 : (i + 1) * 128] = half_lanes(*both)
            for odd in range(2):
                for j in range(2):
                    at = ((2 * i + odd) * 2 + j) * 128
                    be_ref[0:1, at : at + 128] = both[odd][8 + j : 9 + j]
        for g in first:
            g.finish()
        for copy in copies():
            copy.start()

    table = vec_ref[...].astype(bf16)
    level = level_s[...].reshape(LEVELS, D)
    w = win_s[...].reshape(D, 3 * D)
    embed_tile(step, pix_ref, chan_ref, level, table, w, ind_ref, emb_ref, low_ref, qkv_ref, qt_ref, vt_ref, norm_ref)

    @pl.when(step == 0)
    def _():
        for i in range(ways):
            later.swap(i)

    @pl.when(step == last - 1)
    def _():
        for i in range(ways):
            later.share(i)

    @pl.when(step == last)
    def _():
        for copy in copies():
            copy.wait()
        later.finish()


def embed_gather(ways, pix, chan, level, small, w_in, wo):
    whole = lambda i: (0, 0)
    anywhere = pl.BlockSpec(memory_space=pl.ANY)
    specs, shapes = embed_outs()
    shards = [x[None] for x in (level, small, w_in, wo)]
    return pl.pallas_call(
        functools.partial(embed_gather_kernel, ways),
        grid=(SEQ // BLOCK,),
        in_specs=[
            pl.BlockSpec((1, BLOCK), lambda i: (0, i)),
            pl.BlockSpec((EXTRA, BLOCK), whole),
            pl.BlockSpec((D, 128), whole),
            *[anywhere] * 4,
        ],
        out_specs=[*specs, pl.BlockSpec((EXTRA, D), whole), pl.BlockSpec((8, FF), whole), *[anywhere] * 2],
        out_shape=[
            *shapes,
            jax.ShapeDtypeStruct((EXTRA, D), f32),
            jax.ShapeDtypeStruct((8, FF), f32),
            jax.ShapeDtypeStruct((3 * PAIRS, ways, D // ways, PAIR), bf16),
            jax.ShapeDtypeStruct((ways, *wo.shape), bf16),
        ],
        scratch_shapes=[
            *[pltpu.VMEM((ways, *x.shape), bf16) for x in (level, small, w_in)],
            *[Gather.semaphores(ways)] * 4,
            pltpu.SemaphoreType.DMA((3 * PAIRS,)),
        ],
        compiler_params=pltpu.CompilerParams(
            vmem_limit_bytes=VMEM_LIMIT, dimension_semantics=("arbitrary",), collective_id=0, has_side_effects=True
        ),
    )(pix, chan, head_columns(), *shards)


def units():
    found = []
    for band in range(BANDS):
        found += [(band, j) for j in range(max(0, band - REACH), band + 1)]
    return found


def lower_mask(keys, queries):
    key = lax.broadcasted_iota(jnp.int32, (keys, queries), 0)
    return key <= lax.broadcasted_iota(jnp.int32, (keys, queries), 1)


def spare_rows(x):
    row = lax.broadcasted_iota(jnp.int32, (HEAD_DIM, x.shape[1]), 0)
    hi, mid, low = split3(x)
    return jnp.where(row == 0, hi, jnp.where(row == 1, mid, jnp.where(row == 2, low, 0.0)))


class Fetch:
    def __init__(self, ways, sources, outs, sems):
        self.place = Place(ways)
        self.wide, self.narrow = [Gather(self.place, s, o, m, 0) for s, o, m in zip(sources, outs, sems)]

    def point(self, pair, name):
        half = self.place.n // 2
        steps_of = lambda method, parts: [functools.partial(method, i) for i in parts]
        near, far = range(half), range(half, self.place.n)
        wide, narrow = self.wide, self.narrow
        plan = {
            (0, 0): [self.place.hello],
            (0, 5): [self.place.greeted, wide.start, narrow.start],
            (0, 9): [functools.partial(wide.swap, 0), functools.partial(narrow.swap, 0)],
            (1, 5): steps_of(wide.swap, near[1:]),
            (1, 9): steps_of(wide.swap, far),
            (2, 5): steps_of(narrow.swap, near[1:]),
            (2, 9): steps_of(narrow.swap, far) + steps_of(wide.share, near),
            (3, 5): steps_of(wide.share, far) + steps_of(narrow.share, near),
            (3, 9): steps_of(narrow.share, far) + [wide.finish, narrow.finish],
        }
        for (when, where), steps in plan.items():
            if where == name:

                @pl.when(pair == when)
                def _():
                    for step in steps:
                        step()


def attend_kernel(ways, linked, *refs):
    q_ref, k_ref, vt_ref, *refs = refs
    sources, refs = (refs[:2], refs[2:]) if linked else (None, refs)
    o_ref, qe_ref, *refs = refs
    outs, refs = (refs[:2], refs[2:]) if linked else (None, refs)
    acc, lsum, probs, *sems = refs
    pair = pl.program_id(0)
    fetch = Fetch(ways, sources, outs, sems) if linked else None
    lane = lax.broadcasted_iota(jnp.int32, (BLOCK, PAIR), 1)

    def head_only(q, h, other):
        mine = (lane < HEAD_DIM) if h == 0 else (lane >= HEAD_DIM)
        return jnp.where(mine, q, other)

    for unit, (band, j) in enumerate(units()):
        if linked:
            fetch.point(pair, unit)
        here = slice(band * BLOCK, (band + 1) * BLOCK)
        first = j == max(0, band - REACH)
        q = q_ref[here, :]
        off = jnp.zeros_like(q)
        tiles = [(0, BLOCK, BLOCK)] if j < band else [(t * SUB, SUB, (t + 1) * SUB) for t in range(BLOCK // SUB)]
        for h in range(2):
            qm = head_only(q, h, off)
            for at, width, count in tiles:
                ts = slice(at, at + width)
                scores = mm_nt(k_ref[j * BLOCK : j * BLOCK + count, :], qm[ts])
                p = jnp.exp2(scores * LOG2E)
                if j == band:
                    diag = jnp.where(lower_mask(SUB, SUB), p[count - SUB :], 0.0)
                    p = diag if count == SUB else jnp.concatenate([p[: count - SUB], diag], 0)
                part = p.reshape(count // 8, 8, width).sum(0)
                if not first:
                    part += lsum[h, :, ts]
                lsum[h, :, ts] = part
                probs[h, :count, ts] = p.astype(bf16)
        ext = [None, None]
        for h in range(2):
            mine = slice(h * HEAD_DIM, (h + 1) * HEAD_DIM)
            for at, width, count in tiles:
                ts = slice(at, at + width)
                out = mm(vt_ref[mine, j * BLOCK : j * BLOCK + count], probs[h, :count, ts])
                if not first:
                    out += acc[mine, ts]
                acc[mine, ts] = out
            if j == band:
                whole = lsum[h].sum(0, keepdims=True)
                acc[mine, :] = acc[mine, :] / whole
                ext[1 - h] = spare_rows(-jnp.log(whole))
        if j == band:
            o_ref[here, :] = acc[...].T.astype(bf16)
            extra = jnp.concatenate(ext, 0).T.astype(bf16)
            qe_ref[here, :PAIR] = head_only(q, 0, extra)
            qe_ref[here, PAIR:] = head_only(q, 1, extra)
    if linked:
        fetch.point(pair, len(units()))


def attend(ways, qkv, vt, shards=None):
    linked = shards is not None
    anywhere = pl.BlockSpec(memory_space=pl.ANY)
    extra, outs, sems, compiler = [], [], [], params("arbitrary")
    if linked:
        extra = [x[None] for x in shards]
        outs = [jax.ShapeDtypeStruct((ways, *x.shape), bf16) for x in shards]
        sems = [Gather.semaphores(ways)] * 2
        compiler = pltpu.CompilerParams(
            vmem_limit_bytes=VMEM_LIMIT, dimension_semantics=("arbitrary",), collective_id=2, has_side_effects=True
        )
    return pl.pallas_call(
        functools.partial(attend_kernel, ways, linked),
        grid=(PAIRS,),
        in_specs=[
            pl.BlockSpec((SEQ, PAIR), lambda p: (0, p)),
            pl.BlockSpec((SEQ, PAIR), lambda p: (0, PAIRS + p)),
            pl.BlockSpec((PAIR, SEQ), lambda p: (p, 0)),
            *[anywhere] * len(extra),
        ],
        out_specs=[
            pl.BlockSpec((SEQ, PAIR), lambda p: (0, p)),
            pl.BlockSpec((SEQ, 2 * PAIR), lambda p: (0, p)),
            *[anywhere] * len(extra),
        ],
        out_shape=[
            jax.ShapeDtypeStruct((SEQ, D), bf16),
            jax.ShapeDtypeStruct((SEQ, 2 * D), bf16),
            *outs,
        ],
        scratch_shapes=[
            pltpu.VMEM((PAIR, BLOCK), f32),
            pltpu.VMEM((2, 8, BLOCK), f32),
            pltpu.VMEM((2, BLOCK, BLOCK), bf16),
            *sems,
        ],
        compiler_params=compiler,
    )(qkv, qkv, vt, *extra)


def repair_kernel(
    norm_ref, qkv_ref, vt_ref, _att, _qe, att_ref, qe_ref, q_s, k_s, vt_s, o_s, e_s, acc, top, lsum, sems
):
    bound = jnp.max(norm_ref[0:1] * norm_ref[1:2])

    @pl.when(jnp.logical_not(bound < SAFE * SAFE))
    def _():
        lane = lax.broadcasted_iota(jnp.int32, (BLOCK, PAIR), 1)
        chunk = 128

        @pl.loop(0, PAIRS)
        def _(pair):
            at = pl.multiple_of(pair * PAIR, PAIR)
            loads = [
                pltpu.make_async_copy(qkv_ref.at[:, pl.ds(at, PAIR)], q_s, sems.at[0]),
                pltpu.make_async_copy(qkv_ref.at[:, pl.ds(pl.multiple_of(at + D, PAIR), PAIR)], k_s, sems.at[1]),
                pltpu.make_async_copy(vt_ref.at[pl.ds(at, PAIR)], vt_s, sems.at[2]),
            ]
            for load in loads:
                load.start()
            for load in loads:
                load.wait()

            @pl.loop(0, BANDS)
            def _(band):
                here = pl.ds(pl.multiple_of(band * BLOCK, BLOCK), BLOCK)
                q = q_s[here, :]
                ext = [None, None]
                begin = jnp.maximum(band - REACH, 0) * (BLOCK // chunk)
                end = (band + 1) * (BLOCK // chunk)
                for h in range(2):
                    mine = slice(h * HEAD_DIM, (h + 1) * HEAD_DIM)
                    qm = jnp.where((lane < HEAD_DIM) if h == 0 else (lane >= HEAD_DIM), q, jnp.zeros_like(q))

                    def masked(i):
                        start = pl.multiple_of(i * chunk, chunk)
                        scores = mm_nt(k_s[pl.ds(start, chunk), :], qm)
                        key = lax.broadcasted_iota(jnp.int32, scores.shape, 0) + start
                        query = lax.broadcasted_iota(jnp.int32, scores.shape, 1) + band * BLOCK
                        return start, jnp.where(key <= query, scores, -1e30)

                    top[...] = jnp.full(top.shape, -1e30, f32)
                    lsum[...] = jnp.zeros_like(lsum)
                    acc[mine] = jnp.zeros((HEAD_DIM, BLOCK), f32)

                    @pl.loop(begin, end)
                    def _(i):
                        top[...] = jnp.maximum(top[...], masked(i)[1].max(0, keepdims=True))

                    @pl.loop(begin, end)
                    def _(i):
                        start, scores = masked(i)
                        p = jnp.exp2((scores - top[0:1]) * LOG2E)
                        lsum[...] += p.reshape(chunk // 8, 8, BLOCK).sum(0)
                        acc[mine] += mm(vt_s[mine, pl.ds(start, chunk)], p.astype(bf16))

                    whole = lsum[...].sum(0, keepdims=True)
                    acc[mine] = acc[mine] / whole
                    ext[1 - h] = spare_rows(-(top[0:1] + jnp.log(whole)))
                o_s[here, :] = acc[...].T.astype(bf16)
                extra = jnp.concatenate(ext, 0).T.astype(bf16)
                e_s[here, :PAIR] = jnp.where(lane < HEAD_DIM, q, extra)
                e_s[here, PAIR:] = jnp.where(lane < HEAD_DIM, extra, q)

            stores = [
                pltpu.make_async_copy(o_s, att_ref.at[:, pl.ds(at, PAIR)], sems.at[0]),
                pltpu.make_async_copy(
                    e_s, qe_ref.at[:, pl.ds(pl.multiple_of(2 * at, 2 * PAIR), 2 * PAIR)], sems.at[1]
                ),
            ]
            for store in stores:
                store.start()
            for store in stores:
                store.wait()


def repair(sizes, qkv, vt, att, qe):
    anywhere = pl.BlockSpec(memory_space=pl.ANY)
    return pl.pallas_call(
        repair_kernel,
        in_specs=[pl.BlockSpec(memory_space=pltpu.VMEM), *[anywhere] * 4],
        out_specs=[anywhere] * 2,
        out_shape=[jax.ShapeDtypeStruct(x.shape, x.dtype) for x in (att, qe)],
        scratch_shapes=[
            pltpu.VMEM((SEQ, PAIR), bf16),
            pltpu.VMEM((SEQ, PAIR), bf16),
            pltpu.VMEM((PAIR, SEQ), bf16),
            pltpu.VMEM((SEQ, PAIR), bf16),
            pltpu.VMEM((SEQ, 2 * PAIR), bf16),
            pltpu.VMEM((PAIR, BLOCK), f32),
            pltpu.VMEM((8, BLOCK), f32),
            pltpu.VMEM((8, BLOCK), f32),
            pltpu.SemaphoreType.DMA((3,)),
        ],
        input_output_aliases={3: 0, 4: 1},
        compiler_params=params(),
    )(sizes, qkv, vt, att, qe)


def mean(x):
    return jnp.mean(x, -1, keepdims=True)


def norm(x):
    centered = x - mean(x)
    factor = lax.rsqrt(mean(centered * centered) + EPS)
    return centered * factor, factor


def norm_back(scaled, normed, factor):
    return factor * (scaled - mean(scaled) - normed * mean(scaled * normed))


def total(x):
    return x.sum(0, keepdims=True)


def middle_kernel(
    att_ref, emb_ref, cot_ref, wo_ref, we_ref, ws_ref, vec_ref, be_ref, pick_ref,
    out_ref, go_ref, de_ref, dt_ref, gwo_out, gwe_out, gws_out, gvec_ref, gbe_ref, gwo_ref, gwe_ref, gws_ref,
):
    @pl.when(pl.program_id(0) == 0)
    def _():
        for ref in (gwo_ref, gwe_ref, gws_ref, gvec_ref, gbe_ref):
            ref[...] = jnp.zeros_like(ref)

    gain1, bias1, bs, gain2, bias2 = [vec_ref[i : i + 1, :] for i in range(5)]
    att = att_ref[...]
    cot = cot_ref[...]
    normed1, factor1 = norm(emb_ref[...] + mm(att, wo_ref[...]))
    hidden = normed1 * gain1 + bias1
    low = hidden.astype(bf16)
    preact = mm(low, we_ref[...]) + be_ref[0:1, :]
    sig = jax.nn.sigmoid(preact)
    activ = (preact * sig).astype(bf16)
    slope = sig * (1.0 + preact * (1.0 - sig))
    normed2, factor2 = norm(hidden + mm(activ, ws_ref[...]) + bs)
    out_ref[...] = (normed2 * gain2 + bias2).astype(bf16)
    gtwo = norm_back(cot * gain2, normed2, factor2)
    gbranch = gtwo.astype(bf16)
    gws_ref[...] += mm_tn(activ, gbranch)
    gpre = (mm_nt(gbranch, ws_ref[...]) * slope).astype(bf16)
    gbe_ref[0:1, :] += total(gpre.astype(f32))
    gwe_ref[...] += mm_tn(low, gpre)
    ghidden = gtwo + mm_nt(gpre, we_ref[...])
    gone = norm_back(ghidden * gain1, normed1, factor1)
    go_ref[...] = gone
    gatt_branch = gone.astype(bf16)
    gwo_ref[...] += mm_tn(att, gatt_branch)
    gatt = mm_nt(gatt_branch, wo_ref[...]).astype(bf16)
    dt_ref[...] = gatt.T
    gvec_ref[0:1, :] += total(ghidden * normed1)
    gvec_ref[1:2, :] += total(ghidden)
    gvec_ref[2:3, :] += total(gbranch.astype(f32))
    gvec_ref[3:4, :] += total(cot * normed2)
    gvec_ref[4:5, :] += total(cot)

    @pl.when(pl.program_id(0) == pl.num_programs(0) - 1)
    def _():
        gwo_out[...] = gwo_ref[...].astype(bf16)
        gwe_out[...] = gwe_ref[...].astype(bf16)
        gws_out[...] = gws_ref[...].astype(bf16)

    prod = gatt.astype(f32) * att.astype(f32)
    hi, mid, _ = split3(prod)
    pick = pick_ref[...]
    half = D // 2
    place = lax.broadcasted_iota(jnp.int32, (att.shape[0], half), 1) % HEAD_DIM
    lane = lax.broadcasted_iota(jnp.int32, (att.shape[0], PAIR), 1)
    for part in range(2):
        cols = slice(part * half, (part + 1) * half)
        inner = mm(hi[:, cols].astype(bf16), pick) + mm(mid[:, cols].astype(bf16), pick)
        a, b, c = split3(inner)
        ext = jnp.where(place == 0, a, jnp.where(place == 1, b, jnp.where(place == 2, c, 0.0))).astype(bf16)
        for i in range(2):
            pair = 2 * part + i
            e = ext[:, i * PAIR : (i + 1) * PAIR]
            d = gatt[:, pair * PAIR : (pair + 1) * PAIR]
            de_ref[:, 2 * pair * PAIR : (2 * pair + 1) * PAIR] = jnp.where(lane < HEAD_DIM, d, e)
            de_ref[:, (2 * pair + 1) * PAIR : (2 * pair + 2) * PAIR] = jnp.where(lane < HEAD_DIM, e, d)


def middle(att, emb, cot, wo, we, ws, vec, be):
    tile = 768
    half = D // 2
    src = np.arange(half)[:, None] // HEAD_DIM
    dst = np.arange(half)[None, :]
    other = (dst // HEAD_DIM) ^ 1
    pick = np.where((src == other) & (dst % HEAD_DIM < 3), -1.0, 0.0).astype(bf16)
    whole = lambda i: (0, 0)
    rows = lambda i: (i, 0)
    cols = lambda i: (0, i)
    one = pl.Buffered(1)
    return pl.pallas_call(
        middle_kernel,
        grid=(SEQ // tile,),
        in_specs=[
            pl.BlockSpec((tile, D), rows),
            pl.BlockSpec((tile, D), rows),
            pl.BlockSpec((tile, D), rows),
            pl.BlockSpec((D, D), whole, pipeline_mode=one),
            pl.BlockSpec((D, FF), whole, pipeline_mode=one),
            pl.BlockSpec((FF, D), whole, pipeline_mode=one),
            pl.BlockSpec((EXTRA, D), whole),
            pl.BlockSpec((8, FF), whole),
            pl.BlockSpec((half, half), whole),
        ],
        out_specs=[
            pl.BlockSpec((tile, D), rows),
            pl.BlockSpec((tile, D), rows),
            pl.BlockSpec((tile, 2 * D), rows),
            pl.BlockSpec((D, tile), cols),
            pl.BlockSpec((D, D), whole, pipeline_mode=one),
            pl.BlockSpec((D, FF), whole, pipeline_mode=one),
            pl.BlockSpec((FF, D), whole, pipeline_mode=one),
            pl.BlockSpec((8, D), whole),
            pl.BlockSpec((8, FF), whole),
        ],
        out_shape=[
            jax.ShapeDtypeStruct((SEQ, D), bf16),
            jax.ShapeDtypeStruct((SEQ, D), f32),
            jax.ShapeDtypeStruct((SEQ, 2 * D), bf16),
            jax.ShapeDtypeStruct((D, SEQ), bf16),
            jax.ShapeDtypeStruct((D, D), bf16),
            jax.ShapeDtypeStruct((D, FF), bf16),
            jax.ShapeDtypeStruct((FF, D), bf16),
            jax.ShapeDtypeStruct((8, D), f32),
            jax.ShapeDtypeStruct((8, FF), f32),
        ],
        scratch_shapes=[pltpu.VMEM((D, D), f32), pltpu.VMEM((D, FF), f32), pltpu.VMEM((FF, D), f32)],
        compiler_params=params("arbitrary"),
    )(att, emb, cot, wo, we, ws, vec, be, pick)


def back_kernel(ways, linked, *refs):
    refs = list(refs)
    take = lambda count: [refs.pop(0) for _ in range(count)]
    qe_ref, k_ref, v_ref, de_ref, qt_ref, dt_ref, low_ref, w_ref, pix_ref, chan_ref, go_ref = take(11)
    given = take(5) if linked else None
    outs = take(6 if linked else 3)
    ke, ve, km, probs, slopes, dkt, dvt, dqa, grads, gemb, sem = take(11)
    pair = pl.program_id(0)
    copy = pltpu.make_async_copy(go_ref, gemb, sem)
    sums = Sums(ways, given, outs, refs) if linked else None

    def point(name):
        if linked:
            sums.point(pair, name)

    @pl.when(pair == 0)
    def _():
        copy.start()

    point("begin")
    lane = lax.broadcasted_iota(jnp.int32, (BLOCK, PAIR), 1)
    for band in range(BANDS):
        here = slice(band * BLOCK, (band + 1) * BLOCK)
        k = k_ref[here, :]
        v = v_ref[here, :]
        one = jnp.ones_like(k)
        zero = jnp.zeros_like(k)
        right = jnp.where(lane < HEAD_DIM + 3, one, zero)
        left = jnp.where(lane < 3, one, zero)
        ke[0, here] = jnp.where(lane < HEAD_DIM, k, right)
        ke[1, here] = jnp.where(lane < HEAD_DIM, left, k)
        ve[0, here] = jnp.where(lane < HEAD_DIM, v, right)
        ve[1, here] = jnp.where(lane < HEAD_DIM, left, v)
        km[0, here] = jnp.where(lane < HEAD_DIM, k, zero)
        km[1, here] = jnp.where(lane < HEAD_DIM, zero, k)
    for unit, (band, j) in enumerate(units()):
        point(unit)
        t0 = band * BLOCK
        k0 = j * BLOCK
        first = j == max(0, band - REACH)
        tiles = [(0, BLOCK)] if j < band else [(i * SUB, SUB) for i in range(BLOCK // SUB)]
        for h in range(2):
            mine = slice(h * HEAD_DIM, (h + 1) * HEAD_DIM)
            lanes = slice(h * PAIR, (h + 1) * PAIR)
            for at, count in tiles:
                ts = slice(t0 + at, t0 + BLOCK)
                ks = slice(k0 + at, k0 + at + count)
                scores = mm_nt(qe_ref[ts, lanes], ke[h, ks])
                p = jnp.exp2(scores * LOG2E)
                if j == band:
                    t = lax.broadcasted_iota(jnp.int32, p.shape, 0)
                    p = jnp.where(lax.broadcasted_iota(jnp.int32, p.shape, 1) <= t, p, 0.0)
                dp = mm_nt(de_ref[ts, lanes], ve[h, ks])
                cols = slice(at, at + count)
                probs[h, at:, cols] = p.astype(bf16)
                slopes[h, at:, cols] = (p * dp).astype(bf16)
        for h in range(2):
            mine = slice(h * HEAD_DIM, (h + 1) * HEAD_DIM)
            for at, count in tiles:
                ts = slice(t0 + at, t0 + BLOCK)
                ks = slice(k0 + at, k0 + at + count)
                cols = slice(at, at + count)
                dv = mm(dt_ref[mine, ts], probs[h, at:, cols])
                dk = mm(qt_ref[mine, ts], slopes[h, at:, cols])
                if j == band:
                    dvt[mine, ks] = dv
                    dkt[mine, ks] = dk
                else:
                    dvt[mine, ks] += dv
                    dkt[mine, ks] += dk
        if j < band:
            dq = mm(slopes[0], km[0, k0 : k0 + BLOCK]) + mm(slopes[1], km[1, k0 : k0 + BLOCK])
            if first:
                dqa[...] = dq
            else:
                dqa[...] += dq
        else:
            for i in range(BLOCK // SUB):
                count = (i + 1) * SUB
                rows = slice(i * SUB, count)
                dq = mm(slopes[0, rows, :count], km[0, k0 : k0 + count])
                dq += mm(slopes[1, rows, :count], km[1, k0 : k0 + count])
                if not first:
                    dq += dqa[rows]
                grads[t0 + i * SUB : t0 + count, :PAIR] = (dq * HEAD_DIM**-0.5).astype(bf16)
    for band in range(BANDS):
        here = slice(band * BLOCK, (band + 1) * BLOCK)
        grads[here, PAIR : 2 * PAIR] = dkt[:, here].T.astype(bf16)
        grads[here, 2 * PAIR :] = dvt[:, here].T.astype(bf16)

    gw = mm_tn(low_ref[...], grads[...]).astype(bf16)
    if linked:
        sums.take_pair(pair, gw)
        point("ready")
    else:
        outs[0][0] = gw

    @pl.when(pair == 0)
    def _():
        copy.wait()

    w = jnp.concatenate([w_ref[0, 0], w_ref[1, 0], w_ref[2, 0]], 1)
    for band in range(BANDS):
        here = slice(band * BLOCK, (band + 1) * BLOCK)
        gemb[here] += mm_nt(grads[here, :], w)
    point("end")

    @pl.when(pair == PAIRS - 1)
    def _():
        table = None
        for band in range(BANDS):
            here = slice(band * BLOCK, (band + 1) * BLOCK)
            rows = jnp.concatenate([one_hot_rows(pix_ref[:, here]), chan_ref[...]], 0)
            part = mm(rows, gemb[here].astype(bf16))
            table = part if band == 0 else table + part
        count = LEVELS // ways
        for f in range(ways):
            mine = table[f * count : (f + 1) * count].astype(bf16)
            to = sums.lev_src.at[f] if linked else outs[1].at[f]
            to[:count] = mine[:, : D // 2]
            to[count:] = mine[:, D // 2 :]
        if linked:
            sums.last(table[LEVELS : LEVELS + 8])
        else:
            outs[2][...] = table[LEVELS:]


def back(ways, qe, qkv, de, qt, dt, low, w4, pix, chan, gone, given=None):
    one = pl.Buffered(1)
    rows = D // ways
    linked = given is not None
    anywhere = pl.BlockSpec(memory_space=pl.ANY)
    out_specs = [
        pl.BlockSpec((1, D, 3 * PAIR), lambda p: (p, 0, 0)),
        pl.BlockSpec((ways, 2 * LEVELS // ways, D // 2), lambda p: (0, 0, 0)),
        pl.BlockSpec((EXTRA, D), lambda p: (0, 0)),
    ]
    out_shape = [
        jax.ShapeDtypeStruct((PAIRS, D, 3 * PAIR), bf16),
        jax.ShapeDtypeStruct((ways, 2 * LEVELS // ways, D // 2), bf16),
        jax.ShapeDtypeStruct((EXTRA, D), f32),
    ]
    extra, extra_specs, extra_scratch = [], [], []
    compiler = params("arbitrary")
    if linked:
        split = lambda x: x.reshape(ways, x.shape[0] // ways, x.shape[1])
        gwo, gwe, gws, gvec, gbe = given
        extra = [split(gwo), split(gwe), split(gws), gvec, gbe]
        extra_specs = [anywhere] * 3
        extra_specs += [pl.BlockSpec(x.shape, lambda p: (0, 0)) for x in (gvec, gbe)]
        shapes = [(rows, D), (rows, FF), (FF // ways, D), (rows, 3 * D), (LEVELS // ways, D), (EXTRA, 128)]
        out_specs = [pl.BlockSpec(shape, lambda p: (0, 0), pipeline_mode=one) for shape in shapes]
        out_shape = [jax.ShapeDtypeStruct(shape, f32) for shape in shapes]
        extra_scratch = Sums.scratch(ways)
        compiler = pltpu.CompilerParams(
            vmem_limit_bytes=VMEM_LIMIT, dimension_semantics=("arbitrary",), collective_id=1, has_side_effects=True
        )
    return pl.pallas_call(
        functools.partial(back_kernel, ways, linked),
        grid=(PAIRS,),
        in_specs=[
            pl.BlockSpec((SEQ, 2 * PAIR), lambda p: (0, p)),
            pl.BlockSpec((SEQ, PAIR), lambda p: (0, PAIRS + p)),
            pl.BlockSpec((SEQ, PAIR), lambda p: (0, 2 * PAIRS + p)),
            pl.BlockSpec((SEQ, 2 * PAIR), lambda p: (0, p)),
            pl.BlockSpec((PAIR, SEQ), lambda p: (p, 0)),
            pl.BlockSpec((PAIR, SEQ), lambda p: (p, 0)),
            pl.BlockSpec((SEQ, D), lambda p: (0, 0), pipeline_mode=one),
            pl.BlockSpec((3, 1, D, PAIR), lambda p: (0, p, 0, 0)),
            pl.BlockSpec((1, SEQ), lambda p: (0, 0)),
            pl.BlockSpec((EXTRA, BLOCK), lambda p: (0, 0)),
            anywhere,
            *extra_specs,
        ],
        out_specs=out_specs,
        out_shape=out_shape,
        scratch_shapes=[
            pltpu.VMEM((2, SEQ, PAIR), bf16),
            pltpu.VMEM((2, SEQ, PAIR), bf16),
            pltpu.VMEM((2, SEQ, PAIR), bf16),
            pltpu.VMEM((2, BLOCK, BLOCK), bf16),
            pltpu.VMEM((2, BLOCK, BLOCK), bf16),
            pltpu.VMEM((PAIR, SEQ), f32),
            pltpu.VMEM((PAIR, SEQ), f32),
            pltpu.VMEM((BLOCK, PAIR), f32),
            pltpu.VMEM((SEQ, 3 * PAIR), bf16),
            pltpu.VMEM((SEQ, D), f32),
            pltpu.SemaphoreType.DMA,
            *extra_scratch,
        ],
        compiler_params=compiler,
    )(qe, qkv, qkv, de, qt, dt, low, w4, pix, chan, gone, *extra)


class Sums:
    EARLY = ((0, 3), (0, "ready"), (1, "ready"), (2, "ready"), (3, 3))
    NEXT = ((0, "ready"), (1, 3), (1, "ready"), (2, "ready"), (3, "ready"))

    @staticmethod
    def sizes(ways):
        rows = D // ways
        return [(FF // ways, D), (rows, FF), (rows, D)] + [(rows, 3 * PAIR)] * PAIRS + [(2 * LEVELS // ways, D // 2)]

    @staticmethod
    def scratch(ways):
        sizes = Sums.sizes(ways)
        scratch = [pltpu.VMEM(size, f32) for size in sizes]
        scratch += [pltpu.VMEM((PAIRS, ways, *sizes[3]), bf16), pltpu.VMEM((ways, *sizes[-1]), bf16)]
        scratch += [pltpu.VMEM((ways, EXTRA, 128), f32), pltpu.VMEM((EXTRA, 128), f32)]
        for size in sizes:
            scratch += Reduce.scratch(ways, *size)
        return scratch + ReduceSmall.scratch(ways, EXTRA, 128)

    def __init__(self, ways, given, outs, scratch):
        self.ways, self.outs = ways, outs
        self.place = Place(ways)
        wo, we, ws, self.gvec, self.gbe = given
        scratch = list(scratch)
        take = lambda count: [scratch.pop(0) for _ in range(count)]
        self.results = take(4 + PAIRS)
        self.in_src, self.lev_src = take(2)
        self.small_src, self.small_out = take(2)
        sources = [ws, we, wo, *[self.in_src.at[p] for p in range(PAIRS)], self.lev_src]
        chunks = [Reduce(self.place, s, r, take(5)) for s, r in zip(sources, self.results)]
        self.early, self.pairs, self.lev = chunks[:3], chunks[3:-1], chunks[-1]
        self.small = ReduceSmall(self.place, self.small_src, self.small_out, take(4))

    def point(self, pair, name):
        @pl.when(pair == 0)
        def _():
            if name == "begin":
                self.place.hello()
            if name == 3:
                self.place.greeted()

        for stage, (when, where) in enumerate(self.EARLY):
            if where == name:

                @pl.when(pair == when)
                def _():
                    for chunk in self.early:
                        chunk.stages[stage](chunk)

        for p, chunk in reversed(list(enumerate(self.pairs))):
            for stage, (after, where) in enumerate(self.NEXT):
                if where == name and p + after < PAIRS:

                    @pl.when(pair == p + after)
                    def _():
                        chunk.stages[stage](chunk)

    def take_pair(self, pair, gw):
        self.in_src[pair] = gw.reshape(self.in_src.shape[1:])

    def last(self, channels):
        comb = self.gvec[...] + channels
        self.small_src[...] = jnp.zeros_like(self.small_src)
        for f in range(self.place.n):
            cols = comb[:, f // 2 * 128 : (f // 2 + 1) * 128]
            self.small_src[f, 0:8] = cols if f % 2 == 0 else pltpu.roll(cols, HEAD_DIM, 1)
            for j in range(2):
                at = (f * 2 + j) * 128
                self.small_src[f, 8 + j : 9 + j] = self.gbe[0:1, at : at + 128]
        done = {chunk: sum(p + after < PAIRS for after, _ in self.NEXT) for p, chunk in enumerate(self.pairs)}
        done.update({self.lev: 0, self.small: 0})
        while any(at < len(Reduce.stages) for at in done.values()):
            for chunk, at in reversed(list(done.items())):
                if at < len(Reduce.stages):
                    chunk.stages[at](chunk)
                    done[chunk] = at + 1
        o_out, e_out, s_out, in_out, lev_out, small_out = self.outs
        s_out[...], e_out[...], o_out[...] = [x[...] for x in self.results[:3]]
        for p in range(PAIRS):
            for part in range(3):
                at = (part * PAIRS + p) * PAIR
                in_out[:, at : at + PAIR] = self.results[3 + p][:, part * PAIR : (part + 1) * PAIR]
        half = lev_out.shape[0]
        lev_out[:, : D // 2] = self.results[-1][:half]
        lev_out[:, D // 2 :] = self.results[-1][half:]
        small_out[...] = self.small_out[...]


def place_kernel(o, e, s, win, lev, small, *outs):
    names = ("lev", "chan", "win", "o", "gain1", "bias1", "e", "eb", "s", "sb", "gain2", "bias2")
    to = dict(zip(names, outs))
    for name, ref in (("lev", lev), ("win", win), ("o", o), ("e", e), ("s", s)):
        to[name][...] = ref[...]
    each = to["chan"].shape[1]
    to["chan"][...] = small[5:8, :each]
    for i, name in enumerate(("gain1", "bias1", "sb", "gain2", "bias2")):
        to[name][...] = small[i : i + 1, :each]
    for i in range(2):
        to["eb"][:, i * 128 : (i + 1) * 128] = small[8 + i : 9 + i]


def place_results(ways, o, e, s, win, lev, small):
    each = D // ways
    vec = (1, each)
    shapes = [
        lev.shape, (CHANNELS, each), win.shape, o.shape, vec, vec, e.shape, (1, FF // ways), s.shape, vec, vec, vec,
    ]
    outs = pl.pallas_call(
        place_kernel,
        out_shape=[jax.ShapeDtypeStruct(shape, f32) for shape in shapes],
        compiler_params=params(),
    )(o, e, s, win, lev, small)
    return [x.reshape(-1) if x.shape[0] == 1 else x for x in outs]


def channel_rows():
    pos = np.arange(BLOCK) % CHANNELS + 5
    return (np.arange(EXTRA)[:, None] == pos[None, :]).astype(bf16)


def image(ways, pix, cot, chan, embedded, weights, shards=None):
    emb, low, qkv, qt, vt, sizes = embedded
    w4, wo, vec, be, we, ws = weights
    att, qe, *fetched = attend(ways, qkv, vt, shards)
    if shards is not None:
        we, ws = [x.reshape(-1, x.shape[2]) for x in fetched]
    att, qe = repair(sizes, qkv, vt, att, qe)
    out, gone, de, dt, *grads = middle(att, emb, cot, wo, we, ws, vec, be)
    if shards is not None:
        return out, *back(ways, qe, qkv, de, qt, dt, low, w4, pix, chan, gone, grads)
    return out, *grads, *back(ways, qe, qkv, de, qt, dt, low, w4, pix, chan, gone)


def pack_small(vectors, channels, bias):
    size = bias.shape[0] // 128
    rows = jnp.concatenate([jnp.stack(vectors), channels])
    rows = jnp.pad(rows, ((0, 0), (0, 128 - rows.shape[1])))
    return jnp.concatenate([rows, bias.reshape(size, 128), jnp.zeros((EXTRA - 8 - size, 128), bf16)])


def body(
    ways, pixels, level_table, channel_table, attend_in, attend_out, first_gain, first_bias, expand_weight,
    expand_bias, shrink_weight, shrink_bias, second_gain, second_bias, cotangent,
):
    chan = channel_rows()
    vectors = (first_gain, first_bias, shrink_bias, second_gain, second_bias)
    small = pack_small(vectors, channel_table, expand_bias)
    *embedded, vec, be, w4, wo = embed_gather(ways, pixels, chan, level_table, small, attend_in, attend_out)
    weights = (w4.reshape(3, PAIRS, D, PAIR), wo.reshape(D, D), vec, be, None, None)
    shards = (expand_weight, shrink_weight)
    out, *sums = image(ways, pixels, cotangent[0], chan, embedded, weights, shards)
    return out[None], *place_results(ways, *sums)


def plain_body(
    ways, pixels, level_table, channel_table, attend_in, attend_out, first_gain, first_bias, expand_weight,
    expand_bias, shrink_weight, shrink_bias, second_gain, second_bias, cotangent,
):
    gather = lambda x, axis=0: lax.all_gather(x, "fsdp", axis=axis, tiled=True)
    vectors = jnp.stack((first_gain, first_bias, shrink_bias, second_gain, second_bias))
    chan = channel_rows()
    small = gather(jnp.concatenate([vectors, channel_table]), 1)
    table = jnp.pad(small, ((0, EXTRA - 8), (0, 0)))
    level = gather(level_table)
    w_in = gather(attend_in)
    be = jnp.pad(gather(expand_bias).astype(f32)[None], ((0, 7), (0, 0)))
    w4 = w_in.reshape(D, 3, PAIRS, PAIR).transpose(1, 2, 0, 3)
    weights = (w4, gather(attend_out), table.astype(f32), be, gather(expand_weight), gather(shrink_weight))
    outs = []
    sums = None
    for i in range(pixels.shape[0]):
        pix = pixels[i : i + 1]
        got = image(ways, pix, cotangent[i], chan, embed_plain(pix, chan, level, table, w_in), weights)
        outs.append(got[0])
        grads = [x.astype(f32) for x in got[1:]]
        sums = grads if sums is None else [a + b for a, b in zip(sums, grads)]
    gwo, gwe, gws, gvec, gbe, gw, glev, gchan = sums
    gwin = gw.reshape(PAIRS, D, 3, PAIR).transpose(1, 2, 0, 3).reshape(D, 3 * D)
    count = LEVELS // ways
    glev = glev.reshape(ways, 2, count, D // 2).transpose(0, 2, 1, 3).reshape(LEVELS, D)

    def scatter(x, axis=0):
        return lax.psum(lax.psum_scatter(x, "fsdp", scatter_dimension=axis, tiled=True), "dp")

    small = scatter(gvec + gchan[:8], 1)
    return (
        jnp.stack(outs), scatter(glev), small[5:8], scatter(gwin), scatter(gwo), small[0], small[1], scatter(gwe),
        scatter(gbe[0]), scatter(gws), small[2], small[3], small[4],
    )


def solution(mesh):
    row = P("fsdp", None)
    vector = P("fsdp")
    shared = P(("fsdp", "dp"), None, None)
    weights = (
        row, P(None, "fsdp"), row, row, vector, vector, row, vector, row, vector, vector, vector,
    )
    ways = mesh.shape["fsdp"]
    fits = ways == 8 and mesh.shape["dp"] == 4

    def program(pixels, *rest):
        return (body if fits and pixels.shape[0] == 1 else plain_body)(ways, pixels, *rest)

    return jax.shard_map(
        program,
        mesh=mesh,
        in_specs=(P(("fsdp", "dp"), None), *weights, shared),
        out_specs=(shared, *weights),
        check_vma=False,
    )
```
